32 devices in a mesh: dp: 8 (over z, y), blk: 4 (over x, core).
Axes of the slice: x: 2, y: 2, z: 4, core: 2. Of those that a mesh axis runs over, the one named last changes fastest.
Arguments:
- frames: bfloat16 [8, 1024, 1024], P('dp', 'blk'), may hold values from -6 to 6
- skip_frames: bfloat16 [8, 1024, 1024], P('dp', 'blk'), may hold values from -6 to 6
- cotangent: bfloat16 [8, 1024, 1024], P('dp', 'blk'), may hold values from -6 to 6
- seg_ids: int32 [8, 1024], P('dp', 'blk'), may hold values from 0 to 31, as said below
- positions: int32 [8, 1024], P('dp', 'blk'), may hold values from 0 to 511, as said below
- w_skip: float32 [2048, 1024], P('dp'), may hold values from -0.125 to 0.125
- b_skip: float32 [1024], P('dp'), may hold values from -1 to 1
- gain_attn: float32 [1024], P('dp'), may hold values from 0.25 to 1.75
- bias_attn: float32 [1024], P('dp'), may hold values from -1 to 1
- w_qkv: float32 [1024, 3072], P('dp'), may hold values from -0.1875 to 0.1875
- w_out: float32 [1024, 1024], P('dp'), may hold values from -0.375 to 0.375
- gain_ffn: float32 [1024], P('dp'), may hold values from 0.25 to 1.75
- bias_ffn: float32 [1024], P('dp'), may hold values from -1 to 1
- w_up: float32 [1024, 4096], P('dp'), may hold values from -0.1875 to 0.1875
- b_up: float32 [4096], P('dp'), may hold values from -1 to 1
- w_down: float32 [4096, 1024], P('dp'), may hold values from -0.09375 to 0.09375
- b_down: float32 [1024], P('dp'), may hold values from -1 to 1
Outputs:
- output: bfloat16 [8, 1024, 1024], P('dp', 'blk')
- grad_frames: bfloat16 [8, 1024, 1024], P('dp', 'blk')
- grad_skip: bfloat16 [8, 1024, 1024], P('dp', 'blk')
- grad_w_skip: float32 [2048, 1024], P('dp')
- grad_b_skip: float32 [1024], P('dp')
- grad_gain_attn: float32 [1024], P('dp')
- grad_bias_attn: float32 [1024], P('dp')
- grad_w_qkv: float32 [1024, 3072], P('dp')
- grad_w_out: float32 [1024, 1024], P('dp')
- grad_gain_ffn: float32 [1024], P('dp')
- grad_bias_ffn: float32 [1024], P('dp')
- grad_w_up: float32 [1024, 4096], P('dp')
- grad_b_up: float32 [4096], P('dp')
- grad_w_down: float32 [4096, 1024], P('dp')
- grad_b_down: float32 [1024], P('dp')
The draws below stay inside these ranges and needn't reach their ends.
Inputs may be any that keep to these rules, and one draw needn't show every extreme that they name: `seg_ids`: each row holds exactly 32 items, packed back to back in a drawn order and numbered 0, 1, 2, ... in that order; frame v of the packed order (v from 0) lies at slot (v % 4) * 256 + v // 4 of the row. `positions`: positions count from 0 within an item along the packed order; every row holds exactly one item of 512 frames.
All inputs are finite; a program needn't handle non-finite values.
Results may differ from the reference program's by a relative error of at most 0.025.
Values may be sent and summed in bfloat16 or wider, within the bound.
A program may use at most 256 MiB of HBM per device.

```python
import math
import jax
import jax.numpy as jnp
from jax import lax

D = 1024
H = 16
FF = 4096
FR = 256
ROW = 1024
ROWS = 8
LONG = 512
ITEMS = 32


def packed_row(key):
    place_key, cut_key = jax.random.split(key, 2)
    rest = ROW - LONG
    short_count = ITEMS - 1
    shuffled = jax.random.permutation(cut_key, rest - 1).astype(jnp.int32) + 1
    cuts = jnp.sort(shuffled[:short_count - 1])
    bounds = jnp.concatenate([jnp.zeros((1,), jnp.int32), cuts, jnp.full((1,), rest, jnp.int32)])
    short_lengths = (bounds[1:] - bounds[:-1]).astype(jnp.int32)
    long_place = jax.random.randint(place_key, (), 0, ITEMS).astype(jnp.int32)
    item_index = jnp.arange(ITEMS, dtype=jnp.int32)
    short_index = jnp.clip(item_index - (item_index > long_place).astype(jnp.int32), 0, short_count - 1)
    lengths = jnp.where(item_index == long_place, LONG, short_lengths[short_index]).astype(jnp.int32)
    starts = (jnp.cumsum(lengths) - lengths).astype(jnp.int32)
    virtual = jnp.arange(ROW, dtype=jnp.int32)
    seg_virtual = (jnp.searchsorted(starts, virtual, side='right') - 1).astype(jnp.int32)
    pos_virtual = (virtual - starts[seg_virtual]).astype(jnp.int32)
    slots = jnp.arange(ROW, dtype=jnp.int32)
    device_count = ROW // FR
    source = slots % FR * device_count + slots // FR
    return jnp.stack([seg_virtual[source], pos_virtual[source]])


def packed_layout(key):
    row_keys = jax.random.split(key, ROWS)
    return jax.vmap(packed_row)(row_keys)


def draw_seg_ids(key, part):
    return packed_layout(key)[:, 0, :].astype(jnp.int32)


def draw_positions(key, part):
    return packed_layout(key)[:, 1, :].astype(jnp.int32)


def shard_levels(key, extent, cuts, low, largest):
    loudness = 1.0
    for axis_at, parts in cuts:
        heights = jax.random.uniform(jax.random.fold_in(jax.random.fold_in(key, 6), axis_at), (parts,), jnp.float32, low / len(cuts), largest / len(cuts))
        loudness = loudness * jnp.repeat(jnp.exp(heights), extent[axis_at] // parts).reshape((-1,) + (1,) * (len(extent) - 1 - axis_at))
    return loudness


def scatter_about(key, dims, scale, limit, cuts=(), held_as=jnp.bfloat16):
    array = jax.random.normal(key, dims, jnp.float32) * scale
    if len(cuts) > 0:
        array = shard_levels(key, dims, cuts, -0.22, 0.18) * array
    return jnp.clip(array, min=-limit, max=limit).astype(held_as)


def setup_inputs(seed: int = 0) -> dict:
    arg_keys = jax.random.split(jax.random.key(seed), 18)
    frames = scatter_about(arg_keys[0], (ROWS, ROW, D), 1.0, 6.0, ((0, 8), (1, 4)))
    skip_frames = scatter_about(arg_keys[1], (ROWS, ROW, D), 1.0, 6.0, ((0, 8), (1, 4)))
    cotangent = scatter_about(arg_keys[2], (ROWS, ROW, D), 1.0, 6.0, ((0, 8), (1, 4)))
    seg_ids = draw_seg_ids(jax.random.fold_in(arg_keys[17], 71), 0)
    positions = draw_positions(jax.random.fold_in(arg_keys[17], 71), 0)
    w_skip = scatter_about(arg_keys[5], (2 * D, D), (2 * D) ** -0.5, 0.125, ((0, 8),), jnp.float32)
    b_skip = scatter_about(arg_keys[6], (D,), 0.2, 1.0, ((0, 8),), jnp.float32)
    gain_attn = jnp.clip(1.0 + 0.15 * jax.random.normal(arg_keys[7], (D,), jnp.float32), 0.25, 1.75)
    bias_attn = scatter_about(arg_keys[8], (D,), 0.2, 1.0, ((0, 8),), jnp.float32)
    w_qkv = scatter_about(arg_keys[9], (D, 3 * D), D ** -0.5, 0.1875, ((0, 8),), jnp.float32)
    w_out = scatter_about(arg_keys[10], (D, D), (D // 4) ** -0.5, 0.375, ((0, 8),), jnp.float32)
    gain_ffn = jnp.clip(1.0 + 0.15 * jax.random.normal(arg_keys[11], (D,), jnp.float32), 0.25, 1.75)
    bias_ffn = scatter_about(arg_keys[12], (D,), 0.2, 1.0, ((0, 8),), jnp.float32)
    w_up = scatter_about(arg_keys[13], (D, FF), D ** -0.5, 0.1875, ((0, 8),), jnp.float32)
    b_up = scatter_about(arg_keys[14], (FF,), 0.2, 1.0, ((0, 8),), jnp.float32)
    w_down = scatter_about(arg_keys[15], (FF, D), FF ** -0.5, 0.09375, ((0, 8),), jnp.float32)
    b_down = scatter_about(arg_keys[16], (D,), 0.2, 1.0, ((0, 8),), jnp.float32)
    return dict(frames=frames, skip_frames=skip_frames, cotangent=cotangent, seg_ids=seg_ids, positions=positions, w_skip=w_skip, b_skip=b_skip, gain_attn=gain_attn, bias_attn=bias_attn, w_qkv=w_qkv, w_out=w_out, gain_ffn=gain_ffn, bias_ffn=bias_ffn, w_up=w_up, b_up=b_up, w_down=w_down, b_down=b_down)


@jax.custom_vjp
def low(v):
    return lax.optimization_barrier(v.astype(jnp.bfloat16)).astype(jnp.float32)

@jax.custom_vjp
def low_back(v):
    return v

def low_keep(v):
    return (low(v), None)

def low_pass(kept, grad):
    return (grad,)

def back_keep(v):
    return (v, None)

def back_low(kept, grad):
    return (low(grad),)
low.defvjp(low_keep, low_pass)
low_back.defvjp(back_keep, back_low)
HIGHEST = lax.Precision.HIGHEST
EPSILON = 1e-05

def layer_norm(hidden, gain, offset):
    centred = hidden - lax.optimization_barrier(jnp.mean(hidden, axis=-1, keepdims=True))
    spread = lax.optimization_barrier(jnp.mean(centred * centred, axis=-1, keepdims=True))
    return centred * lax.rsqrt(spread + EPSILON) * gain + offset

def alibi_slopes(head_count):
    return 2.0 ** (-8.0 * (jnp.arange(head_count) + 1.0) / head_count)

def attend_row(mixed, seg_row, pos_row):
    row_len = mixed.shape[0]
    model_width = mixed.shape[1] // 3
    queries = mixed[:, :model_width].reshape(row_len, H, -1)
    keys_all = mixed[:, model_width:2 * model_width].reshape(row_len, H, -1)
    values_all = mixed[:, 2 * model_width:].reshape(row_len, H, -1)
    self_shift = lax.optimization_barrier(jnp.sum(queries * keys_all, axis=-1)) * 0.125
    slopes = alibi_slopes(H)
    block_size = math.gcd(row_len, 512)
    count_blocks = row_len // block_size

    def one_block(block_args):
        query_blk, shift_blk, seg_blk, pos_blk = block_args
        raw_scores = jnp.einsum('qhd,khd->hqk', query_blk, keys_all, precision=HIGHEST) * 0.125
        distance = jnp.abs(pos_blk[:, None] - pos_row[None, :]).astype(raw_scores.dtype)
        raw_scores = low_back(raw_scores - slopes[:, None, None].astype(raw_scores.dtype) * distance[None])
        same_item = (seg_blk[:, None] == seg_row[None, :])[None]
        exp_terms = jnp.where(same_item, jnp.exp(jnp.where(same_item, raw_scores - shift_blk.T[:, :, None], 0.0)), 0.0)
        totals = lax.optimization_barrier(jnp.sum(exp_terms, axis=-1))
        summed = low_back(jnp.einsum('hqk,khd->qhd', low(exp_terms), values_all, precision=HIGHEST))
        return summed / totals.T[:, :, None]
    blocks = lax.map(jax.checkpoint(one_block), (queries.reshape(count_blocks, block_size, H, -1), self_shift.reshape(count_blocks, block_size, H), seg_row.reshape(count_blocks, block_size), pos_row.reshape(count_blocks, block_size)))
    return blocks.reshape(row_len, model_width)

def row_forward(params, frame_row, skip_row, seg_row, pos_row):
    w_skip, b_skip, gain_attn, bias_attn, w_qkv, w_out, gain_ffn, bias_ffn, w_up, b_up, w_down, b_down = params
    joined = jnp.concatenate([frame_row, skip_row], axis=-1)
    merged = low_back(jnp.dot(joined, w_skip, precision=HIGHEST) + b_skip)
    normed = low(layer_norm(merged, gain_attn, bias_attn))
    mixed = low(low_back(jnp.dot(normed, w_qkv, precision=HIGHEST)))
    attended = low(low_back(attend_row(mixed, seg_row, pos_row)))
    middle = merged + low_back(jnp.dot(attended, w_out, precision=HIGHEST))
    second = low(layer_norm(middle, gain_ffn, bias_ffn))
    hidden = low_back(jnp.dot(second, w_up, precision=HIGHEST) + b_up)
    active = low(jax.nn.gelu(hidden, approximate=False))
    return middle + jnp.dot(active, w_down, precision=HIGHEST) + b_down

def forward(params, frame_set, skip_set, seg_ids, positions):
    lowered = tuple((low(param) for param in params))
    checked = jax.checkpoint(row_forward)

    def one_row(row_args):
        frame_row, skip_row, seg_row, pos_row = row_args
        return checked(lowered, frame_row, skip_row, seg_row, pos_row)
    return lax.map(one_row, (frame_set, skip_set, seg_ids, positions))

def reference(frames, skip_frames, cotangent, seg_ids, positions, w_skip, b_skip, gain_attn, bias_attn, w_qkv, w_out, gain_ffn, bias_ffn, w_up, b_up, w_down, b_down):
    params = (w_skip, b_skip, gain_attn, bias_attn, w_qkv, w_out, gain_ffn, bias_ffn, w_up, b_up, w_down, b_down)

    def whole(param_set, frame_set, skip_set):
        return forward(param_set, frame_set, skip_set, seg_ids, positions)
    output, pull = jax.vjp(whole, params, frames.astype(jnp.float32), skip_frames.astype(jnp.float32))
    grad_params, grad_frames, grad_skip = pull(cotangent.astype(jnp.float32))
    grad_w_skip, grad_b_skip, grad_gain_attn, grad_bias_attn, grad_w_qkv, grad_w_out, grad_gain_ffn, grad_bias_ffn, grad_w_up, grad_b_up, grad_w_down, grad_b_down = grad_params
    return (output.astype(jnp.bfloat16), grad_frames.astype(jnp.bfloat16), grad_skip.astype(jnp.bfloat16), grad_w_skip, grad_b_skip, grad_gain_attn, grad_bias_attn, grad_w_qkv, grad_w_out, grad_gain_ffn, grad_bias_ffn, grad_w_up, grad_b_up, grad_w_down, grad_b_down)
```

```python
import functools
import math

import jax
import jax.numpy as jnp
from jax import lax
from jax.experimental import pallas as pl
from jax.experimental.pallas import tpu as pltpu
from jax.sharding import PartitionSpec as P

H = 16
EPSILON = 1e-05
LOW = jnp.bfloat16
F32 = jnp.float32
MESH = pl.DeviceIdType.MESH
FAR = 1e30


def dot(left, right):
    return jnp.dot(left, right, preferred_element_type=F32)


def dot_nt(left, right):
    return lax.dot_general(left, right, (((1,), (1,)), ((), ())), preferred_element_type=F32)


def loop(count, body):
    def visit(index, carry):
        body(index)
        return carry

    lax.fori_loop(0, count, visit, 0)


def aligned(start, size):
    return pl.ds(pl.multiple_of(start, size), size)


class Sizes:
    def __init__(self, mesh_shape, frames, w_up):
        self.n_dp, self.n_blk = mesh_shape["dp"], mesh_shape["blk"]
        self.nz = self.n_dp // 2
        self.groups = self.n_blk // 2
        self.rows = frames.shape[1]
        self.width = frames.shape[2]
        self.hidden = w_up.shape[1]
        self.shard = self.width // self.n_dp
        self.cols = self.width // self.groups
        self.heads = H // self.groups
        self.units = self.hidden // self.groups
        self.part = self.units // self.n_dp
        self.direct = self.part % 128 == 0
        self.up_rows = -(-self.units // self.width)


class Wires:
    def __init__(self, send_sems, recv_sems):
        self.send_sems, self.recv_sems, self.used = send_sems, recv_sems, 0

    def take(self, count=1):
        first = self.used
        self.used += count
        assert self.used <= self.send_sems.shape[0]
        return first

    def copy(self, ends, index=None):
        return Copy(self, ends, self.take() if index is None else index)


class Copy:
    def __init__(self, wires, ends, index):
        self.wires, self.ends, self.index = wires, ends, index

    def made(self):
        source, target, peer = self.ends()
        return pltpu.make_async_remote_copy(
            src_ref=source,
            dst_ref=target,
            send_sem=self.wires.send_sems.at[self.index],
            recv_sem=self.wires.recv_sems.at[self.index],
            device_id=peer,
            device_id_type=MESH,
        )

    def start(self):
        self.made().start()

    def wait_send(self):
        self.made().wait_send()

    def wait_recv(self):
        self.made().wait_recv()

    def wait(self):
        self.made().wait()


class Place:
    def __init__(self, sizes):
        self.dp, self.blk = lax.axis_index("dp"), lax.axis_index("blk")
        self.z, self.y = lax.div(self.dp, 2), lax.rem(self.dp, 2)
        self.g, self.c = lax.div(self.blk, 2), lax.rem(self.blk, 2)
        self.sizes = sizes

    def z_at(self, step):
        nz = self.sizes.nz
        return lax.rem(self.z + (step + nz), nz)

    def g_at(self, step):
        groups = self.sizes.groups
        return lax.rem(self.g + (step + groups), groups)

    def z_peer(self, step):
        return (self.z_at(step) * 2 + self.y, self.blk)

    def y_peer(self):
        return (self.z * 2 + 1 - self.y, self.blk)

    def x_peer(self, step):
        return (self.dp, self.g_at(step) * 2 + self.c)

    def c_peer(self):
        return (self.dp, self.g * 2 + 1 - self.c)


class Gather:
    def __init__(self, place, wires, ref, half, spread, whole_core=False):
        self.place, self.wires, self.ref = place, wires, ref
        self.half, self.spread, self.whole_core = half, spread, whole_core
        sizes = place.sizes
        self.nz = sizes.nz
        self.groups = sizes.groups if spread else 1
        self.z_copies, self.y_copies, self.x_copies, self.c_copies = {}, {}, {}, {}

    def piece(self, k, step=0):
        place = self.place
        z_index = place.z_at(-(k % self.nz))
        y_index = place.y if k < self.nz else 1 - place.y
        if self.whole_core:
            return self.ref.at[z_index, y_index]
        rows = aligned(place.c * self.half, self.half)
        if not self.spread:
            return self.ref.at[z_index, y_index, rows]
        cols = place.sizes.cols
        return self.ref.at[z_index, y_index, rows, aligned(place.g_at(-step) * cols, cols)]

    def send(self, copies, key, piece, peer):
        copies[key] = self.wires.copy(lambda: (piece(), piece(), peer()))
        copies[key].start()

    def start(self):
        for step in range(1, self.nz):
            self.send(
                self.z_copies, step, lambda: self.piece(0), lambda step=step: self.place.z_peer(step)
            )
        self.forward(0)

    def forward(self, k):
        def piece():
            return self.piece(k)

        if k < self.nz:
            self.send(self.y_copies, k, piece, self.place.y_peer)
        for step in range(1, self.groups):
            self.send(self.x_copies, (step, k), piece, lambda step=step: self.place.x_peer(step))
        if not self.whole_core:
            self.send(self.c_copies, (0, k), piece, self.place.c_peer)

    def z_step(self, step):
        self.z_copies[step].wait_recv()
        self.forward(step)

    def y_step(self, k):
        self.y_copies[k].wait_recv()
        self.forward(self.nz + k)

    def x_step(self, k):
        for step in range(1, self.groups):
            self.x_copies[step, k].wait_recv()
            self.send(
                self.c_copies, (step, k), lambda step=step: self.piece(k, step), self.place.c_peer
            )

    def z_steps(self):
        for step in range(1, self.nz):
            self.z_step(step)

    def y_steps(self):
        for k in range(self.nz):
            self.y_step(k)

    def x_steps(self):
        for k in range(2 * self.nz):
            self.x_step(k)

    def finish(self):
        for copy in self.c_copies.values():
            copy.wait_recv()

    def drain(self):
        for copies in (self.z_copies, self.y_copies, self.x_copies, self.c_copies):
            for copy in copies.values():
                copy.wait_send()
            copies.clear()


class Exchange:
    def __init__(self, place, wires):
        self.place, self.groups = place, place.sizes.groups
        self.wires = wires
        self.first = wires.take(self.groups)

    def copy(self, step, source, target):
        return self.wires.copy(
            lambda: (source(), target(), self.place.x_peer(step)), self.first + step
        )


class Reduce:
    def __init__(self, place, wires, grad, half, spread, core_in, x_in, y_in, z_in, out):
        self.place, self.wires, self.grad, self.half, self.spread = place, wires, grad, half, spread
        self.core_in, self.x_in, self.y_in, self.z_in, self.out = core_in, x_in, y_in, z_in, out
        self.nz, self.groups = place.sizes.nz, place.sizes.groups
        self.core_copies, self.x_copies, self.z_copies = {}, {}, {}
        self.fin_copies, self.fwd_copies = {}, {}

    def side(self, part):
        return 1 - self.place.y if part == 0 else self.place.y

    def core_send(self, part):
        def ends():
            side = self.side(part)
            rows = aligned((1 - self.place.c) * self.half, self.half)
            return self.grad.at[:, side, rows], self.core_in.at[:, side], self.place.c_peer()

        copy = self.wires.copy(ends)
        copy.start()
        self.core_copies[part] = copy

    def core_add(self, part):
        side = self.side(part)
        rows = aligned(self.place.c * self.half, self.half)
        self.core_copies[part].wait_recv()

        def body(z):
            self.core_in[z, side] = self.core_in[z, side] + self.grad[z, side, rows]

        loop(self.nz, body)
        if self.spread:
            cols = self.place.sizes.cols
            for step in range(1, self.groups):
                def ends(step=step):
                    side = self.side(part)
                    theirs = aligned(self.place.g_at(step) * cols, cols)
                    return (
                        self.core_in.at[:, side, :, theirs],
                        self.x_in.at[step - 1, :, side],
                        self.place.x_peer(step),
                    )

                copy = self.wires.copy(ends)
                copy.start()
                self.x_copies[part, step] = copy
        elif part == 0:
            self.y_send()

    def x_add(self, part):
        side = self.side(part)
        cols = self.place.sizes.cols
        mine = aligned(self.place.g * cols, cols)
        for step in range(1, self.groups):
            self.x_copies[part, step].wait_recv()

        def body(z):
            total = self.core_in[z, side, :, mine].astype(F32)
            for step in range(1, self.groups):
                total = total + self.x_in[step - 1, z, side].astype(F32)
            self.x_in[0, z, side] = total.astype(LOW)

        loop(self.nz, body)
        if part == 0:
            self.y_send()

    def held(self):
        return self.x_in.at[0] if self.spread else self.core_in

    def y_send(self):
        self.y_copy = self.wires.copy(
            lambda: (self.held().at[:, self.side(0)], self.y_in, self.place.y_peer())
        )
        self.y_copy.start()

    def y_add(self):
        self.y_copy.wait()
        side = self.side(1)
        held = self.held()

        def body(z):
            self.y_in[z] = self.y_in[z] + held[z, side]

        loop(self.nz, body)
        for step in range(1, self.nz):
            copy = self.wires.copy(
                lambda step=step: (
                    self.y_in.at[self.place.z_at(step)],
                    self.z_in.at[step - 1],
                    self.place.z_peer(step),
                )
            )
            copy.start()
            self.z_copies[step] = copy

    def z_add(self):
        place = self.place
        for step in range(1, self.nz):
            self.z_copies[step].wait_recv()

        def body(i):
            at = aligned(i * 16, 16)
            total = self.y_in[place.z, at].astype(F32)
            for step in range(1, self.nz):
                total = total + self.z_in[step - 1, at].astype(F32)
            self.out[place.g, place.c, at] = total.astype(LOW)

        loop(self.half // 16, body)
        for step in range(1, self.groups):
            self.fin_copies[step] = self.wires.copy(
                lambda step=step: self.spot(0) * 2 + (place.x_peer(step),)
            )
            self.fin_copies[step].start()
        self.forward(0)

    def spread_on(self):
        for step in range(1, self.groups):
            self.fin_copies[step].wait_recv()
            self.forward(step)

    def spot(self, step):
        return (self.out.at[self.place.g_at(-step), self.place.c],)

    def forward(self, step):
        self.fwd_copies[step] = self.wires.copy(
            lambda: self.spot(step) * 2 + (self.place.c_peer(),)
        )
        self.fwd_copies[step].start()

    def drain(self):
        for copies in (self.core_copies, self.x_copies, self.z_copies, self.fin_copies):
            for copy in copies.values():
                copy.wait_send()

    def finish(self):
        for copy in self.fwd_copies.values():
            copy.wait()


def norm_terms(held):
    centred = held - jnp.mean(held, axis=-1, keepdims=True)
    scale = lax.rsqrt(jnp.mean(centred * centred, axis=-1, keepdims=True) + EPSILON)
    return centred * scale, scale


def kernel(sizes, *refs):
    names = (
        "frames", "skip", "cot", "seg", "b_skip", "gain_a", "bias_a", "gain_f", "bias_f",
        "b_down", "b_up", "w_skip", "w_qkv", "w_out", "w_up", "w_down", "o_out", "o_frames",
        "o_skip", "p_skip", "p_qkv", "p_out", "p_up", "p_down", "o_small", "o_up", "io",
        "cot_all", "ws", "wqkv", "wout", "wup", "wdown", "small", "vecs", "bup", "segs", "segc",
        "merged", "middle", "gmid", "normed", "second", "kv", "qt", "kt", "shift", "attt", "tot",
        "att_own", "att_send", "active", "ghid", "p_send", "p_recv", "gb", "ga_in", "gm", "dkv",
        "far", "vt", "c_skip", "c_out", "c_up", "c_down", "x_skip", "x_out", "y_skip", "y_qkv",
        "y_out", "y_up", "y_down", "z_skip", "z_qkv", "z_out", "z_up", "z_down", "sums",
        "sum_in", "turned", "outp", "send_sems", "recv_sems", "local_sems",
    )
    assert len(names) == len(refs), (len(names), len(refs))
    v = dict(zip(names, refs))
    place = Place(sizes)
    wires = Wires(v["send_sems"], v["recv_sems"])
    local = v["local_sems"]
    nz, groups, n_dp, n_blk = sizes.nz, sizes.groups, sizes.n_dp, sizes.n_blk
    rows, width, cols, units = sizes.rows, sizes.width, sizes.cols, sizes.units
    heads = sizes.heads
    z, y, g, c = place.z, place.y, place.g, place.c

    barrier = pltpu.get_barrier_semaphore()
    partners = [place.z_peer(step) for step in range(1, nz)] + [place.y_peer()]
    partners += [place.x_peer(step) for step in range(1, groups)] + [place.c_peer()]
    for partner in partners:
        pl.semaphore_signal(barrier, inc=1, device_id=partner, device_id_type=MESH)

    fr_v, sk_v = v["io"].at[0], v["io"].at[1]

    def input_loads():
        return [
            pltpu.make_async_copy(v["frames"].at[0], fr_v, local.at[0]),
            pltpu.make_async_copy(v["skip"].at[0], sk_v, local.at[1]),
        ]

    loads = input_loads() + [
        pltpu.make_async_copy(v["cot"].at[0], v["cot_all"].at[g], local.at[2]),
    ]

    h_skip, h_qkv = v["ws"].shape[2] // 2, v["wqkv"].shape[2] // 2
    h_out, h_up, h_down = v["wout"].shape[2] // 2, v["wup"].shape[2] // 2, v["wdown"].shape[2] // 2

    stages = {}

    def fetch(name, start, size, buffer, top, index):
        parts = v[name].shape[1] // width
        copies = [
            pltpu.make_async_copy(
                v[name].at[aligned(start, size), part * width : (part + 1) * width],
                buffer.at[top + part * size : top + (part + 1) * size],
                local.at[index + part],
            )
            for part in range(parts)
        ]
        for copy in copies:
            copy.start()
        stages[name] = copies

    merged, middle, gmid, outp = v["merged"], v["middle"], v["gmid"], v["outp"]
    fetch("w_skip", c * h_skip, h_skip, merged, 0, 3)
    fetch("w_qkv", c * h_qkv, h_qkv, gmid, 0, 4)
    fetch("w_out", c * h_out, h_out, merged, h_skip, 7)
    fetch("w_up", c * h_up, h_up, outp, 0, 8)
    fetch("w_down", (g * 2 + c) * h_down, h_down, middle, 0, 12)
    for load in loads:
        load.start()
    ws, wqkv, wout, wup, wdown = v["ws"], v["wqkv"], v["wout"], v["wup"], v["wdown"]
    own_cols = aligned(g * cols, cols)

    def arrived(name):
        for copy in stages[name]:
            copy.wait()

    arrived("w_skip")
    ws[z, y, aligned(c * h_skip, h_skip), own_cols] = merged[0:h_skip, own_cols].astype(LOW)
    arrived("w_qkv")
    for third in range(3):
        wqkv[z, y, aligned(c * h_qkv, h_qkv), third * cols : (third + 1) * cols] = gmid[
            third * h_qkv : (third + 1) * h_qkv, own_cols
        ].astype(LOW)
    arrived("w_out")
    wout[z, y, aligned(c * h_out, h_out), own_cols] = merged[
        h_skip : h_skip + h_out, own_cols
    ].astype(LOW)
    arrived("w_up")
    up_rows = aligned(c * h_up, h_up)
    if sizes.direct:
        part = sizes.part
        per_row = width // (part * groups)
        for s in range(n_dp):
            at = (s // per_row) * h_up
            wup[z, y, up_rows, s * part : (s + 1) * part] = outp[
                at : at + h_up, aligned(g * part + s % per_row * part * groups, part)
            ].astype(LOW)
    else:
        at = pl.multiple_of(lax.div(g * units, width) * h_up, h_up)
        wup[z, y, up_rows] = outp[
            pl.ds(at, h_up), aligned(lax.rem(g * units, width), units)
        ].astype(LOW)
    arrived("w_down")
    wdown[z, y, aligned(c * h_down, h_down)] = middle[0:h_down].astype(LOW)

    small = v["small"]
    for row, name in enumerate(("b_skip", "gain_a", "bias_a", "gain_f", "bias_f", "b_down")):
        small[z, y, row : row + 1, 0 : sizes.shard] = v[name][...].astype(LOW).astype(F32)
    if sizes.direct:
        own_up = v["b_up"][:, aligned(g * sizes.part, sizes.part)]
    else:
        own_up = v["b_up"][...]
    small[z, y, 6:7, 0 : sizes.part] = own_up.astype(LOW).astype(F32)
    segs = v["segs"]
    segs[c, g] = jnp.broadcast_to(v["seg"][...].astype(F32), (8, rows))

    pl.semaphore_wait(barrier, len(partners))

    g_small = Gather(place, wires, small, 0, False, whole_core=True)
    g_skip = Gather(place, wires, v["ws"], h_skip, True)
    g_qkv = Gather(place, wires, v["wqkv"], h_qkv, False)
    g_out = Gather(place, wires, v["wout"], h_out, True)
    g_up = Gather(place, wires, v["wup"], h_up, False)
    g_down = Gather(place, wires, v["wdown"], h_down, False)
    seg_swap = Exchange(place, wires)
    seg_copies = []
    for step in range(1, groups):
        seg_copies.append(seg_swap.copy(step, lambda: segs.at[c, g], lambda: segs.at[c, g]))
        seg_copies[-1].start()
    g_small.start()
    g_skip.start()
    g_qkv.start()
    g_out.start()
    g_up.start()
    g_down.start()
    for copy in seg_copies:
        copy.wait_recv()
    seg_core = wires.copy(lambda: (segs.at[c], segs.at[c], place.c_peer()))
    seg_core.start()
    for step in range(1, nz):
        g_skip.z_step(step)
        g_small.z_step(step)
    for k in range(nz):
        g_skip.x_step(k)
        g_skip.y_step(k)
        g_small.y_step(k)
    for k in range(nz, 2 * nz):
        g_skip.x_step(k)

    for load in loads:
        load.wait()
    vecs = v["vecs"]
    for row in range(6):
        vecs[row : row + 1] = jnp.concatenate(
            [small[s // 2, s % 2, row : row + 1, 0 : sizes.shard] for s in range(n_dp)], axis=1
        )
    v["bup"][...] = jnp.concatenate(
        [small[s // 2, s % 2, 6:7, 0 : sizes.part] for s in range(n_dp)], axis=1
    )
    seg_core.wait_recv()
    segc = v["segc"]
    for core in range(2):

        def turn(block, core=core):
            turned_ids = jnp.broadcast_to(segs[core, block, 0:1], (128, rows)).T
            segc[core, block] = turned_ids.astype(LOW)

        loop(groups, turn)
    g_qkv.z_steps()
    g_skip.finish()

    tile = min(256, width)

    def merge_tile(n):
        lane = aligned(n * tile, tile)
        merged[:, lane] = (
            dot(fr_v[...], ws[0 : nz // 2, :, :, lane].reshape(width, tile))
            + dot(sk_v[...], ws[nz // 2 : nz, :, :, lane].reshape(width, tile))
            + vecs[0:1, lane]
        )

    loop(width // tile, merge_tile)
    chunk = 64

    def norm_into(held, gain_row, target):
        def body(i):
            at = aligned(i * chunk, chunk)
            unit, _ = norm_terms(held[at])
            target[at] = (
                unit * vecs[gain_row : gain_row + 1] + vecs[gain_row + 1 : gain_row + 2]
            ).astype(LOW)

        loop(rows // chunk, body)

    def norm_back(held, gain_row, incoming, finish):
        def body(i, carry):
            at = aligned(i * chunk, chunk)
            unit, scale = norm_terms(held[at])
            t = incoming(at)
            scaled = t * vecs[gain_row : gain_row + 1]
            grad = scale * (
                scaled
                - jnp.mean(scaled, axis=-1, keepdims=True)
                - unit * jnp.mean(scaled * unit, axis=-1, keepdims=True)
            )
            finish(at, grad)
            return (
                carry[0] + jnp.sum(t * unit, axis=0, keepdims=True),
                carry[1] + jnp.sum(t, axis=0, keepdims=True),
            )

        zero = jnp.zeros((1, width), F32)
        return lax.fori_loop(0, rows // chunk, body, (zero, zero))

    normed, second, cot_all = v["normed"], v["second"], v["cot_all"]

    def share(buffer):
        swap = Exchange(place, wires)
        copies = [
            swap.copy(step, lambda: buffer.at[g], lambda: buffer.at[g])
            for step in range(1, groups)
        ]
        for copy in copies:
            copy.start()
        return copies

    norm_into(merged, 1, normed.at[g])
    normed_copies = share(normed)
    cot_copies = share(cot_all)

    kv, qt, kt = v["kv"], v["qt"], v["kt"]
    shift = v["shift"]
    pick = (
        lax.broadcasted_iota(jnp.int32, (max(8, heads), cols), 1)
        // (width // H)
        == lax.broadcasted_iota(jnp.int32, (max(8, heads), cols), 0)
    ).astype(F32)
    kv_first = wires.take(groups)

    def kv_copy(block, step):
        return wires.copy(
            lambda: (kv.at[c, block], kv.at[c, block], place.c_peer()), kv_first + step
        )

    def mix(block, step):
        rows_in = normed[block]
        for third in range(3):
            value = dot(
                rows_in,
                wqkv[:, :, :, third * cols : (third + 1) * cols].reshape(width, cols),
            ).astype(LOW)
            if third == 0:
                query = value
            else:
                kv[c, block, :, (third - 1) * cols : third * cols] = value
        kv_copy(block, step).start()
        found = 0.0
        for at in range(0, cols, 128):
            part = query[:, at : at + 128].astype(F32)
            product = part * kv[c, block, :, at : at + 128].astype(F32)
            found = found + lax.dot_general(
                pick[:, at : at + 128],
                product,
                (((1,), (1,)), ((), ())),
                precision=lax.Precision.HIGHEST,
                preferred_element_type=F32,
            )
            qt[block, at : at + 128] = (part * 0.125).T.astype(LOW)
        for head in range(heads):
            shift[block, head] = found[head : head + 1] * 0.125

    g_qkv.y_steps()
    g_qkv.finish()
    mix(g, 0)
    g_out.z_steps()
    for copy in normed_copies:
        copy.wait_recv()

    def mix_other(step):
        mix(place.g_at(-step), step)

    lax.fori_loop(1, groups, lambda step, carry: (mix_other(step), carry)[1], 0)
    g_up.z_step(1)
    g_out.y_steps()

    kv_waits = [kv_copy(place.g_at(-step), step) for step in range(groups)]
    for copy in kv_waits:
        copy.wait_recv()

    def slope_row(head):
        index = jnp.full((1, rows), g * heads + head, jnp.int32).astype(F32)
        return jnp.exp2((index + 1.0) * (-8.0 / H))

    def fill_far(block):
        place_k = lax.broadcasted_iota(jnp.int32, (rows, rows), 0) * n_blk
        place_q = lax.broadcasted_iota(jnp.int32, (rows, rows), 1) * n_blk + (block * 2 + c)
        apart = place_k - place_q
        seg_q = segs[c, block, 0:1]
        for core in range(2):

            def body(b, core=core):
                seg_k = segc[core, b].astype(F32)
                same = jnp.concatenate([seg_k] * (rows // 128), axis=1) == seg_q
                distance = jnp.abs(apart + (b * 2 + core)).astype(F32)
                far[core, b] = jnp.where(same, distance, FAR)

            loop(groups, body)

    def padded(half_value, half):
        zero = jnp.zeros_like(half_value)
        return jnp.concatenate([half_value, zero] if half == 0 else [zero, half_value], axis=0)

    head_width = width // H
    pair_width = 2 * head_width
    attt, tot = v["attt"], v["tot"]

    def score_terms(pair, core, b, queries_pad, slope, moved):
        keys = kv[core, b, :, aligned(pair * pair_width, pair_width)]
        return jnp.exp(dot(keys, queries_pad) - slope * far[core, b] - moved)

    def over_keys(body, first):
        def visit(index, carry):
            return body(lax.div(index, groups), lax.rem(index, groups), carry)

        return lax.fori_loop(0, 2 * groups, visit, first)

    def head_at(pair, half):
        return aligned(pair * pair_width + half * head_width, head_width)

    far, vt = v["far"], v["vt"]

    def attend(block):
        def body(pair):
            lanes = aligned(pair * pair_width, pair_width)
            fixed = []
            for half in range(2):
                head = pair * 2 + half
                fixed.append(
                    (padded(qt[block, head_at(pair, half)], half), slope_row(head), shift[block, head])
                )

            def keys_in(core, b, carry):
                done = []
                for half in range(2):
                    total, summed = carry[half]
                    terms = score_terms(pair, core, b, *fixed[half])
                    total = total + jnp.sum(terms, axis=0, keepdims=True)
                    done.append((total, summed + dot(vt[core, b, lanes], terms.astype(LOW))))
                return tuple(done)

            start = (jnp.zeros((1, rows), F32), jnp.zeros((pair_width, rows), F32))
            found = over_keys(keys_in, (start, start))
            for half in range(2):
                total, summed = found[half]
                tot[block, pair * 2 + half] = total
                own = summed[half * head_width : (half + 1) * head_width]
                attt[block, head_at(pair, half)] = own / total

        loop(heads // 2, body)

    att_own, att_send = v["att_own"], v["att_send"]
    att_first = wires.take(groups)

    def att_copy(step, block):
        return wires.copy(
            lambda: (att_send.at[block], att_own.at[:, own_cols], place.x_peer(step)),
            att_first + step,
        )

    def attention():
        for core in range(2):

            def turn(b, core=core):
                vt[core, b] = kv[core, b, :, cols : 2 * cols].T
                kt[core, b] = kv[core, b, :, 0:cols].T

            loop(groups, turn)

        def other(step, carry):
            block = place.g_at(step)
            fill_far(block)
            attend(block)
            att_send[block] = attt[block].T.astype(LOW)
            att_copy(step, block).start()
            return carry

        lax.fori_loop(1, groups, other, 0)
        g_up.z_step(2)
        g_out.x_steps()
        fill_far(g)
        attend(g)
        att_own[:, own_cols] = attt[g].T.astype(LOW)

    attention()
    for step in range(3, nz):
        g_up.z_step(step)
    g_out.finish()
    for step in range(1, groups):
        att_copy(step, place.g_at(step)).wait_recv()

    def middle_tile(n):
        lane = aligned(n * tile, tile)
        middle[:, lane] = merged[:, lane] + dot(
            att_own[...], wout[:, :, :, lane].reshape(width, tile)
        )

    loop(width // tile, middle_tile)
    norm_into(middle, 3, second.at[g])
    second_copies = share(second)
    g_up.y_steps()
    g_down.z_steps()
    g_up.finish()
    g_down.y_steps()
    g_down.finish()

    active, ghid = v["active"], v["ghid"]
    unit_tile = 256
    shard_rows = wdown.shape[2]

    def down_rows(u):
        if shard_rows >= unit_tile:
            per = shard_rows // unit_tile
            s = lax.div(u, per)
            return wdown[lax.div(s, 2), lax.rem(s, 2), aligned(lax.rem(u, per) * unit_tile, unit_tile)]
        per = unit_tile // (2 * shard_rows)
        return wdown[pl.ds(u * per, per)].reshape(unit_tile, width)

    for copy in cot_copies:
        copy.wait_recv()

    def feed(block):
        def body(u):
            lane = aligned(u * unit_tile, unit_tile)
            pre = dot(second[block], wup[:, :, :, lane].reshape(width, unit_tile)) + v["bup"][:, lane]
            back = dot_nt(cot_all[block], down_rows(u))
            normal = 0.5 * (1.0 + lax.erf(pre * (0.5**0.5)))
            active[block, :, lane] = (pre * normal).astype(LOW)
            slope = normal + pre * (jnp.exp(-0.5 * pre * pre) * (1.0 / math.sqrt(2.0 * math.pi)))
            ghid[block, :, lane] = (back * slope).astype(LOW)

        loop(units // unit_tile, body)

    def row_chunks(ref, most=512):
        per = min(nz, max(1, most // (2 * ref.shape[2])))
        return nz // per, per, per * 2 * ref.shape[2]

    def back_product(left, weight, store):
        count, per, size = row_chunks(weight)

        def body(j):
            value = dot_nt(left[...], weight[pl.ds(j * per, per)].reshape(size, weight.shape[3]))
            store(aligned(j * size, size), value)

        loop(count, body)

    lend = groups > 2
    p_send, p_recv = v["io"] if lend else v["p_send"], v["p_recv"]

    def store_into(ref, kind):
        def store(lane, value):
            ref[:, lane] = value.astype(kind)

        return store

    feed(g)
    for copy in second_copies:
        copy.wait_recv()
    second_first = wires.take(groups)

    def part_copy(step, first):
        return wires.copy(
            lambda: (p_send.at[part_slot(step)], p_recv.at[step - 1], place.x_peer(step)),
            first + step,
        )

    def part_slot(step):
        return 0 if groups == 2 else lax.rem(step, 2)

    def send_part(step, left, weight, first):
        if groups > 3:

            @pl.when(step > 2)
            def _():
                part_copy(step - 2, first).wait_send()

        back_product(left, weight, store_into(p_send.at[part_slot(step)], LOW))
        part_copy(step, first).start()

    def parts_sent(first):
        for step in range(max(1, groups - 2), groups):
            part_copy(step, first).wait_send()

    def other_feed(step, carry):
        block = place.g_at(step)
        feed(block)
        send_part(step, ghid.at[block], wup, second_first)
        return carry

    lax.fori_loop(1, groups, other_feed, 0)
    back_product(ghid.at[g], wup, store_into(gmid, F32))

    def down_tile(left, target, n):
        lane = aligned(n * tile, tile)
        target(lane, dot(left[...], wdown[:, :, :, lane].reshape(units, tile)))

    turned = v["turned"]

    def weight_grad(left, right, grad, left_at):
        count, per, size = row_chunks(grad, turned.shape[0])
        wide = grad.shape[3]
        step_cols = min(256, wide)
        depth = left.shape[0] if len(left.shape) == 2 else left.shape[0] * left.shape[1]

        def body(j):
            lane = aligned(j * size, size)
            part = left[:, lane] if len(left.shape) == 2 else left[:, :, lane]
            turned[0:size, 0:depth] = part.reshape(depth, size).T

            def inner(n):
                out = aligned(n * step_cols, step_cols)
                part = right[:, out] if len(right.shape) == 2 else right[:, :, out]
                value = dot(turned[0:size, 0:depth], part.reshape(depth, step_cols))
                grad[pl.ds(left_at + j * per, per), :, :, out] = value.astype(LOW).reshape(
                    per, 2, size // per // 2, step_cols
                )

            loop(wide // step_cols, inner)

        if len(left.shape) == 2 and left.shape[1] < n_dp * grad.shape[2]:
            count = count * left.shape[1] // (n_dp * grad.shape[2])
        loop(count, body)

    g_up.drain()
    g_down.drain()
    weight_grad(second, ghid, wup, 0)
    r_up = Reduce(
        place, wires, wup, h_up, False, v["c_up"], None, v["y_up"], v["z_up"], v["p_up"]
    )
    r_up.core_send(0)
    r_up.core_send(1)

    for copy in second_copies:
        copy.wait_send()

    def other_down(step, carry):
        block = place.g_at(step)

        def keep(lane, value):
            second[block, :, lane] = value.astype(LOW)

        loop(width // tile, lambda n: down_tile(active.at[block], keep, n))
        return carry

    lax.fori_loop(1, groups, other_down, 0)

    def own_down(lane, value):
        outp[:, lane] = value + vecs[5:6, lane]

    loop(width // tile, lambda n: down_tile(active.at[g], own_down, n))
    weight_grad(active, cot_all, wdown, 0)
    c_down = v["c_skip"] if v["c_skip"].shape == v["wdown"].shape[:2] + (h_down, width) else v["c_down"]
    r_down = Reduce(
        place, wires, wdown, h_down, False, c_down, None, v["y_down"], v["z_down"], v["p_down"]
    )
    r_down.core_send(0)
    r_down.core_send(1)
    sums = v["sums"]
    sums[...] = jnp.zeros_like(sums)

    def column_sums(read, count, wide):
        def body(i, total):
            return total + jnp.sum(read(i).astype(F32), axis=0, keepdims=True)

        return lax.fori_loop(0, count, body, jnp.zeros((1, wide), F32))

    per_block = rows // chunk
    ghid_sum = column_sums(
        lambda i: ghid[lax.div(i, per_block), aligned(lax.rem(i, per_block) * chunk, chunk)],
        groups * per_block,
        units,
    )
    if units >= width:
        for row in range(sizes.up_rows):
            sums[6 + row : 7 + row] = ghid_sum[:, row * width : (row + 1) * width]
    else:
        sums[6:7, 0:units] = ghid_sum
    sums[5:6] = column_sums(lambda i: cot_all[g, aligned(i * chunk, chunk)], per_block, width)
    r_up.core_add(0)
    r_up.core_add(1)

    for step in range(1, groups):
        part_copy(step, second_first).wait_recv()

    def second_in(at):
        t = gmid[at]
        for step in range(1, groups):
            t = t + p_recv[step - 1, at].astype(F32)
        return t

    gb = v["gb"]

    def second_out(at, grad):
        total = grad + cot_all[g, at].astype(F32)
        gmid[at] = total
        gb[at] = total.astype(LOW)

    gain_sum, bias_sum = norm_back(middle, 3, second_in, second_out)
    sums[3:4] = gain_sum
    sums[4:5] = bias_sum

    ga_in, ga_send = v["ga_in"], att_send
    for step in range(1, groups):
        att_copy(step, place.g_at(step)).wait_send()
    ga_first = wires.take(groups)

    def ga_copy(step):
        block = place.g_at(step)
        return wires.copy(
            lambda: (ga_send.at[block], ga_in.at[g], place.x_peer(step)), ga_first + step
        )

    count, per, size = row_chunks(wout)

    def branch_back(j):
        value = dot_nt(gb[...], wout[pl.ds(j * per, per)].reshape(size, width)).astype(LOW)
        for b in range(max(1, size // cols)):
            if size >= cols:
                ga_send[j * (size // cols) + b] = value[:, b * cols : (b + 1) * cols]
            else:
                ga_send[lax.div(j, cols // size), :, aligned(lax.rem(j, cols // size) * size, size)] = value

    loop(count, branch_back)
    for step in range(1, groups):
        ga_copy(step).start()
    ga_in[g] = ga_send[g]
    out_swap = Exchange(place, wires)
    out_copies = [
        out_swap.copy(
            step, lambda step=step: second.at[place.g_at(step)], lambda: cot_all.at[g]
        )
        for step in range(1, groups)
    ]
    r_down.core_add(0)
    r_down.core_add(1)
    g_out.drain()
    weight_grad(att_own, gb, wout, 0)
    r_out = Reduce(
        place, wires, wout, h_out, True, v["c_out"], v["x_out"], v["y_out"], v["z_out"], v["p_out"]
    )
    r_out.core_send(0)
    r_out.core_send(1)

    gm = v["gm"]

    dkv = v["dkv"]
    gat, gqt, skt = vt.at[0, 0], vt.at[0, 1], vt.at[1, 0]

    def back_attend(block, first):
        gat[...] = ga_in[block].T

        def body(pair):
            lanes = aligned(pair * pair_width, pair_width)
            later = aligned(cols + pair * pair_width, pair_width)
            fixed, scores = [], []
            for half in range(2):
                head = pair * 2 + half
                at = head_at(pair, half)
                total = tot[block, head]
                grad_att = gat[at].astype(F32)
                scaled = padded(grad_att / total, half)
                grad_total = -jnp.sum(grad_att * attt[block, at], axis=0, keepdims=True) / total
                queries = qt[block, at]
                scores.append((padded(queries, half), slope_row(head), shift[block, head]))
                fixed.append(
                    (
                        scaled.astype(LOW),
                        scaled.T.astype(LOW),
                        grad_total,
                        padded(queries.astype(F32), half).T.astype(LOW),
                    )
                )

            def keys_in(core, b, carry):
                values = kv[core, b, :, later]
                key_grad, value_grad, done = 0.0, 0.0, []
                for half in range(2):
                    shift_sum, query_grad = carry[half]
                    scaled, scaled_nat, grad_total, queries_nat = fixed[half]
                    terms = score_terms(pair, core, b, *scores[half])
                    grad_score = terms * (dot(values, scaled) + grad_total)
                    shift_sum = shift_sum - jnp.sum(grad_score, axis=0, keepdims=True)
                    grad_low = grad_score.astype(LOW)
                    value_grad = value_grad + dot(terms.astype(LOW), scaled_nat)
                    key_grad = key_grad + dot(grad_low, queries_nat)
                    done.append((shift_sum, query_grad + dot(kt[core, b, lanes], grad_low)))
                for at, found in ((lanes, key_grad), (later, value_grad)):
                    if not first:
                        found = found + dkv[core, b, :, at].astype(F32)
                    dkv[core, b, :, at] = found.astype(LOW)
                return tuple(done)

            start = (jnp.zeros((1, rows), F32), jnp.zeros((pair_width, rows), F32))
            found = over_keys(keys_in, (start, start))
            for half in range(2):
                shift_sum, query_grad = found[half]
                at = head_at(pair, half)
                own = query_grad[half * head_width : (half + 1) * head_width]
                own_keys = kt[c, block, at].astype(F32)
                gqt[at] = (0.125 * (own + shift_sum * own_keys)).astype(LOW)
                skt[at] = (shift_sum * qt[block, at].astype(F32)).astype(LOW)

        loop(heads // 2, body)
        gm[block, :, 0:cols] = gqt[...].T
        dkv[c, block, :, 0:cols] = dkv[c, block, :, 0:cols] + skt[...].T

    dkv_wire = wires.take(1)

    def dkv_copy():
        return wires.copy(
            lambda: (dkv.at[1 - c], gm.at[:, :, cols : 3 * cols], place.c_peer()), dkv_wire
        )

    def back_attention():
        fill_far(g)
        back_attend(g, True)
        r_out.core_add(0)
        r_out.core_add(1)
        r_up.y_add()
        for step in range(1, groups):
            ga_copy(step).wait_recv()
        for copy in cot_copies:
            copy.wait_send()
        for copy in out_copies:
            copy.start()

        def other(step, carry):
            block = place.g_at(-step)
            fill_far(block)
            back_attend(block, False)
            return carry

        lax.fori_loop(1, groups, other, 0)

        dkv_copy().start()
        r_up.z_add()
        r_down.y_add()
        r_out.x_add(0)
        r_out.x_add(1)
        dkv_copy().wait_recv()

        def merge(b):
            gm[b, :, cols : 3 * cols] = gm[b, :, cols : 3 * cols] + dkv[c, b]

        loop(groups, merge)

    back_attention()

    parts_sent(second_first)
    mix_first = wires.take(groups)

    def other_mix(step, carry):
        block = place.g_at(step)
        send_part(step, gm.at[block], wqkv, mix_first)
        return carry

    lax.fori_loop(1, groups, other_mix, 0)
    for copy in out_copies:
        copy.wait_recv()
    ob = second.at[g]

    def out_rows(i):
        at = aligned(i * chunk, chunk)
        value = middle[at] + outp[at]
        for step in range(1, groups):
            value = value + cot_all[place.g_at(-step), at].astype(F32)
        ob[at] = value.astype(LOW)

    loop(rows // chunk, out_rows)
    stores = [pltpu.make_async_copy(ob, v["o_out"].at[0], local.at[0])]
    stores[0].start()
    back_product(gm.at[g], wqkv, store_into(middle, F32))
    g_qkv.drain()
    weight_grad(normed, gm, wqkv, 0)
    c_qkv = v["c_up"].at[:, :, :, 0 : 3 * cols]
    r_qkv = Reduce(
        place, wires, wqkv, h_qkv, False, c_qkv, None, v["y_qkv"], v["z_qkv"], v["p_qkv"]
    )
    r_qkv.core_send(0)
    r_qkv.core_send(1)
    r_down.z_add()
    r_out.y_add()
    r_qkv.core_add(0)
    r_qkv.core_add(1)
    for step in range(1, groups):
        part_copy(step, mix_first).wait_recv()

    def first_in(at):
        t = middle[at]
        for step in range(1, groups):
            t = t + p_recv[step - 1, at].astype(F32)
        return t

    def first_out(at, grad):
        gb[at] = (grad + gmid[at]).astype(LOW)

    gain_sum, bias_sum = norm_back(merged, 1, first_in, first_out)
    sums[1:2] = gain_sum
    sums[2:3] = bias_sum
    sums[0:1] = column_sums(lambda i: gb[aligned(i * chunk, chunk)], per_block, width)

    sum_in = v["sum_in"]

    def sum_swap(slot, peer):
        copy = wires.copy(lambda: (sums, sum_in.at[slot], peer))
        copy.start()
        return copy

    sum_core = sum_swap(0, place.c_peer())

    gj = cot_all

    def joined_back():
        _, _, size = row_chunks(ws)
        span = width // size

        def store(lane_index, value):
            gj[lax.div(lane_index, span), :, aligned(lax.rem(lane_index, span) * size, size)] = value

        count, per, size = row_chunks(ws)

        def body(j):
            value = dot_nt(gb[...], ws[pl.ds(j * per, per)].reshape(size, width))
            store(j, value.astype(LOW))

        loop(count, body)
        for half, name in enumerate(("o_frames", "o_skip")):
            stores.append(pltpu.make_async_copy(gj.at[half], v[name].at[0], local.at[1 + half]))
            stores[-1].start()

    if lend:
        parts_sent(mix_first)
        for store in stores:
            store.wait()
        stores.clear()
        for load in input_loads():
            load.start()
        for load in input_loads():
            load.wait()
    apart = ws.shape == wdown.shape
    grad_skip = wdown if apart else ws
    g_skip.drain()
    r_up.drain()
    r_down.drain()
    if not apart:
        joined_back()
    weight_grad(fr_v, gb, grad_skip, 0)
    weight_grad(sk_v, gb, grad_skip, nz // 2)
    r_skip = Reduce(
        place, wires, grad_skip, h_skip, True, v["c_skip"], v["x_skip"], v["y_skip"], v["z_skip"],
        v["p_skip"],
    )
    r_skip.core_send(0)
    r_skip.core_send(1)
    if apart:
        joined_back()
    r_skip.core_add(0)
    r_skip.core_add(1)
    r_qkv.y_add()
    sum_core.wait()
    sums[...] = sums[...] + sum_in[0]
    sum_x = [sum_swap(step, place.x_peer(step)) for step in range(1, groups)]
    r_out.z_add()
    r_up.spread_on()
    r_down.spread_on()
    for copy in sum_x:
        copy.wait()
    for step in range(1, groups):
        sums[0:6] = sums[0:6] + sum_in[step, 0:6]
    sum_y = sum_swap(groups, place.y_peer())
    r_qkv.z_add()
    r_skip.x_add(0)
    sum_y.wait()
    sums[...] = sums[...] + sum_in[groups]
    sum_z = [sum_swap(groups + step, place.z_peer(step)) for step in range(1, nz)]
    r_out.spread_on()
    r_skip.x_add(1)
    r_qkv.spread_on()
    for copy in sum_z:
        copy.wait()
    for step in range(1, nz):
        sums[...] = sums[...] + sum_in[groups + step]
    o_up = v["o_up"]
    o_up[g] = sums[...]
    v["o_small"][...] = sums[...]
    up_swap = Exchange(place, wires)
    up_copies = [up_swap.copy(step, lambda: o_up.at[g], lambda: o_up.at[g]) for step in range(1, groups)]
    for copy in up_copies:
        copy.start()
    r_skip.y_add()
    r_skip.z_add()
    r_skip.spread_on()

    for copy in up_copies:
        copy.wait()
    for reduced in (r_up, r_down, r_out, r_qkv, r_skip):
        reduced.finish()
    for reduced in (r_out, r_qkv, r_skip):
        reduced.drain()
    for gathered in (g_small, g_out):
        gathered.drain()
    for copy in seg_copies + [seg_core] + normed_copies + kv_waits:
        copy.wait_send()
    for copy in out_copies:
        copy.wait_send()
    for step in range(1, groups):
        ga_copy(step).wait_send()
    if not lend:
        parts_sent(mix_first)
    dkv_copy().wait_send()
    for store in stores:
        store.wait()


def per_device(sizes, *args):
    (
        frames, skip_frames, cotangent, seg_ids, positions,
        w_skip, b_skip, gain_attn, bias_attn, w_qkv, w_out,
        gain_ffn, bias_ffn, w_up, b_up, w_down, b_down,
    ) = args
    del positions
    n_dp, nz, groups = sizes.n_dp, sizes.nz, sizes.groups
    rows, width, cols, units = sizes.rows, sizes.width, sizes.cols, sizes.units
    heads, part, shard = sizes.heads, sizes.part, sizes.shard
    depth = w_up.shape[0]
    if not sizes.direct:
        w_up = (
            w_up.reshape(depth, n_dp, groups, part).transpose(0, 2, 1, 3).reshape(depth, groups * units)
        )
        group = lax.axis_index("blk") // 2
        b_up = lax.dynamic_slice_in_dim(b_up, group * part, part)
    r_skip, r_down = w_skip.shape[0], w_down.shape[0] // groups
    span = -(-max(shard, part) // 128) * 128

    def low(*shape):
        return pltpu.VMEM(shape, LOW)

    def full(*shape):
        return pltpu.VMEM(shape, F32)

    same = (r_skip, width) == (r_down, width)
    scratch = [
        low(2, rows, width), low(groups, rows, width),
        low(nz, 2, r_skip, width), low(nz, 2, depth, 3 * cols), low(nz, 2, depth, width),
        low(nz, 2, depth, units), low(nz, 2, r_down, width),
        full(nz, 2, 8, span), full(8, width), full(1, units),
        full(2, groups, 8, rows), low(2, groups, rows, 128),
        full(rows, width), full(rows, width), full(rows, width),
        low(groups, rows, width), low(groups, rows, width),
        low(2, groups, rows, 2 * cols),
        low(groups, cols, rows), low(2, groups, cols, rows),
        full(groups, heads, 1, rows), full(groups, cols, rows), full(groups, heads, 1, rows),
        low(rows, width), low(groups, rows, cols),
        low(groups, rows, units), low(groups, rows, units),
        low(1, 16, 128) if groups > 2 else low(1, rows, width),
        low(groups - 1, rows, width),
        low(rows, width), low(groups, rows, cols),
        low(groups, rows, 3 * cols),
        low(2, groups, rows, 2 * cols),
        full(2, groups, rows, rows), low(2, groups, cols, rows),
        low(nz, 2, r_skip // 2, width), low(nz, 2, depth // 2, width),
        low(nz, 2, depth // 2, units),
        low(1, 1, 16, 128) if same else low(nz, 2, r_down // 2, width),
        low(groups - 1, nz, 2, r_skip // 2, cols), low(groups - 1, nz, 2, depth // 2, cols),
        low(nz, r_skip // 2, cols), low(nz, depth // 2, 3 * cols), low(nz, depth // 2, cols),
        low(nz, depth // 2, units), low(nz, r_down // 2, width),
        low(nz - 1, r_skip // 2, cols), low(nz - 1, depth // 2, 3 * cols),
        low(nz - 1, depth // 2, cols), low(nz - 1, depth // 2, units),
        low(nz - 1, r_down // 2, width),
        full(8, width), full(groups + nz, 8, width),
        low(512 if groups * rows <= 512 else 256, groups * rows), full(rows, width),
    ]
    wires = 200 if groups * n_dp <= 16 else 1200
    scratch += [pltpu.SemaphoreType.DMA((wires,)), pltpu.SemaphoreType.DMA((wires,))]
    scratch += [pltpu.SemaphoreType.DMA((16,))]
    hbm, vmem = pl.BlockSpec(memory_space=pl.ANY), pl.BlockSpec(memory_space=pltpu.VMEM)
    whole = jax.ShapeDtypeStruct((1, rows, width), LOW)

    def piece(*shape):
        return jax.ShapeDtypeStruct((groups, 2) + shape, LOW)

    vectors = (b_skip, gain_attn, bias_attn, gain_ffn, bias_ffn, b_down, b_up)
    found = pl.pallas_call(
        functools.partial(kernel, sizes),
        out_shape=(
            whole, whole, whole,
            piece(r_skip // 2, cols), piece(depth // 2, 3 * cols), piece(depth // 2, cols),
            piece(depth // 2, units), piece(r_down // 2, width),
            jax.ShapeDtypeStruct((8, width), F32), jax.ShapeDtypeStruct((groups, 8, width), F32),
        ),
        in_specs=[hbm] * 3 + [vmem] * 8 + [hbm] * 5,
        out_specs=[hbm] * 3 + [vmem] * 7,
        scratch_shapes=scratch,
        compiler_params=pltpu.CompilerParams(
            collective_id=0, has_side_effects=True, vmem_limit_bytes=64 * 2**20
        ),
    )(
        frames, skip_frames, cotangent, seg_ids,
        *[vector.reshape(1, -1) for vector in vectors],
        w_skip, w_qkv, w_out, w_up, w_down,
    )
    output, grad_frames, grad_skip, p_skip, p_qkv, p_out, p_up, p_down, small, up = found

    def joined(pieces, inner):
        half = pieces.shape[2]
        split = pieces.reshape(groups, 2, half, inner, -1).transpose(1, 2, 3, 0, 4)
        return split.reshape(2 * half, -1).astype(F32)

    own = lax.dynamic_slice_in_dim(small, lax.axis_index("dp") * shard, shard, 1)
    flat = up[:, 6 : 6 + sizes.up_rows].reshape(groups, -1)
    own_up = lax.dynamic_slice_in_dim(flat, lax.axis_index("dp") * part, part, 1).reshape(-1)
    return (
        output, grad_frames, grad_skip,
        joined(p_skip, 1), own[0], own[1], own[2], joined(p_qkv, 3), joined(p_out, 1),
        own[3], own[4], joined(p_up, n_dp), own_up,
        p_down.reshape(-1, width).astype(F32), own[5],
    )


def solution(mesh):
    rows, lone = P("dp", None), P("dp")
    frames = P("dp", "blk", None)
    in_specs = (frames,) * 3 + (P("dp", "blk"),) * 2
    in_specs += (rows, lone, lone, lone, rows, rows, lone, lone, rows, lone, rows, lone)
    out_specs = (frames,) * 3
    out_specs += (rows, lone, lone, lone, rows, rows, lone, lone, rows, lone, rows, lone)

    def body(*args):
        return per_device(Sizes(mesh.shape, args[0], args[13]), *args)

    return jax.shard_map(
        body, mesh=mesh, in_specs=in_specs, out_specs=out_specs, check_vma=False
    )
```

```python
import functools
import math

import jax
import jax.numpy as jnp
from jax import lax
from jax.experimental import pallas as pl
from jax.experimental.pallas import tpu as pltpu
from jax.sharding import PartitionSpec as P

H = 16
EPSILON = 1e-05
LOW = jnp.bfloat16
F32 = jnp.float32
MESH = pl.DeviceIdType.MESH
FAR = 1e30


def dot(left, right):
    return jnp.dot(left, right, preferred_element_type=F32)


def dot_nt(left, right):
    return lax.dot_general(left, right, (((1,), (1,)), ((), ())), preferred_element_type=F32)


def loop(count, body):
    def visit(index, carry):
        body(index)
        return carry

    lax.fori_loop(0, count, visit, 0)


def loop_from(first, last, body):
    def visit(index, carry):
        body(index)
        return carry

    lax.fori_loop(first, last, visit, 0)


def aligned(start, size):
    return pl.ds(pl.multiple_of(start, size), size)


class Sizes:
    def __init__(self, mesh_shape, frames, w_up):
        self.n_dp, self.n_blk = mesh_shape["dp"], mesh_shape["blk"]
        self.nz = self.n_dp // 2
        self.groups = self.n_blk // 2
        self.rows = frames.shape[1]
        self.width = frames.shape[2]
        self.hidden = w_up.shape[1]
        self.shard = self.width // self.n_dp
        self.cols = self.width // self.groups
        self.heads = H // self.groups
        self.units = self.hidden // self.groups
        self.part = self.units // self.n_dp
        self.direct = self.part % 128 == 0
        self.share = max(1, self.width // (self.groups + 2) // 128) * 128
        self.up_rows = -(-self.units // self.width)


class Wires:
    def __init__(self, place, send_sems, recv_sems):
        self.place, self.send_sems, self.recv_sems, self.used = place, send_sems, recv_sems, 0

    def take(self, count=1):
        first = self.used
        self.used += count
        assert self.used <= self.send_sems.shape[0]
        return first

    def copy(self, ends, index=None):
        return Copy(self, ends, self.take() if index is None else index)


class Copy:
    def __init__(self, wires, ends, index):
        self.wires, self.ends, self.index = wires, ends, index

    def made(self):
        source, target, peer = self.ends()
        index = self.index
        if isinstance(index, tuple):
            index = index[0] + self.wires.place.z + index[1]
        return pltpu.make_async_remote_copy(
            src_ref=source,
            dst_ref=target,
            send_sem=self.wires.send_sems.at[index],
            recv_sem=self.wires.recv_sems.at[index],
            device_id=peer,
            device_id_type=MESH,
        )

    def start(self):
        self.made().start()

    def wait_send(self):
        self.made().wait_send()

    def wait_recv(self):
        self.made().wait_recv()

    def wait(self):
        self.made().wait()


class Place:
    def __init__(self, sizes):
        self.dp, self.blk = lax.axis_index("dp"), lax.axis_index("blk")
        self.z, self.y = lax.div(self.dp, 2), lax.rem(self.dp, 2)
        self.g, self.c = lax.div(self.blk, 2), lax.rem(self.blk, 2)
        self.sizes = sizes

    def z_at(self, step):
        nz = self.sizes.nz
        return lax.rem(self.z + (step + nz), nz)

    def g_at(self, step):
        groups = self.sizes.groups
        return lax.rem(self.g + (step + groups), groups)

    def z_peer(self, step):
        return (self.z_at(step) * 2 + self.y, self.blk)

    def z_next(self, way):
        return ((self.z + way) * 2 + self.y, self.blk)

    def if_z(self, *distances):
        low, high = min(distances + (0,)), max(distances + (0,))
        if low < 0 and high > 0:
            return pl.when(jnp.logical_and(self.z >= -low, self.z < self.sizes.nz - high))
        return pl.when(self.z >= -low if low < 0 else self.z < self.sizes.nz - high)

    def y_peer(self):
        return (self.z * 2 + 1 - self.y, self.blk)

    def x_peer(self, step):
        return (self.dp, self.g_at(step) * 2 + self.c)

    def c_peer(self):
        return (self.dp, self.g * 2 + 1 - self.c)


class Gather:
    def __init__(self, place, wires, ref, half, spread=0, span=None, whole_core=False):
        self.place, self.wires, self.ref = place, wires, ref
        self.half, self.spread, self.span, self.whole_core = half, spread, span, whole_core
        self.nz = place.sizes.nz
        self.groups = place.sizes.groups if spread else 1
        self.z_wires = {way: wires.take(self.nz) for way in (1, -1)}
        self.y_wires = wires.take(self.nz)
        self.x_wires = {
            (step, far): wires.take(self.nz) for step in range(1, self.groups) for far in (0, 1)
        }
        self.c_wires = {
            (step, far): 0 if whole_core else wires.take(self.nz)
            for step in range(self.groups)
            for far in (0, 1)
        }

    def at(self, distance, far, step=0):
        place = self.place
        z_index = place.z + distance
        y_index = 1 - place.y if far else place.y
        if self.whole_core:
            return self.ref.at[z_index, y_index]
        rows = aligned(place.c * self.half, self.half)
        if self.span:
            return self.ref.at[z_index, y_index, rows, self.span[0] : self.span[1]]
        if not self.spread:
            return self.ref.at[z_index, y_index, rows]
        cols = aligned(place.g_at(-step) * self.spread, self.spread)
        return self.ref.at[z_index, y_index, rows, cols]

    def copy(self, first, peer, distance, far, step=0):
        def ends():
            piece = self.at(distance, far, step)
            return piece, piece, peer()

        return self.wires.copy(ends, (first, distance))

    def z_copy(self, way, distance):
        return self.copy(self.z_wires[way], lambda: self.place.z_next(way), distance, 0)

    def y_copy(self, distance):
        return self.copy(self.y_wires, self.place.y_peer, distance, 0)

    def y_arrival(self, distance):
        return self.copy(self.y_wires, self.place.y_peer, distance, 1)

    def x_copy(self, step, distance, far):
        first = self.x_wires[step, far]
        return self.copy(first, lambda: self.place.x_peer(step), distance, far)

    def c_copy(self, step, distance, far):
        return self.copy(self.c_wires[step, far], self.place.c_peer, distance, far, step)

    def each(self, reach, body):
        if reach == 0:
            body(0)
            return
        for distance in (-reach, reach):
            self.place.if_z(distance)(functools.partial(body, distance))

    def start(self):
        for way in (1, -1):
            self.place.if_z(way)(lambda way=way: self.z_copy(way, 0).start())

    def own(self):
        self.forward(0, 0)

    def forward(self, distance, far):
        if not far:
            self.y_copy(distance).start()
        for step in range(1, self.groups):
            self.x_copy(step, distance, far).start()
        if not self.whole_core:
            self.c_copy(0, distance, far).start()

    def z_step(self, reach):
        def body(distance):
            way = 1 if distance < 0 else -1
            self.z_copy(way, distance).wait_recv()
            self.place.if_z(way)(lambda: self.z_copy(way, distance).start())
            self.forward(distance, 0)

        self.each(reach, body)

    def y_step(self, reach):
        def body(distance):
            self.y_arrival(distance).wait_recv()
            self.forward(distance, 1)

        self.each(reach, body)

    def x_step(self, reach, far):
        def body(distance):
            for step in range(1, self.groups):
                self.x_copy(step, distance, far).wait_recv()
                self.c_copy(step, distance, far).start()

        self.each(reach, body)

    def z_steps(self):
        for reach in range(1, self.nz):
            self.z_step(reach)

    def y_steps(self):
        for reach in range(self.nz):
            self.y_step(reach)

    def x_steps(self):
        for far in (0, 1):
            for reach in range(self.nz):
                self.x_step(reach, far)

    def c_wait(self, reach, far):
        def body(distance):
            for step in range(self.groups):
                self.c_copy(step, distance, far).wait_recv()

        self.each(reach, body)

    def finish(self):
        for far in (0, 1):
            for reach in range(self.nz):
                self.c_wait(reach, far)

    def drain(self):
        def body(distance):
            for way in (1, -1) if distance == 0 else (1,) if distance < 0 else (-1,):
                self.place.if_z(way)(lambda way=way: self.z_copy(way, distance).wait_send())
            self.y_copy(distance).wait_send()
            for first in self.x_wires:
                self.x_copy(first[0], distance, first[1]).wait_send()
            if not self.whole_core:
                for first in self.c_wires:
                    self.c_copy(first[0], distance, first[1]).wait_send()

        for reach in range(self.nz):
            self.each(reach, body)


class Exchange:
    def __init__(self, place, wires):
        self.place, self.groups = place, place.sizes.groups
        self.wires = wires
        self.first = wires.take(self.groups)

    def copy(self, step, source, target):
        return self.wires.copy(
            lambda: (source(), target(), self.place.x_peer(step)), self.first + step
        )


class Reduce:
    def __init__(self, place, wires, grad, half, spread, core_in, x_in, y_in, z_in, out):
        self.place, self.wires, self.grad, self.half, self.spread = place, wires, grad, half, spread
        self.core_in, self.x_in, self.y_in, self.z_in, self.out = core_in, x_in, y_in, z_in, out
        self.nz, self.groups = place.sizes.nz, place.sizes.groups
        self.core_copies, self.x_copies, self.y_copies, self.z_copies = {}, {}, {}, {}
        self.fin_copies, self.fwd_copies = {}, {}

    def side(self, part):
        return 1 - self.place.y if part == 0 else self.place.y

    def core_send(self, part):
        def ends():
            side = self.side(part)
            rows = aligned((1 - self.place.c) * self.half, self.half)
            return self.grad.at[:, side, rows], self.core_in.at[:, side], self.place.c_peer()

        copy = self.wires.copy(ends)
        copy.start()
        self.core_copies[part] = copy

    def core_add(self, part):
        side = self.side(part)
        rows = aligned(self.place.c * self.half, self.half)
        self.core_copies[part].wait_recv()

        def body(z):
            self.core_in[z, side] = self.core_in[z, side] + self.grad[z, side, rows]

        loop(self.nz, body)
        if self.spread:
            cols = self.place.sizes.cols
            for step in range(1, self.groups):
                def ends(step=step):
                    side = self.side(part)
                    theirs = aligned(self.place.g_at(step) * cols, cols)
                    return (
                        self.core_in.at[:, side, :, theirs],
                        self.x_in.at[step - 1, :, side],
                        self.place.x_peer(step),
                    )

                copy = self.wires.copy(ends)
                copy.start()
                self.x_copies[part, step] = copy
        elif part == 0:
            self.y_send()

    def x_add(self, part):
        side = self.side(part)
        cols = self.place.sizes.cols
        mine = aligned(self.place.g * cols, cols)
        for step in range(1, self.groups):
            self.x_copies[part, step].wait_recv()

        def body(z):
            total = self.core_in[z, side, :, mine].astype(F32)
            for step in range(1, self.groups):
                total = total + self.x_in[step - 1, z, side].astype(F32)
            self.x_in[0, z, side] = total.astype(LOW)

        loop(self.nz, body)
        if part == 0:
            self.y_send()

    def held(self):
        return self.x_in.at[0] if self.spread else self.core_in

    def y_send(self):
        for step in [*range(1, self.nz), 0]:

            def ends(step=step):
                z_index = self.place.z_at(step)
                source = self.held().at[z_index, self.side(0)]
                return source, self.y_in.at[z_index], self.place.y_peer()

            self.y_copies[step] = self.wires.copy(ends)
            self.y_copies[step].start()

    def y_add(self, step):
        self.y_copies[step].wait_recv()
        z_index, side, held = self.place.z_at(step), self.side(1), self.held()
        self.y_in[z_index] = self.y_in[z_index] + held[z_index, side]
        if step:
            copy = self.wires.copy(
                lambda: (
                    self.y_in.at[self.place.z_at(step)],
                    self.z_in.at[step - 1],
                    self.place.z_peer(step),
                )
            )
            copy.start()
            self.z_copies[step] = copy

    def y_tasks(self):
        steps = [*range(1, self.nz), 0]
        return [functools.partial(self.y_add, step) for step in steps]

    def y_sent(self):
        for copy in self.y_copies.values():
            copy.wait_send()
        self.y_copies.clear()

    def z_add(self):
        place = self.place
        for step in range(1, self.nz):
            self.z_copies[step].wait_recv()

        def body(i):
            at = aligned(i * 16, 16)
            total = self.y_in[place.z, at].astype(F32)
            for step in range(1, self.nz):
                total = total + self.z_in[step - 1, at].astype(F32)
            self.out[place.g, place.c, at] = total.astype(LOW)

        loop(self.half // 16, body)
        for step in range(1, self.groups):
            self.fin_copies[step] = self.wires.copy(
                lambda step=step: self.spot(0) * 2 + (place.x_peer(step),)
            )
            self.fin_copies[step].start()
        self.forward(0)

    def spread_on(self):
        for step in range(1, self.groups):
            self.fin_copies[step].wait_recv()
            self.forward(step)

    def spot(self, step):
        return (self.out.at[self.place.g_at(-step), self.place.c],)

    def forward(self, step):
        self.fwd_copies[step] = self.wires.copy(
            lambda: self.spot(step) * 2 + (self.place.c_peer(),)
        )
        self.fwd_copies[step].start()

    def core_sent(self):
        for copy in self.core_copies.values():
            copy.wait_send()
        self.core_copies.clear()

    def drain(self):
        self.core_sent()
        self.y_sent()
        for copies in (self.x_copies, self.z_copies, self.fin_copies):
            for copy in copies.values():
                copy.wait_send()

    def finish(self):
        for copy in self.fwd_copies.values():
            copy.wait()


def norm_terms(held):
    centred = held - jnp.mean(held, axis=-1, keepdims=True)
    scale = lax.rsqrt(jnp.mean(centred * centred, axis=-1, keepdims=True) + EPSILON)
    return centred * scale, scale


def kernel(sizes, *refs):
    names = (
        "frames", "skip", "cot", "seg", "b_skip", "gain_a", "bias_a", "gain_f", "bias_f",
        "b_down", "b_up", "w_skip", "w_qkv", "w_out", "w_up", "w_down", "o_out", "o_frames",
        "o_skip", "p_skip", "p_qkv", "p_out", "p_up", "p_down", "o_small", "o_up", "io",
        "cot_all", "ws", "wqkv", "wout", "wup", "wdown", "small", "vecs", "bup", "segs", "segc",
        "merged", "middle", "gmid", "normed", "second", "kv", "qt", "kt", "shift", "attt", "tot",
        "att_own", "att_send", "active", "ghid", "p_send", "p_recv", "gb", "ga_in", "gm",
        "far", "vt", "c_skip", "c_out", "c_up", "c_down", "x_skip", "x_out", "y_skip", "y_qkv",
        "y_out", "y_up", "y_down", "z_skip", "z_qkv", "z_out", "z_up", "z_down", "joined", "gmx", "grad_down", "sums",
        "sum_in", "turned", "send_sems", "recv_sems", "local_sems", "free_sem",
    )
    assert len(names) == len(refs), (len(names), len(refs))
    v = dict(zip(names, refs))
    place = Place(sizes)
    wires = Wires(place, v["send_sems"], v["recv_sems"])
    local = v["local_sems"]
    nz, groups, n_dp, n_blk = sizes.nz, sizes.groups, sizes.n_dp, sizes.n_blk
    rows, width, cols, units = sizes.rows, sizes.width, sizes.cols, sizes.units
    heads = sizes.heads
    z, y, g, c = place.z, place.y, place.g, place.c

    def each_group(body):
        if groups == 2:
            body(1)
        else:
            loop_from(1, groups, body)

    tasks = []

    def work(count=None):
        for task in tasks[:count]:
            task()
        del tasks[:count]

    barrier = pltpu.get_barrier_semaphore()
    partners = [place.z_peer(step) for step in range(1, nz)] + [place.y_peer()]
    partners += [place.x_peer(step) for step in range(1, groups)] + [place.c_peer()]
    for partner in partners:
        pl.semaphore_signal(barrier, inc=1, device_id=partner, device_id_type=MESH)

    fr_v, sk_v = v["io"].at[0], v["io"].at[1]

    def input_loads():
        return [
            pltpu.make_async_copy(v["frames"].at[0], fr_v, local.at[0]),
            pltpu.make_async_copy(v["skip"].at[0], sk_v, local.at[1]),
        ]

    loads = input_loads() + [
        pltpu.make_async_copy(v["cot"].at[0], v["cot_all"].at[g], local.at[2]),
    ]

    h_skip, h_qkv = v["ws"].shape[2] // 2, v["wqkv"].shape[2] // 2
    h_out, h_up, h_down = v["wout"].shape[2] // 2, v["wup"].shape[2] // 2, v["wdown"].shape[2] // 2

    stages = {}

    def fetch(name, start, size, tops, index):
        copies = [
            pltpu.make_async_copy(
                v[name].at[aligned(start, size), part * width : (part + 1) * width],
                buffer.at[top : top + size],
                local.at[index + part],
            )
            for part, (buffer, top) in enumerate(tops)
        ]
        for copy in copies:
            copy.start()
        stages[name] = copies

    merged, middle, gmid = v["merged"], v["middle"], v["gmid"]
    up_tops = [
        (middle, h_down), (middle, h_down + h_up), (merged, h_skip + h_out), (gmid, 3 * h_qkv)
    ]
    fetch("w_skip", c * h_skip, h_skip, [(merged, 0)], 3)
    fetch("w_qkv", c * h_qkv, h_qkv, [(gmid, third * h_qkv) for third in range(3)], 4)
    fetch("w_out", c * h_out, h_out, [(merged, h_skip)], 7)
    fetch("w_up", c * h_up, h_up, up_tops, 8)
    fetch("w_down", (g * 2 + c) * h_down, h_down, [(middle, 0)], 12)
    for load in loads:
        load.start()
    ws, wqkv, wout, wup, wdown = v["ws"], v["wqkv"], v["wout"], v["wup"], v["wdown"]
    own_cols = aligned(g * cols, cols)

    def arrived(name):
        for copy in stages[name]:
            copy.wait()

    arrived("w_skip")
    share, shared = sizes.share, groups * sizes.share
    own_share, skip_rows = aligned(g * share, share), aligned(c * h_skip, h_skip)
    ws[z, y, skip_rows, own_share] = merged[0:h_skip, own_share].astype(LOW)
    if shared < width:
        ws[z, y, skip_rows, shared:width] = merged[0:h_skip, shared:width].astype(LOW)
    arrived("w_qkv")
    for third in range(3):
        wqkv[z, y, aligned(c * h_qkv, h_qkv), third * cols : (third + 1) * cols] = gmid[
            third * h_qkv : (third + 1) * h_qkv, own_cols
        ].astype(LOW)
    arrived("w_out")
    wout[z, y, aligned(c * h_out, h_out), own_cols] = merged[
        h_skip : h_skip + h_out, own_cols
    ].astype(LOW)
    arrived("w_up")
    up_rows = aligned(c * h_up, h_up)
    if sizes.direct:
        part = sizes.part
        per_row = width // (part * groups)
        for s in range(n_dp):
            buffer, top = up_tops[s // per_row]
            lane = aligned(g * part + s % per_row * part * groups, part)
            wup[z, y, up_rows, s * part : (s + 1) * part] = buffer[top : top + h_up, lane].astype(LOW)
    else:
        for index, (buffer, top) in enumerate(up_tops):

            @pl.when(lax.div(g * units, width) == index)
            def _(buffer=buffer, top=top):
                lane = aligned(lax.rem(g * units, width), units)
                wup[z, y, up_rows] = buffer[top : top + h_up, lane].astype(LOW)

    arrived("w_down")
    wdown[z, y, aligned(c * h_down, h_down)] = middle[0:h_down].astype(LOW)

    small = v["small"]
    for row, name in enumerate(("b_skip", "gain_a", "bias_a", "gain_f", "bias_f", "b_down")):
        small[z, y, row : row + 1, 0 : sizes.shard] = v[name][...].astype(LOW).astype(F32)
    if sizes.direct:
        own_up = v["b_up"][:, aligned(g * sizes.part, sizes.part)]
    else:
        own_up = v["b_up"][...]
    small[z, y, 6:7, 0 : sizes.part] = own_up.astype(LOW).astype(F32)
    segs = v["segs"]
    segs[c, g] = jnp.broadcast_to(v["seg"][...].astype(F32), (8, rows))

    pl.semaphore_wait(barrier, len(partners))

    g_small = Gather(place, wires, small, 0, whole_core=True)
    g_skip = Gather(place, wires, v["ws"], h_skip, spread=share)
    g_rest = Gather(place, wires, v["ws"], h_skip, span=(shared, width))
    g_qkv = Gather(place, wires, v["wqkv"], h_qkv)
    g_out = Gather(place, wires, v["wout"], h_out, spread=cols)
    g_up = Gather(place, wires, v["wup"], h_up)
    g_down = Gather(place, wires, v["wdown"], h_down)
    skips = [g_skip, g_rest] if shared < width else [g_skip]
    seg_swap = Exchange(place, wires)
    seg_copies = []
    for step in range(1, groups):
        seg_copies.append(seg_swap.copy(step, lambda: segs.at[c, g], lambda: segs.at[c, g]))
        seg_copies[-1].start()
    for gather in [g_small] + skips:
        gather.start()
    for gather in skips + [g_small, g_qkv]:
        gather.own()

    joined_copies, joined_parts = [], []
    if sizes.pair:
        for load in loads:
            load.wait()
        lines = rows // 4
        for part in range(8):
            at = part // 4, pl.ds(part % 4 * lines, lines)
            copy = Exchange(place, wires).copy(
                1, lambda at=at: v["io"].at[at], lambda at=at: v["joined"].at[at]
            )
            joined_copies.append(copy)
            joined_parts.append(copy)

    def send_joined(count):
        for copy in joined_parts[:count]:
            copy.start()
        del joined_parts[:count]

    send_joined(1)
    for reach in range(1, nz):
        g_skip.z_step(reach)
        if reach == nz - 1:
            g_qkv.start()
        if reach > 1:
            g_skip.y_step(reach - 2)
        g_skip.x_step(reach - 1, 0)
        send_joined(1)
    for copy in seg_copies:
        copy.wait_recv()
    seg_core = wires.copy(lambda: (segs.at[c], segs.at[c], place.c_peer()))
    seg_core.start()
    for gather in skips[1:] + [g_small]:
        gather.z_steps()
    g_skip.x_step(nz - 1, 0)
    g_skip.y_step(nz - 2)
    g_skip.y_step(nz - 1)
    for reach in range(nz):
        g_skip.x_step(reach, 1)
        for gather in skips[1:] + [g_small]:
            gather.y_step(reach)
    g_up.own()

    if not sizes.pair:
        for load in loads:
            load.wait()
    vecs = v["vecs"]
    for row in range(6):
        vecs[row : row + 1] = jnp.concatenate(
            [small[s // 2, s % 2, row : row + 1, 0 : sizes.shard] for s in range(n_dp)], axis=1
        )
    v["bup"][...] = jnp.concatenate(
        [small[s // 2, s % 2, 6:7, 0 : sizes.part] for s in range(n_dp)], axis=1
    )
    seg_core.wait_recv()
    segc = v["segc"]
    for core in range(2):

        def turn(block, core=core):
            turned_ids = jnp.broadcast_to(segs[core, block, 0:1], (128, rows)).T
            segc[core, block] = turned_ids.astype(LOW)

        loop(groups, turn)
    g_out.start()
    g_qkv.z_step(1)
    for gather in skips:
        gather.finish()

    tile = min(256, width)

    def merge_tile(n):
        lane = aligned(n * tile, tile)
        merged[:, lane] = (
            dot(fr_v[...], ws[0 : nz // 2, :, :, lane].reshape(width, tile))
            + dot(sk_v[...], ws[nz // 2 : nz, :, :, lane].reshape(width, tile))
            + vecs[0:1, lane]
        )

    loop(width // tile, merge_tile)
    g_qkv.z_step(2)
    chunk = 64

    def norm_into(held, gain_row, target):
        def body(i):
            at = aligned(i * chunk, chunk)
            unit, _ = norm_terms(held[at])
            target[at] = (
                unit * vecs[gain_row : gain_row + 1] + vecs[gain_row + 1 : gain_row + 2]
            ).astype(LOW)

        loop(rows // chunk, body)

    def norm_back(held, gain_row, incoming, finish):
        def body(i, carry):
            at = aligned(i * chunk, chunk)
            unit, scale = norm_terms(held[at])
            t = incoming(at)
            scaled = t * vecs[gain_row : gain_row + 1]
            grad = scale * (
                scaled
                - jnp.mean(scaled, axis=-1, keepdims=True)
                - unit * jnp.mean(scaled * unit, axis=-1, keepdims=True)
            )
            finish(at, grad)
            return (
                carry[0] + jnp.sum(t * unit, axis=0, keepdims=True),
                carry[1] + jnp.sum(t, axis=0, keepdims=True),
            )

        zero = jnp.zeros((1, width), F32)
        return lax.fori_loop(0, rows // chunk, body, (zero, zero))

    normed, second, cot_all = v["normed"], v["second"], v["cot_all"]

    def share(buffer):
        swap = Exchange(place, wires)
        copies = [
            swap.copy(step, lambda: buffer.at[g], lambda: buffer.at[g])
            for step in range(1, groups)
        ]
        for copy in copies:
            copy.start()
        return copies

    norm_into(merged, 1, normed.at[g])
    normed_copies = share(normed)

    kv, qt, kt = v["kv"], v["qt"], v["kt"]
    shift = v["shift"]
    pick = (
        lax.broadcasted_iota(jnp.int32, (max(8, heads), cols), 1)
        // (width // H)
        == lax.broadcasted_iota(jnp.int32, (max(8, heads), cols), 0)
    ).astype(F32)
    kv_first = wires.take(groups)

    def kv_copy(block, step):
        return wires.copy(
            lambda: (kv.at[c, block], kv.at[c, block], place.c_peer()), kv_first + step
        )

    def mix(block, step):
        rows_in = normed[block]
        for third in range(3):
            value = dot(
                rows_in,
                wqkv[:, :, :, third * cols : (third + 1) * cols].reshape(width, cols),
            ).astype(LOW)
            if third == 0:
                query = value
            else:
                kv[c, block, :, (third - 1) * cols : third * cols] = value
        kv_copy(block, step).start()
        found = 0.0
        for at in range(0, cols, 128):
            part = query[:, at : at + 128].astype(F32)
            product = part * kv[c, block, :, at : at + 128].astype(F32)
            found = found + lax.dot_general(
                pick[:, at : at + 128],
                product,
                (((1,), (1,)), ((), ())),
                precision=lax.Precision.HIGHEST,
                preferred_element_type=F32,
            )
            qt[block, at : at + 128] = (part * 0.125).T.astype(LOW)
        for head in range(heads):
            shift[block, head] = found[head : head + 1] * 0.125

    g_up.start()
    for step in range(3, nz):
        g_qkv.z_step(step)
    g_out.own()
    g_down.own()
    for k in range(nz - 1):
        g_qkv.y_step(k)
    g_out.z_steps()
    g_qkv.y_step(nz - 1)
    g_qkv.finish()
    g_down.start()
    mix(g, 0)
    for copy in normed_copies:
        copy.wait_recv()

    def mix_other(step):
        mix(place.g_at(-step), step)

    each_group(mix_other)
    g_up.z_step(1)
    g_out.y_steps()

    kv_waits = [kv_copy(place.g_at(-step), step) for step in range(groups)]
    for copy in kv_waits:
        copy.wait_recv()

    def slope_row(head):
        index = jnp.full((1, rows), g * heads + head, jnp.int32).astype(F32)
        return jnp.exp2((index + 1.0) * (-8.0 / H))

    def fill_far(block):
        place_k = lax.broadcasted_iota(jnp.int32, (rows, rows), 0) * n_blk
        place_q = lax.broadcasted_iota(jnp.int32, (rows, rows), 1) * n_blk + (block * 2 + c)
        apart = place_k - place_q
        seg_q = segs[c, block, 0:1]
        for core in range(2):

            def body(b, core=core):
                seg_k = segc[core, b].astype(F32)
                same = jnp.concatenate([seg_k] * (rows // 128), axis=1) == seg_q
                distance = jnp.abs(apart + (b * 2 + core)).astype(F32)
                far[core, b] = jnp.where(same, distance, FAR)

            loop(groups, body)

    def padded(half_value, half):
        zero = jnp.zeros_like(half_value)
        return jnp.concatenate([half_value, zero] if half == 0 else [zero, half_value], axis=0)

    head_width = width // H
    pair_width = 2 * head_width
    attt, tot = v["attt"], v["tot"]

    def score_terms(pair, core, b, queries_pad, slope, moved):
        keys = kv[core, b, :, aligned(pair * pair_width, pair_width)]
        return jnp.exp(dot(keys, queries_pad) - slope * far[core, b] - moved)

    def over_keys(body, first):
        def visit(index, carry):
            return body(lax.div(index, groups), lax.rem(index, groups), carry)

        return lax.fori_loop(0, 2 * groups, visit, first)

    def head_at(pair, half):
        return aligned(pair * pair_width + half * head_width, head_width)

    far, vt = v["far"], v["vt"]

    def attend(block):
        def body(pair):
            lanes = aligned(pair * pair_width, pair_width)
            fixed = []
            for half in range(2):
                head = pair * 2 + half
                fixed.append(
                    (padded(qt[block, head_at(pair, half)], half), slope_row(head), shift[block, head])
                )

            def keys_in(core, b, carry):
                done = []
                for half in range(2):
                    total, summed = carry[half]
                    terms = score_terms(pair, core, b, *fixed[half])
                    total = total + jnp.sum(terms, axis=0, keepdims=True)
                    done.append((total, summed + dot(vt[core, b, lanes], terms.astype(LOW))))
                return tuple(done)

            start = (jnp.zeros((1, rows), F32), jnp.zeros((pair_width, rows), F32))
            found = over_keys(keys_in, (start, start))
            for half in range(2):
                total, summed = found[half]
                tot[block, pair * 2 + half] = total
                own = summed[half * head_width : (half + 1) * head_width]
                attt[block, head_at(pair, half)] = own / total

        loop(heads // 2, body)

    att_own, att_send = v["att_own"], v["att_send"]
    att_first = wires.take(groups)

    def att_copy(step, block):
        return wires.copy(
            lambda: (att_send.at[block], att_own.at[:, own_cols], place.x_peer(step)),
            att_first + step,
        )

    def attention():
        for core in range(2):

            def turn(b, core=core):
                vt[core, b] = kv[core, b, :, cols : 2 * cols].T
                kt[core, b] = kv[core, b, :, 0:cols].T

            loop(groups, turn)

        def other(step, carry):
            block = place.g_at(step)
            fill_far(block)
            attend(block)
            att_send[block] = attt[block].T.astype(LOW)
            att_copy(step, block).start()
            return carry

        lax.fori_loop(1, groups, other, 0)
        g_up.z_step(2)
        g_out.x_steps()
        fill_far(g)
        attend(g)
        send_joined(1)
        att_own[:, own_cols] = attt[g].T.astype(LOW)

    attention()
    g_out.finish()
    for step in range(1, groups):
        att_copy(step, place.g_at(step)).wait_recv()

    def middle_tile(n):
        lane = aligned(n * tile, tile)
        middle[:, lane] = merged[:, lane] + dot(
            att_own[...], wout[:, :, :, lane].reshape(width, tile)
        )

    loop(width // tile, middle_tile)
    norm_into(middle, 3, second.at[g])
    second_copies = share(second)
    cot_copies = share(cot_all)
    for step in range(3, nz):
        g_up.z_step(step)
    g_up.y_steps()
    g_down.z_step(1)
    g_up.finish()

    active, ghid = v["active"], v["ghid"]
    unit_tile = 256
    shard_rows = wdown.shape[2]

    def feed(block):
        def body(u):
            lane = aligned(u * unit_tile, unit_tile)
            pre = dot(second[block], wup[:, :, :, lane].reshape(width, unit_tile)) + v["bup"][:, lane]
            normal = 0.5 * (1.0 + lax.erf(pre * (0.5**0.5)))
            active[block, :, lane] = (pre * normal).astype(LOW)
            slope = normal + pre * (jnp.exp(-0.5 * pre * pre) * (1.0 / math.sqrt(2.0 * math.pi)))
            ghid[block, :, lane] = slope.astype(LOW)

        loop(units // unit_tile, body)

    def feed_back(lane, weight):
        def body(block):
            back = dot_nt(cot_all[block], weight)
            ghid[block, :, lane] = (back * ghid[block, :, lane].astype(F32)).astype(LOW)

        for block in range(groups) if groups == 2 else ():
            body(block)
        if groups > 2:
            loop(groups, body)

    def row_chunks(ref, most=512):
        per = min(nz, max(1, most // (2 * ref.shape[2])))
        return nz // per, per, per * 2 * ref.shape[2]

    def back_product(left, weight, store):
        count, per, size = row_chunks(weight)

        def body(j):
            value = dot_nt(left[...], weight[pl.ds(j * per, per)].reshape(size, weight.shape[3]))
            store(aligned(j * size, size), value)

        loop(count, body)

    lend = groups > 2
    p_send, p_recv = v["io"] if lend else v["p_send"], v["p_recv"]

    def store_into(ref, kind):
        def store(lane, value):
            ref[:, lane] = value.astype(kind)

        return store

    turned = v["turned"]

    def weight_grad(lefts, right, grad, left_at=0):
        count, per, size = row_chunks(grad, turned.shape[0])
        step_cols = min(256, grad.shape[3])
        depth = len(lefts) * rows
        count = count * lefts[0].shape[1] // (n_dp * grad.shape[2])

        def body(j):
            lane = aligned(j * size, size)
            for b, left in enumerate(lefts):
                turned[0:size, b * rows : (b + 1) * rows] = left[:, lane].T

            def inner(n):
                out = aligned(n * step_cols, step_cols)
                part = right[:, out] if len(right.shape) == 2 else right[:, :, out]
                value = dot(turned[0:size, 0:depth], part.reshape(depth, step_cols))
                grad[pl.ds(left_at + j * per, per), :, :, out] = value.astype(LOW).reshape(
                    per, 2, size // per // 2, step_cols
                )

            loop(grad.shape[3] // step_cols, inner)

        loop(count, body)

    def blocks(ref):
        return [ref.at[b] for b in range(groups)]

    feed(g)
    g_down.z_step(2)
    second_first = wires.take(groups)

    def part_copy(step, first):
        return wires.copy(
            lambda: (p_send.at[part_slot(step)], p_recv.at[step - 1], place.x_peer(step)),
            first + step,
        )

    def part_slot(step):
        return 0 if groups == 2 else lax.rem(step, 2)

    def send_part(step, left, weight, first):
        if groups > 3:

            @pl.when(step > 2)
            def _():
                part_copy(step - 2, first).wait_send()

        back_product(left, weight, store_into(p_send.at[part_slot(step)], LOW))
        part_copy(step, first).start()

    def parts_sent(first):
        for step in range(max(1, groups - 2), groups):
            part_copy(step, first).wait_send()

    for copy in second_copies:
        copy.wait_recv()
    each_group(lambda step: feed(place.g_at(step)))
    send_joined(len(joined_parts))
    early = shard_rows == unit_tile
    grad_down = v["grad_down"] if early else wdown
    r_down = Reduce(
        place, wires, grad_down, h_down, False, v["c_down"], None, v["y_down"], v["z_down"],
        v["p_down"],
    )
    if early:

        def feed_shard(z_index, y_index):
            lane = aligned((z_index * 2 + y_index) * unit_tile, unit_tile)
            feed_back(lane, wdown[z_index, y_index])

        for step in range(3, nz):
            g_down.z_step(step)
        for copy in cot_copies:
            copy.wait_recv()
        weight_grad(blocks(active), cot_all, grad_down)
        r_down.core_send(0)
        r_down.core_send(1)
        for reach in range(nz - 1):
            g_down.y_step(reach)
        for reach in range(nz):
            g_down.c_wait(reach, 0)
        loop(nz, lambda z_index: feed_shard(z_index, y))
        g_down.y_step(nz - 1)
        r_down.core_add(0)
        r_down.core_add(1)
        for reach in range(nz):
            g_down.c_wait(reach, 1)
        loop(nz, lambda z_index: feed_shard(z_index, 1 - y))
    else:
        for step in range(3, nz):
            g_down.z_step(step)
        for copy in cot_copies:
            copy.wait_recv()
        g_down.y_steps()
        g_down.finish()
        per = unit_tile // (2 * shard_rows)

        def feed_tile(u):
            weight = wdown[pl.ds(u * per, per)].reshape(unit_tile, width)
            feed_back(aligned(u * unit_tile, unit_tile), weight)

        loop(units // unit_tile, feed_tile)

    each_group(lambda step: send_part(step, ghid.at[place.g_at(step)], wup, second_first))
    back_product(ghid.at[g], wup, store_into(gmid, F32))

    def down_tile(left, target, n):
        lane = aligned(n * tile, tile)
        target(lane, dot(left[...], wdown[:, :, :, lane].reshape(units, tile)))

    g_up.drain()
    g_down.drain()
    weight_grad(blocks(second), ghid, wup)
    r_up = Reduce(
        place, wires, wup, h_up, False, v["c_up"], None, v["y_up"], v["z_up"], v["p_up"]
    )
    r_up.core_send(0)
    r_up.core_send(1)

    for copy in second_copies:
        copy.wait_send()

    def other_down(step):
        block = place.g_at(step)

        def keep(lane, value):
            second[block, :, lane] = value.astype(LOW)

        loop(width // tile, lambda n: down_tile(active.at[block], keep, n))

    each_group(other_down)
    r_up.core_add(0)
    r_up.core_add(1)

    def own_down(lane, value):
        second[g, :, lane] = value.astype(LOW)

    loop(width // tile, lambda n: down_tile(active.at[g], own_down, n))
    if not early:
        weight_grad(blocks(active), cot_all, wdown)
        r_down.core_send(0)
        r_down.core_send(1)
    sums = v["sums"]
    sums[...] = jnp.zeros_like(sums)

    def column_sums(read, count, wide):
        def body(i, total):
            return total + jnp.sum(read(i).astype(F32), axis=0, keepdims=True)

        return lax.fori_loop(0, count, body, jnp.zeros((1, wide), F32))

    per_block = rows // chunk
    ghid_sum = column_sums(
        lambda i: ghid[lax.div(i, per_block), aligned(lax.rem(i, per_block) * chunk, chunk)],
        groups * per_block,
        units,
    )
    if units >= width:
        for row in range(sizes.up_rows):
            sums[6 + row : 7 + row] = ghid_sum[:, row * width : (row + 1) * width]
    else:
        sums[6:7, 0:units] = ghid_sum
    sums[5:6] = column_sums(lambda i: cot_all[g, aligned(i * chunk, chunk)], per_block, width)
    if not early:
        r_down.core_add(0)
        r_down.core_add(1)

    for step in range(1, groups):
        part_copy(step, second_first).wait_recv()

    def second_in(at):
        t = gmid[at]
        for step in range(1, groups):
            t = t + p_recv[step - 1, at].astype(F32)
        return t

    gb = v["gb"]

    def second_out(at, grad):
        total = grad + cot_all[g, at].astype(F32)
        gmid[at] = total
        gb[at] = total.astype(LOW)

    gain_sum, bias_sum = norm_back(middle, 3, second_in, second_out)
    sums[3:4] = gain_sum
    sums[4:5] = bias_sum

    ga_in, ga_send = v["ga_in"], att_send
    for step in range(1, groups):
        att_copy(step, place.g_at(step)).wait_send()
    ga_first = wires.take(groups)

    def ga_copy(step):
        block = place.g_at(step)
        return wires.copy(
            lambda: (ga_send.at[block], ga_in.at[g], place.x_peer(step)), ga_first + step
        )

    count, per, size = row_chunks(wout)

    def branch_back(j):
        value = dot_nt(gb[...], wout[pl.ds(j * per, per)].reshape(size, width)).astype(LOW)
        for b in range(max(1, size // cols)):
            if size >= cols:
                ga_send[j * (size // cols) + b] = value[:, b * cols : (b + 1) * cols]
            else:
                ga_send[lax.div(j, cols // size), :, aligned(lax.rem(j, cols // size) * size, size)] = value

    loop(count, branch_back)
    for step in range(1, groups):
        ga_copy(step).start()
    ga_in[g] = ga_send[g]
    out_swap = Exchange(place, wires)
    out_copies = [
        out_swap.copy(
            step, lambda step=step: second.at[place.g_at(step)], lambda: cot_all.at[g]
        )
        for step in range(1, groups)
    ]
    g_out.drain()
    weight_grad([att_own], gb, wout)
    r_out = Reduce(
        place, wires, wout, h_out, True, v["c_out"], v["x_out"], v["y_out"], v["z_out"], v["p_out"]
    )
    r_out.core_send(0)
    r_out.core_send(1)

    gm = v["gm"]

    def dkv_lanes(core, start, size):
        return aligned(core * 2 * cols + start, size)

    gat, gqt, skt = vt.at[0, 0], vt.at[0, 1], vt.at[1, 0]

    def back_attend(block, first, between):
        gat[...] = ga_in[block].T

        def body(pair):
            lanes = aligned(pair * pair_width, pair_width)
            later = aligned(cols + pair * pair_width, pair_width)
            starts = pair * pair_width, cols + pair * pair_width
            fixed, scores = [], []
            for half in range(2):
                head = pair * 2 + half
                at = head_at(pair, half)
                total = tot[block, head]
                grad_att = gat[at].astype(F32)
                scaled = padded(grad_att / total, half)
                grad_total = -jnp.sum(grad_att * attt[block, at], axis=0, keepdims=True) / total
                queries = qt[block, at]
                scores.append((padded(queries, half), slope_row(head), shift[block, head]))
                fixed.append(
                    (
                        scaled.astype(LOW),
                        scaled.T.astype(LOW),
                        grad_total,
                        padded(queries.astype(F32), half).T.astype(LOW),
                    )
                )

            def keys_in(core, b, carry):
                values = kv[core, b, :, later]
                key_grad, value_grad, done = 0.0, 0.0, []
                for half in range(2):
                    shift_sum, query_grad = carry[half]
                    scaled, scaled_nat, grad_total, queries_nat = fixed[half]
                    terms = score_terms(pair, core, b, *scores[half])
                    grad_score = terms * (dot(values, scaled) + grad_total)
                    shift_sum = shift_sum - jnp.sum(grad_score, axis=0, keepdims=True)
                    grad_low = grad_score.astype(LOW)
                    value_grad = value_grad + dot(terms.astype(LOW), scaled_nat)
                    key_grad = key_grad + dot(grad_low, queries_nat)
                    done.append((shift_sum, query_grad + dot(kt[core, b, lanes], grad_low)))
                for start, found in zip(starts, (key_grad, value_grad)):
                    at = dkv_lanes(core, start, pair_width)
                    if not first:
                        found = found + active[b, :, at].astype(F32)
                    active[b, :, at] = found.astype(LOW)
                return tuple(done)

            start = (jnp.zeros((1, rows), F32), jnp.zeros((pair_width, rows), F32))
            found = over_keys(keys_in, (start, start))
            for half in range(2):
                shift_sum, query_grad = found[half]
                at = head_at(pair, half)
                own = query_grad[half * head_width : (half + 1) * head_width]
                own_keys = kt[c, block, at].astype(F32)
                gqt[at] = (0.125 * (own + shift_sum * own_keys)).astype(LOW)
                skt[at] = (shift_sum * qt[block, at].astype(F32)).astype(LOW)

        middle_pair = heads // 4
        loop_from(0, middle_pair, body)
        between()
        loop_from(middle_pair, heads // 2, body)
        gm[block, :, 0:cols] = gqt[...].T
        at = dkv_lanes(c, 0, cols)
        active[block, :, at] = active[block, :, at] + skt[...].T

    dkv_wire = wires.take(1)

    def dkv_copy():
        return wires.copy(
            lambda: (
                active.at[:, :, dkv_lanes(1 - c, 0, 2 * cols)],
                gm.at[:, :, cols : 3 * cols],
                place.c_peer(),
            ),
            dkv_wire,
        )

    def out_steps():
        r_out.core_add(0)
        r_out.core_add(1)

    def out_x_steps():
        r_out.x_add(0)
        r_out.x_add(1)

    up_tasks, down_tasks = r_up.y_tasks(), r_down.y_tasks()
    tasks += down_tasks[0:2] + [out_steps] + down_tasks[2:]
    fill_far(g)
    work(2)
    back_attend(g, True, lambda: work(2))
    work(2)
    for step in range(1, groups):
        ga_copy(step).wait_recv()
    for copy in cot_copies:
        copy.wait_send()
    for copy in out_copies:
        copy.start()
    tasks += up_tasks[0:1] + [out_x_steps, r_down.z_add] + up_tasks[1:3]

    def other_attend(step):
        block = place.g_at(-step)
        fill_far(block)
        back_attend(block, False, (lambda: work(1)) if groups == 2 else (lambda: None))

    each_group(other_attend)
    if groups > 2:
        work()
    r_down.y_sent()
    dkv_copy().start()
    work()
    dkv_copy().wait_recv()

    def merge(b):
        gm[b, :, cols : 3 * cols] = gm[b, :, cols : 3 * cols] + active[b, :, dkv_lanes(c, 0, 2 * cols)]

    loop(groups, merge)

    parts_sent(second_first)
    mix_first = wires.take(groups)

    each_group(lambda step: send_part(step, gm.at[place.g_at(step)], wqkv, mix_first))
    own_parts = [far.at[i // groups, i % groups] for i in range(width // rows)]

    count, per, size = row_chunks(wqkv)
    for j in range(count):
        value = dot_nt(gm[g], wqkv[j * per : (j + 1) * per].reshape(size, 3 * cols))
        for i in range(size // rows):
            own_parts[j * (size // rows) + i][...] = value[:, i * rows : (i + 1) * rows]
    g_qkv.drain()
    weight_grad(blocks(normed), gm, wqkv)
    c_qkv = v["c_up"].at[:, :, :, 0 : 3 * cols]
    r_qkv = Reduce(
        place, wires, wqkv, h_qkv, False, c_qkv, None, v["y_qkv"], v["z_qkv"], v["p_qkv"]
    )
    tasks += up_tasks[3:]
    work()
    r_up.y_sent()
    pl.semaphore_signal(v["free_sem"], inc=1, device_id=place.c_peer(), device_id_type=MESH)
    pl.semaphore_wait(v["free_sem"], 1)
    r_qkv.core_send(0)
    r_qkv.core_send(1)
    r_qkv.core_add(0)
    r_qkv.core_add(1)
    for step in range(1, groups):
        part_copy(step, mix_first).wait_recv()

    def first_in(at):
        t = jnp.concatenate([part[at] for part in own_parts], axis=1)
        for step in range(1, groups):
            t = t + p_recv[step - 1, at].astype(F32)
        return t

    def first_out(at, grad):
        gb[at] = (grad + gmid[at]).astype(LOW)

    gain_sum, bias_sum = norm_back(merged, 1, first_in, first_out)
    sums[1:2] = gain_sum
    sums[2:3] = bias_sum
    sums[0:1] = column_sums(lambda i: gb[aligned(i * chunk, chunk)], per_block, width)

    sum_in = v["sum_in"]

    def sum_swap(slot, peer):
        copy = wires.copy(lambda: (sums, sum_in.at[slot], peer))
        copy.start()
        return copy

    stores = []
    gj = normed

    def joined_back():
        count, per, size = row_chunks(ws)
        span = width // size

        def body(j):
            value = dot_nt(gb[...], ws[pl.ds(j * per, per)].reshape(size, width))
            at = aligned(lax.rem(j, span) * size, size)
            gj[lax.div(j, span), :, at] = value.astype(LOW)

        loop(count, body)
        for half, name in enumerate(("o_frames", "o_skip")):
            stores.append(pltpu.make_async_copy(gj.at[half], v[name].at[0], local.at[1 + half]))
            stores[-1].start()

    merged_copies = []
    if sizes.pair:
        gmx = v["gmx"]
        merged_swap = Exchange(place, wires)
        other_cols = aligned((1 - g) * cols, cols)
        merged_copies = [
            merged_swap.copy(1, lambda: gb.at[:, other_cols], lambda: gmx.at[1])
        ]
        merged_copies[0].start()
        gmx[0] = gb[:, own_cols]
    sum_core = sum_swap(0, place.c_peer())
    if lend:
        parts_sent(mix_first)
        for load in input_loads():
            load.start()
        for load in input_loads():
            load.wait()
    g_skip.drain()
    for copy in normed_copies:
        copy.wait_send()
    joined_back()
    for copy in out_copies:
        copy.wait_recv()
    ob = second.at[g]

    def out_rows(i):
        at = aligned(i * chunk, chunk)
        value = middle[at] + second[g, at].astype(F32) + vecs[5:6]
        for step in range(1, groups):
            value = value + cot_all[place.g_at(-step), at].astype(F32)
        ob[at] = value.astype(LOW)

    loop(rows // chunk, out_rows)
    stores.append(pltpu.make_async_copy(ob, v["o_out"].at[0], local.at[0]))
    stores[-1].start()
    r_down.core_sent()
    tasks += r_out.y_tasks()
    sum_core.wait()
    sums[...] = sums[...] + sum_in[0]
    sum_x = [sum_swap(step, place.x_peer(step)) for step in range(1, groups)]
    work()
    qkv_tasks = r_qkv.y_tasks()
    if sizes.pair:
        for copy in joined_copies + merged_copies:
            copy.wait()
        grad_skip, c_skip = wdown.at[:, :, :, 0:cols], v["c_down"].at[:, :, :, 0:cols]
        for half in range(2):
            lefts = [v["io"].at[half], v["joined"].at[half]]
            weight_grad(lefts, gmx, grad_skip, half * (nz // 2))
    else:
        grad_skip, c_skip = ws, v["c_skip"]
        weight_grad([fr_v], gb, grad_skip)
        weight_grad([sk_v], gb, grad_skip, nz // 2)
    r_skip = Reduce(
        place, wires, grad_skip, h_skip, not sizes.pair, c_skip, v["x_skip"], v["y_skip"],
        v["z_skip"], v["p_skip"],
    )
    r_skip.core_send(0)
    r_skip.core_send(1)
    for copy in sum_x:
        copy.wait()
    for step in range(1, groups):
        sums[0:6] = sums[0:6] + sum_in[step, 0:6]
    sum_y = sum_swap(groups, place.y_peer())
    r_skip.core_add(0)
    r_skip.core_add(1)
    if not sizes.pair:
        r_skip.x_add(0)
        r_skip.x_add(1)
    tasks += [r_down.spread_on, r_up.z_add, r_out.z_add]
    tasks += qkv_tasks + [r_up.spread_on]
    work()
    sum_y.wait()
    sums[...] = sums[...] + sum_in[groups]
    sum_z = [sum_swap(groups + step, place.z_peer(step)) for step in range(1, nz)]
    skip_tasks = r_skip.y_tasks()
    tasks += [skip_tasks[0], r_out.spread_on] + skip_tasks[1:] + [r_qkv.z_add]
    work()
    for copy in sum_z:
        copy.wait()
    for step in range(1, nz):
        sums[...] = sums[...] + sum_in[groups + step]
    o_up = v["o_up"]
    o_up[g] = sums[...]
    v["o_small"][...] = sums[...]
    up_swap = Exchange(place, wires)
    up_copies = [up_swap.copy(step, lambda: o_up.at[g], lambda: o_up.at[g]) for step in range(1, groups)]
    for copy in up_copies:
        copy.start()
    r_skip.z_add()
    r_qkv.spread_on()
    r_skip.spread_on()

    for copy in up_copies:
        copy.wait()
    for reduced in (r_up, r_down, r_out, r_qkv, r_skip):
        reduced.finish()
        reduced.drain()
    for gathered in [g_small] + skips[1:]:
        gathered.drain()
    for copy in seg_copies + [seg_core] + kv_waits:
        copy.wait_send()
    for copy in out_copies:
        copy.wait_send()
    for step in range(1, groups):
        ga_copy(step).wait_send()
    if not lend:
        parts_sent(mix_first)
    dkv_copy().wait_send()
    for store in stores:
        store.wait()


def finish(sizes, *refs):
    wholes, pieces, small, up = refs[0:3], refs[3:8], refs[8], refs[9]
    whole_outs, outs, vectors, up_out = refs[10:13], refs[13:18], refs[18:24], refs[24]
    held, made, passed, sems = refs[25:30], refs[30:35], refs[35], refs[36]
    groups, cols, width = sizes.groups, sizes.cols, sizes.width
    copies = [
        pltpu.make_async_copy(pieces[i], held[i], sems.at[i]) for i in range(5)
    ]
    moves = [
        pltpu.make_async_copy(wholes[i].at[0], passed.at[i], sems.at[5 + i]) for i in range(3)
    ]
    for copy in moves + copies:
        copy.start()
    stores = []
    for i in range(3):
        moves[i].wait()
        stores.append(pltpu.make_async_copy(passed.at[i], whole_outs[i].at[0], sems.at[13 + i]))
        stores[-1].start()
    for i in range(5):
        copies[i].wait()
        half = held[i].shape[2]
        for group in range(groups):
            for core in range(2):
                rows = slice(core * half, (core + 1) * half)
                if i == 4:
                    top = (group * 2 + core) * half
                    made[i][top : top + half] = held[i][group, core].astype(F32)
                elif i == 3 and sizes.direct:
                    for s in range(sizes.n_dp):
                        at = (s * groups + group) * sizes.part
                        made[i][rows, at : at + sizes.part] = held[i][
                            group, core, :, s * sizes.part : (s + 1) * sizes.part
                        ].astype(F32)
                elif i == 3:
                    made[i][rows, group * sizes.units : (group + 1) * sizes.units] = held[i][
                        group, core
                    ].astype(F32)
                else:
                    for third in range(held[i].shape[3] // cols):
                        at = third * width + group * cols
                        made[i][rows, at : at + cols] = held[i][
                            group, core, :, third * cols : (third + 1) * cols
                        ].astype(F32)
        stores.append(pltpu.make_async_copy(made[i], outs[i], sems.at[8 + i]))
        stores[-1].start()
    dp = lax.axis_index("dp")
    if sizes.shard % 128 == 0 and sizes.direct:
        own = aligned(dp * sizes.shard, sizes.shard)
        for row in range(6):
            vectors[row][...] = small[row : row + 1, own]
        per_row = width // sizes.part
        at = aligned(lax.rem(dp, per_row) * sizes.part, sizes.part)
        for group in range(groups):
            up_out[:, group * sizes.part : (group + 1) * sizes.part] = up[
                group, pl.ds(6 + lax.div(dp, per_row), 1), at
            ]
    else:
        for row in range(6):
            vectors[row][...] = small[row : row + 1]
        for group in range(groups):
            up_out[:, group * sizes.units : (group + 1) * sizes.units] = up[
                group, 6:7, 0 : sizes.units
            ]
    for copy in stores:
        copy.wait()


def per_device(sizes, *args):
    (
        frames, skip_frames, cotangent, seg_ids, positions,
        w_skip, b_skip, gain_attn, bias_attn, w_qkv, w_out,
        gain_ffn, bias_ffn, w_up, b_up, w_down, b_down,
    ) = args
    del positions
    n_dp, nz, groups = sizes.n_dp, sizes.nz, sizes.groups
    rows, width, cols, units = sizes.rows, sizes.width, sizes.cols, sizes.units
    heads, part, shard = sizes.heads, sizes.part, sizes.shard
    depth = w_up.shape[0]
    if not sizes.direct:
        w_up = (
            w_up.reshape(depth, n_dp, groups, part).transpose(0, 2, 1, 3).reshape(depth, groups * units)
        )
        group = lax.axis_index("blk") // 2
        b_up = lax.dynamic_slice_in_dim(b_up, group * part, part)
    r_skip, r_down = w_skip.shape[0], w_down.shape[0] // groups
    span = -(-max(shard, part) // 128) * 128

    def low(*shape):
        return pltpu.VMEM(shape, LOW)

    def full(*shape):
        return pltpu.VMEM(shape, F32)

    sizes.pair = groups == 2 and r_skip == r_down
    scratch = [
        low(2, rows, width), low(groups, rows, width),
        low(nz, 2, r_skip, width), low(nz, 2, depth, 3 * cols), low(nz, 2, depth, width),
        low(nz, 2, depth, units), low(nz, 2, r_down, width),
        full(nz, 2, 8, span), full(8, width), full(1, units),
        full(2, groups, 8, rows), low(2, groups, rows, 128),
        full(rows, width), full(rows, width), full(rows, width),
        low(groups, rows, width), low(groups, rows, width),
        low(2, groups, rows, 2 * cols),
        low(groups, cols, rows), low(2, groups, cols, rows),
        full(groups, heads, 1, rows), full(groups, cols, rows), full(groups, heads, 1, rows),
        low(rows, width), low(groups, rows, cols),
        low(groups, rows, units), low(groups, rows, units),
        low(1, 16, 128) if groups > 2 else low(1, rows, width),
        low(groups - 1, rows, width),
        low(rows, width), low(groups, rows, cols),
        low(groups, rows, 3 * cols),
        full(2, groups, rows, rows), low(2, groups, cols, rows),
        low(1, 16, 128) if sizes.pair else low(nz, 2, r_skip // 2, width),
        low(nz, 2, depth // 2, width),
        low(nz, 2, depth // 2, units),
        low(nz, 2, r_down // 2, width),
        low(1, 16, 128) if sizes.pair else low(groups - 1, nz, 2, r_skip // 2, cols),
        low(groups - 1, nz, 2, depth // 2, cols),
        low(nz, r_skip // 2, cols), low(nz, depth // 2, 3 * cols), low(nz, depth // 2, cols),
        low(nz, depth // 2, units), low(nz, r_down // 2, width),
        low(nz - 1, r_skip // 2, cols), low(nz - 1, depth // 2, 3 * cols),
        low(nz - 1, depth // 2, cols), low(nz - 1, depth // 2, units),
        low(nz - 1, r_down // 2, width),
        low(2, rows, width) if sizes.pair else low(1, 16, 128),
        low(groups, rows, cols) if sizes.pair else low(1, 16, 128),
        low(nz, 2, r_down, width) if 2 * r_down == 512 else low(1, 16, 128),
        full(8, width), full(groups + nz, 8, width),
        low(512 if groups * rows <= 512 else 256, groups * rows),
    ]
    wires = 320 if groups * n_dp <= 16 else 1400
    scratch += [pltpu.SemaphoreType.DMA((wires,)), pltpu.SemaphoreType.DMA((wires,))]
    scratch += [pltpu.SemaphoreType.DMA((16,)), pltpu.SemaphoreType.REGULAR]
    hbm, vmem = pl.BlockSpec(memory_space=pltpu.HBM), pl.BlockSpec(memory_space=pltpu.VMEM)
    whole = jax.ShapeDtypeStruct((1, rows, width), LOW)

    def piece(*shape):
        return jax.ShapeDtypeStruct((groups, 2) + shape, LOW)

    vectors = (b_skip, gain_attn, bias_attn, gain_ffn, bias_ffn, b_down, b_up)
    found = pl.pallas_call(
        functools.partial(kernel, sizes),
        out_shape=(
            whole, whole, whole,
            piece(r_skip // 2, cols), piece(depth // 2, 3 * cols), piece(depth // 2, cols),
            piece(depth // 2, units), piece(r_down // 2, width),
            jax.ShapeDtypeStruct((8, width), F32), jax.ShapeDtypeStruct((groups, 8, width), F32),
        ),
        in_specs=[hbm] * 3 + [vmem] * 8 + [hbm] * 5,
        out_specs=[hbm] * 3 + [vmem] * 7,
        scratch_shapes=scratch,
        compiler_params=pltpu.CompilerParams(
            collective_id=0, has_side_effects=True, vmem_limit_bytes=64 * 2**20
        ),
    )(
        frames, skip_frames, cotangent, seg_ids,
        *[vector.reshape(1, -1) for vector in vectors],
        w_skip, w_qkv, w_out, w_up, w_down,
    )
    easy = shard % 128 == 0 and sizes.direct
    line = jax.ShapeDtypeStruct((1, shard if easy else width), F32)
    shapes = [w_skip.shape, w_qkv.shape, w_out.shape, w_up.shape, w_down.shape]
    done = pl.pallas_call(
        functools.partial(finish, sizes),
        out_shape=(whole,) * 3
        + tuple(jax.ShapeDtypeStruct(shape, F32) for shape in shapes)
        + (line,) * 6
        + (jax.ShapeDtypeStruct((1, groups * (part if easy else units)), F32),),
        in_specs=[hbm] * 8 + [vmem] * 2,
        out_specs=[hbm] * 8 + [vmem] * 7,
        scratch_shapes=[pltpu.VMEM(value.shape, LOW) for value in found[3:8]]
        + [pltpu.VMEM(shape, F32) for shape in shapes]
        + [low(3, rows, width), pltpu.SemaphoreType.DMA((16,))],
        compiler_params=pltpu.CompilerParams(vmem_limit_bytes=60 * 2**20),
    )(*found)
    output, grad_frames, grad_skip, g_skip, g_qkv, g_out, g_up, g_down = done[0:8]
    lines = [value.reshape(-1) for value in done[8:15]]
    if not easy:
        at = lax.axis_index("dp")
        lines[0:6] = [lax.dynamic_slice_in_dim(value, at * shard, shard) for value in lines[0:6]]
        by_group = lines[6].reshape(groups, units)
        lines[6] = lax.dynamic_slice_in_dim(by_group, at * part, part, 1).reshape(-1)
    if not sizes.direct:
        g_up = g_up.reshape(depth, groups, n_dp, part).transpose(0, 2, 1, 3).reshape(depth, -1)
    g_b_skip, g_gain_a, g_bias_a, g_gain_f, g_bias_f, g_b_down, g_b_up = lines
    return (
        output, grad_frames, grad_skip, g_skip, g_b_skip, g_gain_a, g_bias_a, g_qkv, g_out,
        g_gain_f, g_bias_f, g_up, g_b_up, g_down, g_b_down,
    )


def solution(mesh):
    rows, lone = P("dp", None), P("dp")
    frames = P("dp", "blk", None)
    in_specs = (frames,) * 3 + (P("dp", "blk"),) * 2
    in_specs += (rows, lone, lone, lone, rows, rows, lone, lone, rows, lone, rows, lone)
    out_specs = (frames,) * 3
    out_specs += (rows, lone, lone, lone, rows, rows, lone, lone, rows, lone, rows, lone)

    def body(*args):
        return per_device(Sizes(mesh.shape, args[0], args[13]), *args)

    return jax.shard_map(
        body, mesh=mesh, in_specs=in_specs, out_specs=out_specs, check_vma=False
    )
```

```python
import functools
import math

import jax
import jax.numpy as jnp
from jax import lax
from jax.experimental import pallas as pl
from jax.experimental.pallas import tpu as pltpu
from jax.sharding import PartitionSpec as P

H = 16
EPSILON = 1e-05
LOW = jnp.bfloat16
F32 = jnp.float32
MESH = pl.DeviceIdType.MESH
FAR = 1e30


def dot(left, right):
    return jnp.dot(left, right, preferred_element_type=F32)


def dot_nt(left, right):
    return lax.dot_general(left, right, (((1,), (1,)), ((), ())), preferred_element_type=F32)


def loop(count, body, unroll=1):
    def visit(index, carry):
        body(index)
        return carry

    lax.fori_loop(0, count, visit, 0, unroll=min(unroll, count))


def loop_from(first, last, body):
    def visit(index, carry):
        body(index)
        return carry

    lax.fori_loop(first, last, visit, 0)


def aligned(start, size):
    return pl.ds(pl.multiple_of(start, size), size)


class Sizes:
    def __init__(self, mesh_shape, frames, w_up):
        self.n_dp, self.n_blk = mesh_shape["dp"], mesh_shape["blk"]
        self.nz = self.n_dp // 2
        self.groups = self.n_blk // 2
        self.rows = frames.shape[1]
        self.width = frames.shape[2]
        self.hidden = w_up.shape[1]
        self.shard = self.width // self.n_dp
        self.cols = self.width // self.groups
        self.heads = H // self.groups
        self.units = self.hidden // self.groups
        self.part = self.units // self.n_dp
        self.direct = self.part % 128 == 0
        self.share = max(1, self.width // (self.groups + 2) // 128) * 128
        self.up_rows = -(-self.units // self.width)


class Wires:
    def __init__(self, place, send_sems, recv_sems):
        self.place, self.send_sems, self.recv_sems, self.used = place, send_sems, recv_sems, 0

    def take(self, count=1):
        first = self.used
        self.used += count
        assert self.used <= self.send_sems.shape[0]
        return first

    def copy(self, ends, index=None):
        return Copy(self, ends, self.take() if index is None else index)


class Copy:
    def __init__(self, wires, ends, index):
        self.wires, self.ends, self.index = wires, ends, index

    def made(self):
        source, target, peer = self.ends()
        index = self.index
        if isinstance(index, tuple):
            index = index[0] + self.wires.place.z + index[1]
        return pltpu.make_async_remote_copy(
            src_ref=source,
            dst_ref=target,
            send_sem=self.wires.send_sems.at[index],
            recv_sem=self.wires.recv_sems.at[index],
            device_id=peer,
            device_id_type=MESH,
        )

    def start(self):
        self.made().start()

    def wait_send(self):
        self.made().wait_send()

    def wait_recv(self):
        self.made().wait_recv()

    def wait(self):
        self.made().wait()


class Place:
    def __init__(self, sizes):
        self.dp, self.blk = lax.axis_index("dp"), lax.axis_index("blk")
        self.z, self.y = lax.div(self.dp, 2), lax.rem(self.dp, 2)
        self.g, self.c = lax.div(self.blk, 2), lax.rem(self.blk, 2)
        self.sizes = sizes

    def z_at(self, step):
        nz = self.sizes.nz
        return lax.rem(self.z + (step + nz), nz)

    def g_at(self, step):
        groups = self.sizes.groups
        return lax.rem(self.g + (step + groups), groups)

    def z_peer(self, step):
        return (self.z_at(step) * 2 + self.y, self.blk)

    def z_next(self, way):
        return ((self.z + way) * 2 + self.y, self.blk)

    def if_z(self, *distances):
        low, high = min(distances + (0,)), max(distances + (0,))
        if low < 0 and high > 0:
            return pl.when(jnp.logical_and(self.z >= -low, self.z < self.sizes.nz - high))
        return pl.when(self.z >= -low if low < 0 else self.z < self.sizes.nz - high)

    def y_peer(self):
        return (self.z * 2 + 1 - self.y, self.blk)

    def x_peer(self, step):
        return (self.dp, self.g_at(step) * 2 + self.c)

    def c_peer(self):
        return (self.dp, self.g * 2 + 1 - self.c)


class Gather:
    def __init__(self, place, wires, ref, half, spread=0, span=None, whole_core=False):
        self.place, self.wires, self.ref = place, wires, ref
        self.half, self.spread, self.span, self.whole_core = half, spread, span, whole_core
        self.nz = place.sizes.nz
        self.groups = place.sizes.groups if spread else 1
        self.z_wires = {way: wires.take(self.nz) for way in (1, -1)}
        self.y_wires = wires.take(self.nz)
        self.x_wires = {
            (step, far): wires.take(self.nz) for step in range(1, self.groups) for far in (0, 1)
        }
        self.c_wires = {
            (step, far): 0 if whole_core else wires.take(self.nz)
            for step in range(self.groups)
            for far in (0, 1)
        }

    def at(self, distance, far, step=0):
        place = self.place
        z_index = place.z + distance
        y_index = 1 - place.y if far else place.y
        if self.whole_core:
            return self.ref.at[z_index, y_index]
        rows = aligned(place.c * self.half, self.half)
        if self.span:
            return self.ref.at[z_index, y_index, rows, self.span[0] : self.span[1]]
        if not self.spread:
            return self.ref.at[z_index, y_index, rows]
        cols = aligned(place.g_at(-step) * self.spread, self.spread)
        return self.ref.at[z_index, y_index, rows, cols]

    def copy(self, first, peer, distance, far, step=0):
        def ends():
            piece = self.at(distance, far, step)
            return piece, piece, peer()

        return self.wires.copy(ends, (first, distance))

    def z_copy(self, way, distance):
        return self.copy(self.z_wires[way], lambda: self.place.z_next(way), distance, 0)

    def y_copy(self, distance):
        return self.copy(self.y_wires, self.place.y_peer, distance, 0)

    def y_arrival(self, distance):
        return self.copy(self.y_wires, self.place.y_peer, distance, 1)

    def x_copy(self, step, distance, far):
        first = self.x_wires[step, far]
        return self.copy(first, lambda: self.place.x_peer(step), distance, far)

    def c_copy(self, step, distance, far):
        return self.copy(self.c_wires[step, far], self.place.c_peer, distance, far, step)

    def each(self, reach, body):
        if reach == 0:
            body(0)
            return
        for distance in (-reach, reach):
            self.place.if_z(distance)(functools.partial(body, distance))

    def start(self):
        for way in (1, -1):
            self.place.if_z(way)(lambda way=way: self.z_copy(way, 0).start())

    def own(self):
        self.forward(0, 0)

    def forward(self, distance, far):
        if not far:
            self.y_copy(distance).start()
        for step in range(1, self.groups):
            self.x_copy(step, distance, far).start()
        if not self.whole_core:
            self.c_copy(0, distance, far).start()

    def z_step(self, reach):
        def body(distance):
            way = 1 if distance < 0 else -1
            self.z_copy(way, distance).wait_recv()
            self.place.if_z(way)(lambda: self.z_copy(way, distance).start())
            self.forward(distance, 0)

        self.each(reach, body)

    def y_step(self, reach):
        def body(distance):
            self.y_arrival(distance).wait_recv()
            self.forward(distance, 1)

        self.each(reach, body)

    def x_step(self, reach, far):
        def body(distance):
            for step in range(1, self.groups):
                self.x_copy(step, distance, far).wait_recv()
                self.c_copy(step, distance, far).start()

        self.each(reach, body)

    def z_steps(self):
        for reach in range(1, self.nz):
            self.z_step(reach)

    def y_steps(self):
        for reach in range(self.nz):
            self.y_step(reach)

    def x_steps(self):
        for far in (0, 1):
            for reach in range(self.nz):
                self.x_step(reach, far)

    def c_wait(self, reach, far):
        def body(distance):
            for step in range(self.groups):
                self.c_copy(step, distance, far).wait_recv()

        self.each(reach, body)

    def finish(self):
        for far in (0, 1):
            for reach in range(self.nz):
                self.c_wait(reach, far)

    def drain(self):
        def body(distance):
            for way in (1, -1) if distance == 0 else (1,) if distance < 0 else (-1,):
                self.place.if_z(way)(lambda way=way: self.z_copy(way, distance).wait_send())
            self.y_copy(distance).wait_send()
            for first in self.x_wires:
                self.x_copy(first[0], distance, first[1]).wait_send()
            if not self.whole_core:
                for first in self.c_wires:
                    self.c_copy(first[0], distance, first[1]).wait_send()

        for reach in range(self.nz):
            self.each(reach, body)


class Exchange:
    def __init__(self, place, wires):
        self.place, self.groups = place, place.sizes.groups
        self.wires = wires
        self.first = wires.take(self.groups)

    def copy(self, step, source, target):
        return self.wires.copy(
            lambda: (source(), target(), self.place.x_peer(step)), self.first + step
        )


class Reduce:
    def __init__(self, place, wires, grad, half, spread, core_in, x_in, y_in, z_in, out):
        self.place, self.wires, self.grad, self.half, self.spread = place, wires, grad, half, spread
        self.core_in, self.x_in, self.y_in, self.z_in, self.out = core_in, x_in, y_in, z_in, out
        self.nz, self.groups = place.sizes.nz, place.sizes.groups
        self.core_copies, self.x_copies, self.y_copies, self.z_copies = {}, {}, {}, {}
        self.fin_copies, self.fwd_copies = {}, {}

    def side(self, part):
        return 1 - self.place.y if part == 0 else self.place.y

    def core_send(self, part):
        def ends():
            side = self.side(part)
            rows = aligned((1 - self.place.c) * self.half, self.half)
            return self.grad.at[:, side, rows], self.core_in.at[:, side], self.place.c_peer()

        copy = self.wires.copy(ends)
        copy.start()
        self.core_copies[part] = copy

    def core_add(self, part):
        side = self.side(part)
        rows = aligned(self.place.c * self.half, self.half)
        self.core_copies[part].wait_recv()

        def body(z):
            self.core_in[z, side] = self.core_in[z, side] + self.grad[z, side, rows]

        loop(self.nz, body)
        if self.spread:
            cols = self.place.sizes.cols
            for step in range(1, self.groups):
                def ends(step=step):
                    side = self.side(part)
                    theirs = aligned(self.place.g_at(step) * cols, cols)
                    return (
                        self.core_in.at[:, side, :, theirs],
                        self.x_in.at[step - 1, :, side],
                        self.place.x_peer(step),
                    )

                copy = self.wires.copy(ends)
                copy.start()
                self.x_copies[part, step] = copy
        elif part == 0:
            self.y_send()

    def x_add(self, part):
        side = self.side(part)
        cols = self.place.sizes.cols
        mine = aligned(self.place.g * cols, cols)
        for step in range(1, self.groups):
            self.x_copies[part, step].wait_recv()

        def body(z):
            total = self.core_in[z, side, :, mine].astype(F32)
            for step in range(1, self.groups):
                total = total + self.x_in[step - 1, z, side].astype(F32)
            self.x_in[0, z, side] = total.astype(LOW)

        loop(self.nz, body)
        if part == 0:
            self.y_send()

    def held(self):
        return self.x_in.at[0] if self.spread else self.core_in

    def y_send(self):
        for step in [*range(1, self.nz), 0]:

            def ends(step=step):
                z_index = self.place.z_at(step)
                source = self.held().at[z_index, self.side(0)]
                return source, self.y_in.at[z_index], self.place.y_peer()

            self.y_copies[step] = self.wires.copy(ends)
            self.y_copies[step].start()

    def y_add(self, step):
        self.y_copies[step].wait_recv()
        z_index, side, held = self.place.z_at(step), self.side(1), self.held()
        self.y_in[z_index] = self.y_in[z_index] + held[z_index, side]
        if step:
            copy = self.wires.copy(
                lambda: (
                    self.y_in.at[self.place.z_at(step)],
                    self.z_in.at[step - 1],
                    self.place.z_peer(step),
                )
            )
            copy.start()
            self.z_copies[step] = copy

    def y_tasks(self):
        steps = [*range(1, self.nz), 0]
        return [functools.partial(self.y_add, step) for step in steps]

    def y_sent(self):
        for copy in self.y_copies.values():
            copy.wait_send()
        self.y_copies.clear()

    def z_add(self):
        place = self.place
        for step in range(1, self.nz):
            self.z_copies[step].wait_recv()

        def body(i):
            at = aligned(i * 16, 16)
            total = self.y_in[place.z, at].astype(F32)
            for step in range(1, self.nz):
                total = total + self.z_in[step - 1, at].astype(F32)
            self.out[place.g, place.c, at] = total.astype(LOW)

        loop(self.half // 16, body)
        for step in range(1, self.groups):
            self.fin_copies[step] = self.wires.copy(
                lambda step=step: self.spot(0) * 2 + (place.x_peer(step),)
            )
            self.fin_copies[step].start()
        self.forward(0)

    def spread_on(self):
        for step in range(1, self.groups):
            self.fin_copies[step].wait_recv()
            self.forward(step)

    def spot(self, step):
        return (self.out.at[self.place.g_at(-step), self.place.c],)

    def forward(self, step):
        self.fwd_copies[step] = self.wires.copy(
            lambda: self.spot(step) * 2 + (self.place.c_peer(),)
        )
        self.fwd_copies[step].start()

    def core_sent(self):
        for copy in self.core_copies.values():
            copy.wait_send()
        self.core_copies.clear()

    def drain(self):
        self.core_sent()
        self.y_sent()
        for copies in (self.x_copies, self.z_copies, self.fin_copies):
            for copy in copies.values():
                copy.wait_send()

    def finish(self):
        for copy in self.fwd_copies.values():
            copy.wait()


def norm_terms(held):
    centred = held - jnp.mean(held, axis=-1, keepdims=True)
    scale = lax.rsqrt(jnp.mean(centred * centred, axis=-1, keepdims=True) + EPSILON)
    return centred * scale, scale


ORDER = (
    "skip_own", "small_start", "small_own", "out_own", "qkv_own", "skip_start", "rest_start",
    "small_z1", "seg_start", "cot_share", "qkv_start", "rest_own", "qkv_y0", "skip_z1", "skip_y0",
    "rest_z1", "seg_pass", "out_start", "skip_z2", "skip_x0", "rest_z2", "skip_y1", "small_z2",
    "skip_z3", "qkv_z1", "rest_y0", "skip_y2", "skip_x1", "skip_x2", "small_z3", "rest_z3",
    "skip_y3", "skip_w0", "qkv_z2", "out_y0", "rest_y1", "out_z1", "skip_w1", "skip_w2",
    "joined_0", "joined_1", "rest_a", "skip_x3", "small_y0", "out_x0", "small_y1", "rest_y2",
    "small_y2", "qkv_z3", "rest_y3", "skip_w3", "skip_a", "out_z2", "rest_b", "small_y3", "qkv_a",
    "up_start", "vectors", "skip_b", "out_x1", "merge", "norm_first", "up_z1", "out_y1", "out_x2",
    "qkv_y1", "qkv_y2", "qkv_y3", "qkv_b", "seg_turn", "up_own", "down_start", "out_w0", "out_z3",
    "mix_own", "up_z2", "down_own", "mix_others", "turn_keys", "out_y2", "att_other_a", "out_y3",
    "out_w1", "att_other_b", "att_own_a", "out_w2", "out_w3", "att_own_b", "up_z3", "down_z1",
    "out_b", "out_x3", "joined_2", "out_a", "mid", "up_y0", "up_y1", "down_z2", "up_y2", "down_y0",
    "down_z3", "joined_3", "joined_4", "joined_5", "up_a", "down_a", "up_y3", "joined_6",
    "joined_7", "up_b", "feed_own", "feed_others", "grad_d", "down_y1", "rd_c0", "feed_a",
    "down_y2", "down_y3", "rd_c1", "down_b", "feed_b", "part_send", "rd_y1", "part_own", "grad_u",
    "rd_y2", "out_parts", "rd_y3", "ru_c0", "norm_second", "branch", "grad_o", "back_own_a",
    "ro_c0", "ru_c1", "back_own_b", "ru_y1", "ga_wait", "back_other_a", "ro_c1", "back_other_b",
    "rd_y0", "ru_y2", "ro_x0", "sums_early", "merge_keys", "mix_send", "mix_back", "rd_z", "ro_x1",
    "ru_y3", "grad_q", "ru_y0", "up_free", "qkv_send", "ro_y1", "rq_c0", "ro_y2", "ro_y3", "rq_c1",
    "norm_merged", "merged_send", "ru_z", "rq_y1", "rq_y2", "sum_0", "sum_1", "grad_s", "rs_c0",
    "ro_y0", "ro_z", "out_send", "rs_c1", "rq_y3", "rs_y1", "rs_y2", "rq_y0", "rq_z", "sum_2",
    "rs_y3", "rs_y0", "ru_f", "output", "rd_f", "sum_3", "rs_z", "rq_f", "inputs_back", "sum_4",
    "ro_f", "rs_f",
)


def kernel(sizes, *refs):
    names = (
        "frames", "skip", "cot", "seg", "b_skip", "gain_a", "bias_a", "gain_f", "bias_f",
        "b_down", "b_up", "w_skip", "w_qkv", "w_out", "w_up", "w_down", "o_out", "o_frames",
        "o_skip", "p_skip", "p_qkv", "p_out", "p_up", "p_down", "o_small", "o_up", "io",
        "cot_all", "ws", "wqkv", "wout", "wup", "wdown", "small", "vecs", "bup", "segs", "segc",
        "merged", "middle", "gmid", "normed", "second", "kv", "qt", "kt", "shift", "attt", "tot",
        "att_own", "att_send", "active", "ghid", "p_send", "p_recv", "gb", "ga_in", "gm",
        "far", "vt", "c_skip", "c_out", "c_up", "c_down", "x_skip", "x_out", "y_skip", "y_qkv",
        "y_out", "y_up", "y_down", "z_skip", "z_qkv", "z_out", "z_up", "z_down", "joined", "gmx",
        "grad_down", "sums", "sum_in", "turned", "send_sems", "recv_sems", "local_sems",
        "free_sem",
    )
    assert len(names) == len(refs), (len(names), len(refs))
    v = dict(zip(names, refs))
    place = Place(sizes)
    wires = Wires(place, v["send_sems"], v["recv_sems"])
    local = v["local_sems"]
    nz, groups, n_dp, n_blk = sizes.nz, sizes.groups, sizes.n_dp, sizes.n_blk
    rows, width, cols, units = sizes.rows, sizes.width, sizes.cols, sizes.units
    heads = sizes.heads
    z, y, g, c = place.z, place.y, place.g, place.c

    def each_group(body):
        if groups == 2:
            body(1)
        else:
            loop_from(1, groups, body)

    barrier = pltpu.get_barrier_semaphore()
    partners = [place.z_peer(step) for step in range(1, nz)] + [place.y_peer()]
    partners += [place.x_peer(step) for step in range(1, groups)] + [place.c_peer()]
    for partner in partners:
        pl.semaphore_signal(barrier, inc=1, device_id=partner, device_id_type=MESH)

    fr_v, sk_v = v["io"].at[0], v["io"].at[1]

    def input_loads():
        return [
            pltpu.make_async_copy(v["frames"].at[0], fr_v, local.at[0]),
            pltpu.make_async_copy(v["skip"].at[0], sk_v, local.at[1]),
        ]

    loads = input_loads() + [
        pltpu.make_async_copy(v["cot"].at[0], v["cot_all"].at[g], local.at[2]),
    ]

    h_skip, h_qkv = v["ws"].shape[2] // 2, v["wqkv"].shape[2] // 2
    h_out, h_up, h_down = v["wout"].shape[2] // 2, v["wup"].shape[2] // 2, v["wdown"].shape[2] // 2

    stages = {}

    def fetch(name, start, size, tops, index):
        copies = [
            pltpu.make_async_copy(
                v[name].at[aligned(start, size), part * width : (part + 1) * width],
                buffer.at[top : top + size],
                local.at[index + part],
            )
            for part, (buffer, top) in enumerate(tops)
        ]
        for copy in copies:
            copy.start()
        stages[name] = copies

    merged, middle, gmid = v["merged"], v["middle"], v["gmid"]
    up_tops = [
        (middle, h_down), (middle, h_down + h_up), (merged, h_skip + h_out), (gmid, 3 * h_qkv)
    ]
    fetch("w_skip", c * h_skip, h_skip, [(merged, 0)], 3)
    fetch("w_qkv", c * h_qkv, h_qkv, [(gmid, third * h_qkv) for third in range(3)], 4)
    fetch("w_out", c * h_out, h_out, [(merged, h_skip)], 7)
    fetch("w_up", c * h_up, h_up, up_tops, 8)
    fetch("w_down", (g * 2 + c) * h_down, h_down, [(middle, 0)], 12)
    for load in loads:
        load.start()
    ws, wqkv, wout, wup, wdown = v["ws"], v["wqkv"], v["wout"], v["wup"], v["wdown"]
    own_cols = aligned(g * cols, cols)

    def arrived(name):
        for copy in stages[name]:
            copy.wait()

    arrived("w_skip")
    share, shared = sizes.share, groups * sizes.share
    own_share, skip_rows = aligned(g * share, share), aligned(c * h_skip, h_skip)
    ws[z, y, skip_rows, own_share] = merged[0:h_skip, own_share].astype(LOW)
    if shared < width:
        ws[z, y, skip_rows, shared:width] = merged[0:h_skip, shared:width].astype(LOW)
    arrived("w_qkv")
    for third in range(3):
        wqkv[z, y, aligned(c * h_qkv, h_qkv), third * cols : (third + 1) * cols] = gmid[
            third * h_qkv : (third + 1) * h_qkv, own_cols
        ].astype(LOW)
    arrived("w_out")
    wout[z, y, aligned(c * h_out, h_out), own_cols] = merged[
        h_skip : h_skip + h_out, own_cols
    ].astype(LOW)
    arrived("w_up")
    up_rows = aligned(c * h_up, h_up)
    if sizes.direct:
        part = sizes.part
        per_row = width // (part * groups)
        for s in range(n_dp):
            buffer, top = up_tops[s // per_row]
            lane = aligned(g * part + s % per_row * part * groups, part)
            wup[z, y, up_rows, s * part : (s + 1) * part] = buffer[top : top + h_up, lane].astype(LOW)
    else:
        for index, (buffer, top) in enumerate(up_tops):

            @pl.when(lax.div(g * units, width) == index)
            def _(buffer=buffer, top=top):
                lane = aligned(lax.rem(g * units, width), units)
                wup[z, y, up_rows] = buffer[top : top + h_up, lane].astype(LOW)

    arrived("w_down")
    wdown[z, y, aligned(c * h_down, h_down)] = middle[0:h_down].astype(LOW)

    small = v["small"]
    for row, name in enumerate(("b_skip", "gain_a", "bias_a", "gain_f", "bias_f", "b_down")):
        small[z, y, row : row + 1, 0 : sizes.shard] = v[name][...].astype(LOW).astype(F32)
    if sizes.direct:
        own_up = v["b_up"][:, aligned(g * sizes.part, sizes.part)]
    else:
        own_up = v["b_up"][...]
    small[z, y, 6:7, 0 : sizes.part] = own_up.astype(LOW).astype(F32)
    segs = v["segs"]
    segs[c, g] = jnp.broadcast_to(v["seg"][...].astype(F32), (8, rows))

    pl.semaphore_wait(barrier, len(partners))

    for load in loads:
        load.wait()
    steps = {}

    def step(function):
        steps[function.__name__] = function
        return function

    def none():
        pass

    last_reach = 3

    def reaches(reach):
        return range(reach, nz) if reach == last_reach else (reach,)

    def gather_steps(name, gather):
        many = {
            "z": [gather.z_step, range(1, last_reach + 1)],
            "y": [gather.y_step, range(last_reach + 1)],
        }
        if gather.spread:
            many["x"] = [lambda reach: gather.x_step(reach, 0), range(last_reach + 1)]
            many["w"] = [lambda reach: gather.x_step(reach, 1), range(last_reach + 1)]
        steps[name + "_start"], steps[name + "_own"] = gather.start, gather.own

        def run(method, reach):
            for one in reaches(reach):
                method(one)

        for letter, (method, which) in many.items():
            for reach in which:
                steps[f"{name}_{letter}{reach}"] = functools.partial(run, method, reach)
        if not gather.whole_core:
            steps[name + "_a"] = lambda: [gather.c_wait(reach, 0) for reach in range(nz)]
            steps[name + "_b"] = lambda: [gather.c_wait(reach, 1) for reach in range(nz)]

    g_small = Gather(place, wires, small, 0, whole_core=True)
    g_skip = Gather(place, wires, v["ws"], h_skip, spread=share)
    g_qkv = Gather(place, wires, v["wqkv"], h_qkv)
    g_out = Gather(place, wires, v["wout"], h_out, spread=cols)
    g_up = Gather(place, wires, v["wup"], h_up)
    g_down = Gather(place, wires, v["wdown"], h_down)
    gather_steps("small", g_small)
    gather_steps("skip", g_skip)
    gather_steps("qkv", g_qkv)
    gather_steps("out", g_out)
    gather_steps("up", g_up)
    gather_steps("down", g_down)
    gathers = [g_small, g_skip, g_qkv, g_out, g_up, g_down]
    if shared < width:
        g_rest = Gather(place, wires, v["ws"], h_skip, span=(shared, width))
        gather_steps("rest", g_rest)
        gathers.append(g_rest)
    else:
        for name in ("start", "own", "z1", "z2", "z3", "y0", "y1", "y2", "y3", "a", "b"):
            steps["rest_" + name] = none

    seg_swap = Exchange(place, wires)
    seg_copies = [
        seg_swap.copy(step, lambda: segs.at[c, g], lambda: segs.at[c, g])
        for step in range(1, groups)
    ]
    seg_core = wires.copy(lambda: (segs.at[c], segs.at[c], place.c_peer()))

    @step
    def seg_start():
        for copy in seg_copies:
            copy.start()

    @step
    def seg_pass():
        for copy in seg_copies:
            copy.wait_recv()
        seg_core.start()

    joined_copies = []
    lines = rows // 4
    for part in range(8):
        if sizes.pair:
            at = part // 4, pl.ds(part % 4 * lines, lines)
            copy = Exchange(place, wires).copy(
                1, lambda at=at: v["io"].at[at], lambda at=at: v["joined"].at[at]
            )
            joined_copies.append(copy)
            steps[f"joined_{part}"] = copy.start
        else:
            steps[f"joined_{part}"] = none

    vecs, segc = v["vecs"], v["segc"]

    @step
    def vectors():
        for row in range(6):
            vecs[row : row + 1] = jnp.concatenate(
                [small[s // 2, s % 2, row : row + 1, 0 : sizes.shard] for s in range(n_dp)], axis=1
            )
        v["bup"][...] = jnp.concatenate(
            [small[s // 2, s % 2, 6:7, 0 : sizes.part] for s in range(n_dp)], axis=1
        )

    @step
    def seg_turn():
        seg_core.wait_recv()
        for core in range(2):

            def turn(block, core=core):
                turned_ids = jnp.broadcast_to(segs[core, block, 0:1], (128, rows)).T
                segc[core, block] = turned_ids.astype(LOW)

            loop(groups, turn)

    tile = min(256, width)
    normed, second, cot_all = v["normed"], v["second"], v["cot_all"]

    @step
    def merge():
        def merge_tile(n):
            lane = aligned(n * tile, tile)
            merged[:, lane] = (
                dot(fr_v[...], ws[0 : nz // 2, :, :, lane].reshape(width, tile))
                + dot(sk_v[...], ws[nz // 2 : nz, :, :, lane].reshape(width, tile))
                + vecs[0:1, lane]
            )

        loop(width // tile, merge_tile)

    chunk = 64

    def norm_into(held, gain_row, target):
        def body(i):
            at = aligned(i * chunk, chunk)
            unit, _ = norm_terms(held[at])
            target[at] = (
                unit * vecs[gain_row : gain_row + 1] + vecs[gain_row + 1 : gain_row + 2]
            ).astype(LOW)

        loop(rows // chunk, body)

    def norm_back(held, gain_row, incoming, finish):
        def body(i, carry):
            at = aligned(i * chunk, chunk)
            unit, scale = norm_terms(held[at])
            t = incoming(at)
            scaled = t * vecs[gain_row : gain_row + 1]
            grad = scale * (
                scaled
                - jnp.mean(scaled, axis=-1, keepdims=True)
                - unit * jnp.mean(scaled * unit, axis=-1, keepdims=True)
            )
            finish(at, grad)
            return (
                carry[0] + jnp.sum(t * unit, axis=0, keepdims=True),
                carry[1] + jnp.sum(t, axis=0, keepdims=True),
            )

        zero = jnp.zeros((1, width), F32)
        return lax.fori_loop(0, rows // chunk, body, (zero, zero))


    def sharing(buffer):
        swap = Exchange(place, wires)
        return [
            swap.copy(step, lambda: buffer.at[g], lambda: buffer.at[g])
            for step in range(1, groups)
        ]

    def start_all(copies):
        for copy in copies:
            copy.start()

    def wait_all(copies):
        for copy in copies:
            copy.wait_recv()

    def sent_all(copies):
        for copy in copies:
            copy.wait_send()

    normed_copies, second_copies, cot_copies = sharing(normed), sharing(second), sharing(cot_all)

    @step
    def norm_first():
        norm_into(merged, 1, normed.at[g])
        start_all(normed_copies)

    @step
    def cot_share():
        start_all(cot_copies)

    kv, qt, kt = v["kv"], v["qt"], v["kt"]
    shift = v["shift"]
    pick = (
        lax.broadcasted_iota(jnp.int32, (max(8, heads), cols), 1)
        // (width // H)
        == lax.broadcasted_iota(jnp.int32, (max(8, heads), cols), 0)
    ).astype(F32)
    kv_first = wires.take(groups)

    def kv_copy(block, step):
        return wires.copy(
            lambda: (kv.at[c, block], kv.at[c, block], place.c_peer()), kv_first + step
        )

    def mix(block, step):
        rows_in = normed[block]
        for third in range(3):
            value = dot(
                rows_in,
                wqkv[:, :, :, third * cols : (third + 1) * cols].reshape(width, cols),
            ).astype(LOW)
            if third == 0:
                query = value
            else:
                kv[c, block, :, (third - 1) * cols : third * cols] = value
        kv_copy(block, step).start()
        found = 0.0
        for at in range(0, cols, 128):
            part = query[:, at : at + 128].astype(F32)
            product = part * kv[c, block, :, at : at + 128].astype(F32)
            found = found + lax.dot_general(
                pick[:, at : at + 128],
                product,
                (((1,), (1,)), ((), ())),
                precision=lax.Precision.HIGHEST,
                preferred_element_type=F32,
            )
            qt[block, at : at + 128] = (part * 0.125).T.astype(LOW)
        for head in range(heads):
            shift[block, head] = found[head : head + 1] * 0.125

    @step
    def mix_own():
        mix(g, 0)

    @step
    def mix_others():
        wait_all(normed_copies)
        each_group(lambda step: mix(place.g_at(-step), step))

    kv_waits = [kv_copy(place.g_at(-step), step) for step in range(groups)]
    def slope_row(head):
        index = jnp.full((1, rows), g * heads + head, jnp.int32).astype(F32)
        return jnp.exp2((index + 1.0) * (-8.0 / H))

    def fill_far(block):
        place_k = lax.broadcasted_iota(jnp.int32, (rows, rows), 0) * n_blk
        place_q = lax.broadcasted_iota(jnp.int32, (rows, rows), 1) * n_blk + (block * 2 + c)
        apart = place_k - place_q
        seg_q = segs[c, block, 0:1]
        for core in range(2):

            def body(b, core=core):
                seg_k = segc[core, b].astype(F32)
                same = jnp.concatenate([seg_k] * (rows // 128), axis=1) == seg_q
                distance = jnp.abs(apart + (b * 2 + core)).astype(F32)
                far[core, b] = jnp.where(same, distance, FAR)

            loop(groups, body)

    def padded(half_value, half):
        zero = jnp.zeros_like(half_value)
        return jnp.concatenate([half_value, zero] if half == 0 else [zero, half_value], axis=0)

    head_width = width // H
    pair_width = 2 * head_width
    attt, tot = v["attt"], v["tot"]

    def score_terms(pair, core, b, queries_pad, slope, moved):
        keys = kv[core, b, :, aligned(pair * pair_width, pair_width)]
        return jnp.exp(dot(keys, queries_pad) - slope * far[core, b] - moved)

    def over_keys(body, first):
        def visit(index, carry):
            return body(lax.div(index, groups), lax.rem(index, groups), carry)

        if groups > 2:
            return lax.fori_loop(0, 2 * groups, visit, first)
        for index in range(2 * groups):
            first = body(index // groups, index % groups, first)
        return first

    def head_at(pair, half):
        return aligned(pair * pair_width + half * head_width, head_width)

    far, vt = v["far"], v["vt"]

    pairs = heads // 2

    def attend(block, first, last):
        def body(pair):
            lanes = aligned(pair * pair_width, pair_width)
            fixed = []
            for half in range(2):
                head = pair * 2 + half
                fixed.append(
                    (padded(qt[block, head_at(pair, half)], half), slope_row(head), shift[block, head])
                )

            def keys_in(core, b, carry):
                done = []
                for half in range(2):
                    total, summed = carry[half]
                    terms = score_terms(pair, core, b, *fixed[half])
                    total = total + jnp.sum(terms, axis=0, keepdims=True)
                    done.append((total, summed + dot(vt[core, b, lanes], terms.astype(LOW))))
                return tuple(done)

            start = (jnp.zeros((1, rows), F32), jnp.zeros((pair_width, rows), F32))
            found = over_keys(keys_in, (start, start))
            for half in range(2):
                total, summed = found[half]
                tot[block, pair * 2 + half] = total
                own = summed[half * head_width : (half + 1) * head_width]
                attt[block, head_at(pair, half)] = own / total

        loop_from(first, last, body)

    att_own, att_send = v["att_own"], v["att_send"]
    att_first = wires.take(groups)

    def att_copy(step, block):
        return wires.copy(
            lambda: (att_send.at[block], att_own.at[:, own_cols], place.x_peer(step)),
            att_first + step,
        )

    @step
    def turn_keys():
        wait_all(kv_waits)
        for core in range(2):

            def turn(b, core=core):
                vt[core, b] = kv[core, b, :, cols : 2 * cols].T
                kt[core, b] = kv[core, b, :, 0:cols].T

            loop(groups, turn)

    def attend_end(step):
        block = place.g_at(step)
        att_send[block] = attt[block].T.astype(LOW)
        att_copy(step, block).start()

    def attend_other(step):
        fill_far(place.g_at(step))
        attend(place.g_at(step), 0, pairs)
        attend_end(step)

    in_two = groups == 2

    @step
    def att_other_a():
        if in_two:
            fill_far(place.g_at(1))
            attend(place.g_at(1), 0, pairs // 2)

    @step
    def att_other_b():
        if in_two:
            attend(place.g_at(1), pairs // 2, pairs)
            attend_end(1)
        else:
            each_group(attend_other)

    @step
    def att_own_a():
        fill_far(g)
        attend(g, 0, pairs // 2)

    @step
    def att_own_b():
        attend(g, pairs // 2, pairs)
        att_own[:, own_cols] = attt[g].T.astype(LOW)

    @step
    def mid():
        wait_all([att_copy(step, place.g_at(step)) for step in range(1, groups)])

        def middle_tile(n):
            lane = aligned(n * tile, tile)
            middle[:, lane] = merged[:, lane] + dot(
                att_own[...], wout[:, :, :, lane].reshape(width, tile)
            )

        loop(width // tile, middle_tile)
        norm_into(middle, 3, second.at[g])
        start_all(second_copies)

    active, ghid = v["active"], v["ghid"]
    unit_tile = 256
    shard_rows = wdown.shape[2]

    def feed(block):
        def body(u):
            lane = aligned(u * unit_tile, unit_tile)
            pre = dot(second[block], wup[:, :, :, lane].reshape(width, unit_tile)) + v["bup"][:, lane]
            normal = 0.5 * (1.0 + lax.erf(pre * (0.5**0.5)))
            active[block, :, lane] = (pre * normal).astype(LOW)
            slope = normal + pre * (jnp.exp(-0.5 * pre * pre) * (1.0 / math.sqrt(2.0 * math.pi)))
            ghid[block, :, lane] = slope.astype(LOW)

        loop(units // unit_tile, body)

    def feed_back(lane, weight):
        def body(block):
            back = dot_nt(cot_all[block], weight)
            ghid[block, :, lane] = (back * ghid[block, :, lane].astype(F32)).astype(LOW)

        for block in range(groups) if groups == 2 else ():
            body(block)
        if groups > 2:
            loop(groups, body)

    def row_chunks(ref, most=512):
        per = min(nz, max(1, most // (2 * ref.shape[2])))
        return nz // per, per, per * 2 * ref.shape[2]

    def back_product(left, weight, store):
        count, per, size = row_chunks(weight)

        def body(j):
            value = dot_nt(left[...], weight[pl.ds(j * per, per)].reshape(size, weight.shape[3]))
            store(aligned(j * size, size), value)

        loop(count, body)

    turned = v["turned"]

    def weight_grad(lefts, right, grad, left_at=0):
        count, per, size = row_chunks(grad, turned.shape[0])
        step_cols = min(512, grad.shape[3])
        depth = len(lefts) * rows
        count = count * lefts[0].shape[1] // (n_dp * grad.shape[2])

        def body(j):
            lane = aligned(j * size, size)
            for b, left in enumerate(lefts):
                turned[0:size, b * rows : (b + 1) * rows] = left[:, lane].T

            def inner(n):
                out = aligned(n * step_cols, step_cols)
                part = right[:, out] if len(right.shape) == 2 else right[:, :, out]
                value = dot(turned[0:size, 0:depth], part.reshape(depth, step_cols))
                grad[pl.ds(left_at + j * per, per), :, :, out] = value.astype(LOW).reshape(
                    per, 2, size // per // 2, step_cols
                )

            loop(grad.shape[3] // step_cols, inner, 2)

        loop(count, body)

    def blocks(ref):
        return [ref.at[b] for b in range(groups)]

    @step
    def feed_own():
        feed(g)

    @step
    def feed_others():
        wait_all(second_copies)
        each_group(lambda step: feed(place.g_at(step)))

    early = shard_rows == unit_tile
    grad_down = v["grad_down"] if early else wdown
    r_down = Reduce(
        place, wires, grad_down, h_down, False, v["c_down"], None, v["y_down"], v["z_down"],
        v["p_down"],
    )

    def down_gradient():
        weight_grad(blocks(active), cot_all, grad_down)
        r_down.core_send(0)
        r_down.core_send(1)

    @step
    def grad_d():
        wait_all(cot_copies)
        if early:
            down_gradient()

    def feed_shard(z_index, y_index):
        lane = aligned((z_index * 2 + y_index) * unit_tile, unit_tile)
        feed_back(lane, wdown[z_index, y_index])

    @step
    def feed_a():
        if early:
            loop(nz, lambda z_index: feed_shard(z_index, y))

    @step
    def feed_b():
        if early:
            loop(nz, lambda z_index: feed_shard(z_index, 1 - y))
            return
        per = unit_tile // (2 * shard_rows)

        def feed_tile(u):
            weight = wdown[pl.ds(u * per, per)].reshape(unit_tile, width)
            feed_back(aligned(u * unit_tile, unit_tile), weight)

        loop(units // unit_tile, feed_tile)

    lend = groups > 2
    p_send, p_recv = v["io"] if lend else v["p_send"], v["p_recv"]

    def store_into(ref, kind):
        def store(lane, value):
            ref[:, lane] = value.astype(kind)

        return store

    second_first, mix_first = wires.take(groups), wires.take(groups)

    def part_copy(step, first):
        return wires.copy(
            lambda: (p_send.at[part_slot(step)], p_recv.at[step - 1], place.x_peer(step)),
            first + step,
        )

    def part_slot(step):
        return 0 if groups == 2 else lax.rem(step, 2)

    def send_part(step, left, weight, first):
        if groups > 3:

            @pl.when(step > 2)
            def _():
                part_copy(step - 2, first).wait_send()

        back_product(left, weight, store_into(p_send.at[part_slot(step)], LOW))
        part_copy(step, first).start()

    def parts_sent(first):
        for step in range(max(1, groups - 2), groups):
            part_copy(step, first).wait_send()

    @step
    def part_send():
        each_group(lambda step: send_part(step, ghid.at[place.g_at(step)], wup, second_first))

    @step
    def part_own():
        back_product(ghid.at[g], wup, store_into(gmid, F32))

    def down_tile(left, target, n):
        lane = aligned(n * tile, tile)
        target(lane, dot(left[...], wdown[:, :, :, lane].reshape(units, tile)))

    r_up = Reduce(
        place, wires, wup, h_up, False, v["c_up"], None, v["y_up"], v["z_up"], v["p_up"]
    )

    @step
    def grad_u():
        g_up.drain()
        weight_grad(blocks(second), ghid, wup)
        r_up.core_send(0)
        r_up.core_send(1)

    def other_down(step):
        block = place.g_at(step)

        def keep(lane, value):
            second[block, :, lane] = value.astype(LOW)

        loop(width // tile, lambda n: down_tile(active.at[block], keep, n))

    def own_down(lane, value):
        second[g, :, lane] = value.astype(LOW)

    @step
    def out_parts():
        sent_all(second_copies)
        each_group(other_down)
        loop(width // tile, lambda n: down_tile(active.at[g], own_down, n))
        g_down.drain()
        if not early:
            down_gradient()
            r_down.core_add(0)
            r_down.core_add(1)

    sums = v["sums"]
    sums[...] = jnp.zeros_like(sums)

    def column_sums(read, count, wide):
        def body(i, total):
            return total + jnp.sum(read(i).astype(F32), axis=0, keepdims=True)

        return lax.fori_loop(0, count, body, jnp.zeros((1, wide), F32))

    per_block = rows // chunk
    @step
    def sums_early():
        ghid_sum = column_sums(
            lambda i: ghid[lax.div(i, per_block), aligned(lax.rem(i, per_block) * chunk, chunk)],
            groups * per_block,
            units,
        )
        if units >= width:
            for row in range(sizes.up_rows):
                sums[6 + row : 7 + row] = ghid_sum[:, row * width : (row + 1) * width]
        else:
            sums[6:7, 0:units] = ghid_sum
        sums[5:6] = column_sums(lambda i: cot_all[g, aligned(i * chunk, chunk)], per_block, width)

    gb = v["gb"]

    @step
    def norm_second():
        wait_all([part_copy(step, second_first) for step in range(1, groups)])

        def second_in(at):
            t = gmid[at]
            for step in range(1, groups):
                t = t + p_recv[step - 1, at].astype(F32)
            return t

        def second_out(at, grad):
            total = grad + cot_all[g, at].astype(F32)
            gmid[at] = total
            gb[at] = total.astype(LOW)

        gain_sum, bias_sum = norm_back(middle, 3, second_in, second_out)
        sums[3:4] = gain_sum
        sums[4:5] = bias_sum

    ga_in, ga_send = v["ga_in"], att_send
    ga_first = wires.take(groups)

    def ga_copy(step):
        block = place.g_at(step)
        return wires.copy(
            lambda: (ga_send.at[block], ga_in.at[g], place.x_peer(step)), ga_first + step
        )

    @step
    def branch():
        sent_all([att_copy(step, place.g_at(step)) for step in range(1, groups)])
        count, per, size = row_chunks(wout)

        def branch_back(j):
            value = dot_nt(gb[...], wout[pl.ds(j * per, per)].reshape(size, width)).astype(LOW)
            for b in range(max(1, size // cols)):
                if size >= cols:
                    ga_send[j * (size // cols) + b] = value[:, b * cols : (b + 1) * cols]
                else:
                    lane = aligned(lax.rem(j, cols // size) * size, size)
                    ga_send[lax.div(j, cols // size), :, lane] = value

        loop(count, branch_back)
        start_all([ga_copy(step) for step in range(1, groups)])
        ga_in[g] = ga_send[g]

    out_swap = Exchange(place, wires)
    out_copies = [
        out_swap.copy(
            step, lambda step=step: second.at[place.g_at(step)], lambda: cot_all.at[g]
        )
        for step in range(1, groups)
    ]
    r_out = Reduce(
        place, wires, wout, h_out, True, v["c_out"], v["x_out"], v["y_out"], v["z_out"], v["p_out"]
    )

    @step
    def grad_o():
        g_out.drain()
        weight_grad([att_own], gb, wout)
        r_out.core_send(0)
        r_out.core_send(1)

    gm = v["gm"]

    def dkv_lanes(core, start, size):
        return aligned(core * 2 * cols + start, size)

    gat, gqt, skt = vt.at[0, 0], vt.at[0, 1], vt.at[1, 0]

    def back_start(block):
        fill_far(block)
        gat[...] = ga_in[block].T

    def back_attend(block, fresh, first, last):
        def body(pair):
            lanes = aligned(pair * pair_width, pair_width)
            later = aligned(cols + pair * pair_width, pair_width)
            starts = pair * pair_width, cols + pair * pair_width
            fixed, scores = [], []
            for half in range(2):
                head = pair * 2 + half
                at = head_at(pair, half)
                total = tot[block, head]
                grad_att = gat[at].astype(F32)
                scaled = padded(grad_att / total, half)
                grad_total = -jnp.sum(grad_att * attt[block, at], axis=0, keepdims=True) / total
                queries = qt[block, at]
                scores.append((padded(queries, half), slope_row(head), shift[block, head]))
                fixed.append(
                    (
                        scaled.astype(LOW),
                        scaled.T.astype(LOW),
                        grad_total,
                        padded(queries.astype(F32), half).T.astype(LOW),
                    )
                )

            def keys_in(core, b, carry):
                values = kv[core, b, :, later]
                key_grad, value_grad, done = 0.0, 0.0, []
                for half in range(2):
                    shift_sum, query_grad = carry[half]
                    scaled, scaled_nat, grad_total, queries_nat = fixed[half]
                    terms = score_terms(pair, core, b, *scores[half])
                    grad_score = terms * (dot(values, scaled) + grad_total)
                    shift_sum = shift_sum - jnp.sum(grad_score, axis=0, keepdims=True)
                    grad_low = grad_score.astype(LOW)
                    value_grad = value_grad + dot(terms.astype(LOW), scaled_nat)
                    key_grad = key_grad + dot(grad_low, queries_nat)
                    done.append((shift_sum, query_grad + dot(kt[core, b, lanes], grad_low)))
                for start, found in zip(starts, (key_grad, value_grad)):
                    at = dkv_lanes(core, start, pair_width)
                    if not fresh:
                        found = found + active[b, :, at].astype(F32)
                    active[b, :, at] = found.astype(LOW)
                return tuple(done)

            start = (jnp.zeros((1, rows), F32), jnp.zeros((pair_width, rows), F32))
            found = over_keys(keys_in, (start, start))
            for half in range(2):
                shift_sum, query_grad = found[half]
                at = head_at(pair, half)
                own = query_grad[half * head_width : (half + 1) * head_width]
                own_keys = kt[c, block, at].astype(F32)
                gqt[at] = (0.125 * (own + shift_sum * own_keys)).astype(LOW)
                skt[at] = (shift_sum * qt[block, at].astype(F32)).astype(LOW)

        loop_from(first, last, body)

    def back_end(block):
        gm[block, :, 0:cols] = gqt[...].T
        at = dkv_lanes(c, 0, cols)
        active[block, :, at] = active[block, :, at] + skt[...].T

    dkv_wire = wires.take(1)

    def dkv_copy():
        return wires.copy(
            lambda: (
                active.at[:, :, dkv_lanes(1 - c, 0, 2 * cols)],
                gm.at[:, :, cols : 3 * cols],
                place.c_peer(),
            ),
            dkv_wire,
        )

    def back_other(step):
        block = place.g_at(-step)
        back_start(block)
        back_attend(block, False, 0, pairs)
        back_end(block)

    @step
    def back_own_a():
        back_start(g)
        back_attend(g, True, 0, pairs // 2)

    @step
    def back_own_b():
        back_attend(g, True, pairs // 2, pairs)
        back_end(g)

    @step
    def ga_wait():
        wait_all([ga_copy(step) for step in range(1, groups)])

    @step
    def out_send():
        sent_all(cot_copies)
        start_all(out_copies)

    @step
    def back_other_a():
        if in_two:
            back_start(place.g_at(-1))
            back_attend(place.g_at(-1), False, 0, pairs // 2)

    @step
    def back_other_b():
        if in_two:
            back_attend(place.g_at(-1), False, pairs // 2, pairs)
            back_end(place.g_at(-1))
        else:
            each_group(back_other)
        dkv_copy().start()

    @step
    def merge_keys():
        dkv_copy().wait_recv()

        def merge_block(b):
            at = dkv_lanes(c, 0, 2 * cols)
            gm[b, :, cols : 3 * cols] = gm[b, :, cols : 3 * cols] + active[b, :, at]

        loop(groups, merge_block)

    @step
    def mix_send():
        parts_sent(second_first)
        each_group(lambda step: send_part(step, gm.at[place.g_at(step)], wqkv, mix_first))

    own_parts = [far.at[i // groups, i % groups] for i in range(width // rows)]

    @step
    def mix_back():
        count, per, size = row_chunks(wqkv)
        for j in range(count):
            value = dot_nt(gm[g], wqkv[j * per : (j + 1) * per].reshape(size, 3 * cols))
            for i in range(size // rows):
                own_parts[j * (size // rows) + i][...] = value[:, i * rows : (i + 1) * rows]

    c_qkv = v["c_up"].at[:, :, :, 0 : 3 * cols]
    r_qkv = Reduce(
        place, wires, wqkv, h_qkv, False, c_qkv, None, v["y_qkv"], v["z_qkv"], v["p_qkv"]
    )

    @step
    def grad_q():
        g_qkv.drain()
        weight_grad(blocks(normed), gm, wqkv)

    @step
    def up_free():
        r_up.y_sent()
        pl.semaphore_signal(v["free_sem"], inc=1, device_id=place.c_peer(), device_id_type=MESH)

    @step
    def qkv_send():
        pl.semaphore_wait(v["free_sem"], 1)
        r_qkv.core_send(0)
        r_qkv.core_send(1)

    @step
    def norm_merged():
        wait_all([part_copy(step, mix_first) for step in range(1, groups)])

        def first_in(at):
            t = jnp.concatenate([part[at] for part in own_parts], axis=1)
            for step in range(1, groups):
                t = t + p_recv[step - 1, at].astype(F32)
            return t

        def first_out(at, grad):
            gb[at] = (grad + gmid[at]).astype(LOW)

        gain_sum, bias_sum = norm_back(merged, 1, first_in, first_out)
        sums[1:2] = gain_sum
        sums[2:3] = bias_sum

    gmx = v["gmx"]
    merged_copies = []
    if sizes.pair:
        other_cols = aligned((1 - g) * cols, cols)
        merged_copies = [
            Exchange(place, wires).copy(1, lambda: gb.at[:, other_cols], lambda: gmx.at[1])
        ]

    @step
    def merged_send():
        start_all(merged_copies)
        if sizes.pair:
            gmx[0] = gb[:, own_cols]

    sum_in = v["sum_in"]

    def sum_copy(slot, peer):
        return wires.copy(lambda: (sums, sum_in.at[slot], peer()))

    sum_core = sum_copy(0, place.c_peer)
    sum_x = [sum_copy(k, functools.partial(place.x_peer, k)) for k in range(1, groups)]
    sum_y = sum_copy(groups, place.y_peer)
    sum_z = [sum_copy(groups + k, functools.partial(place.z_peer, k)) for k in range(1, nz)]
    o_up = v["o_up"]
    up_swap = Exchange(place, wires)
    up_copies = [up_swap.copy(k, lambda: o_up.at[g], lambda: o_up.at[g]) for k in range(1, groups)]

    @step
    def sum_0():
        r_down.y_sent()
        sums[0:1] = column_sums(lambda i: gb[aligned(i * chunk, chunk)], per_block, width)
        sum_core.start()

    @step
    def sum_1():
        sum_core.wait()
        sums[...] = sums[...] + sum_in[0]
        start_all(sum_x)

    @step
    def sum_2():
        for copy in sum_x:
            copy.wait()
        for k in range(1, groups):
            sums[0:6] = sums[0:6] + sum_in[k, 0:6]
        sum_y.start()

    @step
    def sum_3():
        sum_y.wait()
        sums[...] = sums[...] + sum_in[groups]
        start_all(sum_z)

    @step
    def sum_4():
        for copy in sum_z:
            copy.wait()
        for k in range(1, nz):
            sums[...] = sums[...] + sum_in[groups + k]
        o_up[g] = sums[...]
        v["o_small"][...] = sums[...]
        start_all(up_copies)

    stores = []
    gj = normed

    @step
    def inputs_back():
        if sizes.pair:
            give_inputs()

    def give_inputs():
        sent_all(normed_copies)
        count, per, size = row_chunks(ws)
        span = width // size

        def body(j):
            value = dot_nt(gb[...], ws[pl.ds(j * per, per)].reshape(size, width))
            at = aligned(lax.rem(j, span) * size, size)
            gj[lax.div(j, span), :, at] = value.astype(LOW)

        loop(count, body)
        for half, name in enumerate(("o_frames", "o_skip")):
            stores.append(pltpu.make_async_copy(gj.at[half], v[name].at[0], local.at[1 + half]))
            stores[-1].start()

    @step
    def output():
        wait_all(out_copies)
        ob = second.at[g]

        def out_rows(i):
            at = aligned(i * chunk, chunk)
            value = middle[at] + second[g, at].astype(F32) + vecs[5:6]
            for step in range(1, groups):
                value = value + cot_all[place.g_at(-step), at].astype(F32)
            ob[at] = value.astype(LOW)

        loop(rows // chunk, out_rows)
        stores.append(pltpu.make_async_copy(ob, v["o_out"].at[0], local.at[0]))
        stores[-1].start()

    if sizes.pair:
        grad_skip, c_skip = wdown.at[:, :, :, 0:cols], v["c_down"].at[:, :, :, 0:cols]
    else:
        grad_skip, c_skip = ws, v["c_skip"]
    r_skip = Reduce(
        place, wires, grad_skip, h_skip, not sizes.pair, c_skip, v["x_skip"], v["y_skip"],
        v["z_skip"], v["p_skip"],
    )

    @step
    def grad_s():
        if sizes.pair:
            for copy in joined_copies + merged_copies:
                copy.wait()
            for half in range(2):
                lefts = [v["io"].at[half], v["joined"].at[half]]
                weight_grad(lefts, gmx, grad_skip, half * (nz // 2))
        else:
            give_inputs()
            parts_sent(mix_first)
            for load in input_loads():
                load.start()
            for load in input_loads():
                load.wait()
            g_skip.drain()
            weight_grad([fr_v], gb, grad_skip)
            weight_grad([sk_v], gb, grad_skip, nz // 2)
        r_skip.core_send(0)
        r_skip.core_send(1)

    def reduce_steps(name, reduced, ready=True):
        for part in range(2):
            add = functools.partial(reduced.core_add, part) if ready else none
            steps[f"{name}_c{part}"] = add

        def add_y(reach):
            for one in reaches(reach):
                reduced.y_add(one)

        for reach in range(last_reach + 1):
            steps[f"{name}_y{reach}"] = functools.partial(add_y, reach)
        steps[name + "_z"], steps[name + "_f"] = reduced.z_add, reduced.spread_on

    reduce_steps("rd", r_down, early)
    reduce_steps("ru", r_up)
    reduce_steps("ro", r_out)
    reduce_steps("rq", r_qkv)
    reduce_steps("rs", r_skip)
    steps["ro_x0"], steps["ro_x1"] = (functools.partial(r_out.x_add, part) for part in range(2))
    if r_skip.spread:
        steps["rs_c1"] = lambda: [r_skip.core_add(1), r_skip.x_add(0), r_skip.x_add(1)]

    assert sorted(ORDER) == sorted(steps), set(ORDER) ^ set(steps)
    order = list(ORDER)
    if not early:
        cut = order.index("out_parts") + 1
        moved = [name for name in order[:cut] if name.startswith("rd_")]
        order[:cut] = [name for name in order[:cut] if not name.startswith("rd_")] + moved
    for name in order:
        steps[name]()

    for copy in up_copies:
        copy.wait()
    for reduced in (r_up, r_down, r_out, r_qkv, r_skip):
        reduced.finish()
        reduced.drain()
    for gather in [g_small, *gathers[6:]] + ([g_skip] if sizes.pair else []):
        gather.drain()
    sent_all(seg_copies + [seg_core] + kv_waits + out_copies)
    sent_all([ga_copy(step) for step in range(1, groups)] + [dkv_copy()])
    if sizes.pair:
        parts_sent(mix_first)
    for store in stores:
        store.wait()


def finish(sizes, *refs):
    wholes, pieces, small, up = refs[0:3], refs[3:8], refs[8], refs[9]
    whole_outs, outs, vectors, up_out = refs[10:13], refs[13:18], refs[18:24], refs[24]
    held, made, passed, sems = refs[25:30], refs[30:35], refs[35], refs[36]
    groups, cols, width = sizes.groups, sizes.cols, sizes.width
    copies = [
        pltpu.make_async_copy(pieces[i], held[i], sems.at[i]) for i in range(5)
    ]
    moves = [
        pltpu.make_async_copy(wholes[i].at[0], passed.at[i], sems.at[5 + i]) for i in range(3)
    ]
    for copy in moves + copies:
        copy.start()
    stores = []
    for i in range(3):
        moves[i].wait()
        stores.append(pltpu.make_async_copy(passed.at[i], whole_outs[i].at[0], sems.at[13 + i]))
        stores[-1].start()
    for i in range(5):
        copies[i].wait()
        half = held[i].shape[2]
        for group in range(groups):
            for core in range(2):
                rows = slice(core * half, (core + 1) * half)
                if i == 4:
                    top = (group * 2 + core) * half
                    made[i][top : top + half] = held[i][group, core].astype(F32)
                elif i == 3 and sizes.direct:
                    for s in range(sizes.n_dp):
                        at = (s * groups + group) * sizes.part
                        made[i][rows, at : at + sizes.part] = held[i][
                            group, core, :, s * sizes.part : (s + 1) * sizes.part
                        ].astype(F32)
                elif i == 3:
                    made[i][rows, group * sizes.units : (group + 1) * sizes.units] = held[i][
                        group, core
                    ].astype(F32)
                else:
                    for third in range(held[i].shape[3] // cols):
                        at = third * width + group * cols
                        made[i][rows, at : at + cols] = held[i][
                            group, core, :, third * cols : (third + 1) * cols
                        ].astype(F32)
        stores.append(pltpu.make_async_copy(made[i], outs[i], sems.at[8 + i]))
        stores[-1].start()
    dp = lax.axis_index("dp")
    if sizes.shard % 128 == 0 and sizes.direct:
        own = aligned(dp * sizes.shard, sizes.shard)
        for row in range(6):
            vectors[row][...] = small[row : row + 1, own]
        per_row = width // sizes.part
        at = aligned(lax.rem(dp, per_row) * sizes.part, sizes.part)
        for group in range(groups):
            up_out[:, group * sizes.part : (group + 1) * sizes.part] = up[
                group, pl.ds(6 + lax.div(dp, per_row), 1), at
            ]
    else:
        for row in range(6):
            vectors[row][...] = small[row : row + 1]
        for group in range(groups):
            up_out[:, group * sizes.units : (group + 1) * sizes.units] = up[
                group, 6:7, 0 : sizes.units
            ]
    for copy in stores:
        copy.wait()


def per_device(sizes, *args):
    (
        frames, skip_frames, cotangent, seg_ids, positions,
        w_skip, b_skip, gain_attn, bias_attn, w_qkv, w_out,
        gain_ffn, bias_ffn, w_up, b_up, w_down, b_down,
    ) = args
    del positions
    n_dp, nz, groups = sizes.n_dp, sizes.nz, sizes.groups
    rows, width, cols, units = sizes.rows, sizes.width, sizes.cols, sizes.units
    heads, part, shard = sizes.heads, sizes.part, sizes.shard
    depth = w_up.shape[0]
    if not sizes.direct:
        w_up = (
            w_up.reshape(depth, n_dp, groups, part).transpose(0, 2, 1, 3).reshape(depth, groups * units)
        )
        group = lax.axis_index("blk") // 2
        b_up = lax.dynamic_slice_in_dim(b_up, group * part, part)
    r_skip, r_down = w_skip.shape[0], w_down.shape[0] // groups
    span = -(-max(shard, part) // 128) * 128

    def low(*shape):
        return pltpu.VMEM(shape, LOW)

    def full(*shape):
        return pltpu.VMEM(shape, F32)

    sizes.pair = groups == 2 and r_skip == r_down
    scratch = [
        low(2, rows, width), low(groups, rows, width),
        low(nz, 2, r_skip, width), low(nz, 2, depth, 3 * cols), low(nz, 2, depth, width),
        low(nz, 2, depth, units), low(nz, 2, r_down, width),
        full(nz, 2, 8, span), full(8, width), full(1, units),
        full(2, groups, 8, rows), low(2, groups, rows, 128),
        full(rows, width), full(rows, width), full(rows, width),
        low(groups, rows, width), low(groups, rows, width),
        low(2, groups, rows, 2 * cols),
        low(groups, cols, rows), low(2, groups, cols, rows),
        full(groups, heads, 1, rows), full(groups, cols, rows), full(groups, heads, 1, rows),
        low(rows, width), low(groups, rows, cols),
        low(groups, rows, units), low(groups, rows, units),
        low(1, 16, 128) if groups > 2 else low(1, rows, width),
        low(groups - 1, rows, width),
        low(rows, width), low(groups, rows, cols),
        low(groups, rows, 3 * cols),
        full(2, groups, rows, rows), low(2, groups, cols, rows),
        low(1, 16, 128) if sizes.pair else low(nz, 2, r_skip // 2, width),
        low(nz, 2, depth // 2, width),
        low(nz, 2, depth // 2, units),
        low(nz, 2, r_down // 2, width),
        low(1, 16, 128) if sizes.pair else low(groups - 1, nz, 2, r_skip // 2, cols),
        low(groups - 1, nz, 2, depth // 2, cols),
        low(nz, r_skip // 2, cols), low(nz, depth // 2, 3 * cols), low(nz, depth // 2, cols),
        low(nz, depth // 2, units), low(nz, r_down // 2, width),
        low(nz - 1, r_skip // 2, cols), low(nz - 1, depth // 2, 3 * cols),
        low(nz - 1, depth // 2, cols), low(nz - 1, depth // 2, units),
        low(nz - 1, r_down // 2, width),
        low(2, rows, width) if sizes.pair else low(1, 16, 128),
        low(groups, rows, cols) if sizes.pair else low(1, 16, 128),
        low(nz, 2, r_down, width) if 2 * r_down == 512 else low(1, 16, 128),
        full(8, width), full(groups + nz, 8, width),
        low(512 if groups * rows <= 512 else 256, groups * rows),
    ]
    wires = 320 if groups * n_dp <= 16 else 1400
    scratch += [pltpu.SemaphoreType.DMA((wires,)), pltpu.SemaphoreType.DMA((wires,))]
    scratch += [pltpu.SemaphoreType.DMA((16,)), pltpu.SemaphoreType.REGULAR]
    hbm, vmem = pl.BlockSpec(memory_space=pltpu.HBM), pl.BlockSpec(memory_space=pltpu.VMEM)
    whole = jax.ShapeDtypeStruct((1, rows, width), LOW)

    def piece(*shape):
        return jax.ShapeDtypeStruct((groups, 2) + shape, LOW)

    vectors = (b_skip, gain_attn, bias_attn, gain_ffn, bias_ffn, b_down, b_up)
    found = pl.pallas_call(
        functools.partial(kernel, sizes),
        out_shape=(
            whole, whole, whole,
            piece(r_skip // 2, cols), piece(depth // 2, 3 * cols), piece(depth // 2, cols),
            piece(depth // 2, units), piece(r_down // 2, width),
            jax.ShapeDtypeStruct((8, width), F32), jax.ShapeDtypeStruct((groups, 8, width), F32),
        ),
        in_specs=[hbm] * 3 + [vmem] * 8 + [hbm] * 5,
        out_specs=[hbm] * 3 + [vmem] * 7,
        scratch_shapes=scratch,
        compiler_params=pltpu.CompilerParams(
            collective_id=0, has_side_effects=True, vmem_limit_bytes=64 * 2**20
        ),
    )(
        frames, skip_frames, cotangent, seg_ids,
        *[vector.reshape(1, -1) for vector in vectors],
        w_skip, w_qkv, w_out, w_up, w_down,
    )
    easy = shard % 128 == 0 and sizes.direct
    line = jax.ShapeDtypeStruct((1, shard if easy else width), F32)
    shapes = [w_skip.shape, w_qkv.shape, w_out.shape, w_up.shape, w_down.shape]
    done = pl.pallas_call(
        functools.partial(finish, sizes),
        out_shape=(whole,) * 3
        + tuple(jax.ShapeDtypeStruct(shape, F32) for shape in shapes)
        + (line,) * 6
        + (jax.ShapeDtypeStruct((1, groups * (part if easy else units)), F32),),
        in_specs=[hbm] * 8 + [vmem] * 2,
        out_specs=[hbm] * 8 + [vmem] * 7,
        scratch_shapes=[pltpu.VMEM(value.shape, LOW) for value in found[3:8]]
        + [pltpu.VMEM(shape, F32) for shape in shapes]
        + [low(3, rows, width), pltpu.SemaphoreType.DMA((16,))],
        compiler_params=pltpu.CompilerParams(vmem_limit_bytes=60 * 2**20),
    )(*found)
    output, grad_frames, grad_skip, g_skip, g_qkv, g_out, g_up, g_down = done[0:8]
    lines = [value.reshape(-1) for value in done[8:15]]
    if not easy:
        at = lax.axis_index("dp")
        lines[0:6] = [lax.dynamic_slice_in_dim(value, at * shard, shard) for value in lines[0:6]]
        by_group = lines[6].reshape(groups, units)
        lines[6] = lax.dynamic_slice_in_dim(by_group, at * part, part, 1).reshape(-1)
    if not sizes.direct:
        g_up = g_up.reshape(depth, groups, n_dp, part).transpose(0, 2, 1, 3).reshape(depth, -1)
    g_b_skip, g_gain_a, g_bias_a, g_gain_f, g_bias_f, g_b_down, g_b_up = lines
    return (
        output, grad_frames, grad_skip, g_skip, g_b_skip, g_gain_a, g_bias_a, g_qkv, g_out,
        g_gain_f, g_bias_f, g_up, g_b_up, g_down, g_b_down,
    )


def solution(mesh):
    rows, lone = P("dp", None), P("dp")
    frames = P("dp", "blk", None)
    in_specs = (frames,) * 3 + (P("dp", "blk"),) * 2
    in_specs += (rows, lone, lone, lone, rows, rows, lone, lone, rows, lone, rows, lone)
    out_specs = (frames,) * 3
    out_specs += (rows, lone, lone, lone, rows, rows, lone, lone, rows, lone, rows, lone)

    def body(*args):
        return per_device(Sizes(mesh.shape, args[0], args[13]), *args)

    return jax.shard_map(
        body, mesh=mesh, in_specs=in_specs, out_specs=out_specs, check_vma=False
    )
```

```python
import functools
import math
import types

import jax
import jax.numpy as jnp
from jax import lax
from jax.experimental import pallas as pl
from jax.experimental.pallas import tpu as pltpu
from jax.sharding import PartitionSpec as P

H = 16
EPSILON = 1e-05
LOW = jnp.bfloat16
F32 = jnp.float32
MESH = pl.DeviceIdType.MESH
FAR = 1e30


def dot(left, right):
    return jnp.dot(left, right, preferred_element_type=F32)


def dot_nt(left, right):
    return lax.dot_general(left, right, (((1,), (1,)), ((), ())), preferred_element_type=F32)


def loop(count, body, unroll=1):
    def visit(index, carry):
        body(index)
        return carry

    lax.fori_loop(0, count, visit, 0, unroll=min(unroll, count))


def loop_from(first, last, body):
    def visit(index, carry):
        body(index)
        return carry

    lax.fori_loop(first, last, visit, 0)


def aligned(start, size):
    return pl.ds(pl.multiple_of(start, size), size)


class Sizes:
    def __init__(self, mesh_shape, frames, w_up):
        self.n_dp, self.n_blk = mesh_shape["dp"], mesh_shape["blk"]
        self.nz = self.n_dp // 2
        self.groups = self.n_blk // 2
        self.rows = frames.shape[1]
        self.width = frames.shape[2]
        self.hidden = w_up.shape[1]
        self.shard = self.width // self.n_dp
        self.cols = self.width // self.groups
        self.heads = H // self.groups
        self.units = self.hidden // self.groups
        self.part = self.units // self.n_dp
        self.direct = self.part % 128 == 0
        self.share = max(1, self.width // (self.groups + 2) // 128) * 128
        self.up_rows = -(-self.units // self.width)


class Wires:
    def __init__(self, place, send_sems, recv_sems):
        self.place, self.send_sems, self.recv_sems, self.used = place, send_sems, recv_sems, 0

    def take(self, count=1):
        first = self.used
        self.used += count
        assert self.used <= self.send_sems.shape[0]
        return first

    def copy(self, ends, index=None):
        return Copy(self, ends, self.take() if index is None else index)


class Copy:
    def __init__(self, wires, ends, index):
        self.wires, self.ends, self.index = wires, ends, index

    def made(self):
        source, target, peer = self.ends()
        index = self.index
        if isinstance(index, tuple):
            index = index[0] + self.wires.place.z + index[1]
        return pltpu.make_async_remote_copy(
            src_ref=source,
            dst_ref=target,
            send_sem=self.wires.send_sems.at[index],
            recv_sem=self.wires.recv_sems.at[index],
            device_id=peer,
            device_id_type=MESH,
        )

    def start(self):
        self.made().start()

    def wait_send(self):
        self.made().wait_send()

    def wait_recv(self):
        self.made().wait_recv()

    def wait(self):
        self.made().wait()


class Place:
    def __init__(self, sizes):
        self.dp, self.blk = lax.axis_index("dp"), lax.axis_index("blk")
        self.z, self.y = lax.div(self.dp, 2), lax.rem(self.dp, 2)
        self.g, self.c = lax.div(self.blk, 2), lax.rem(self.blk, 2)
        self.sizes = sizes

    def z_at(self, step):
        nz = self.sizes.nz
        return lax.rem(self.z + (step + nz), nz)

    def g_at(self, step):
        groups = self.sizes.groups
        return lax.rem(self.g + (step + groups), groups)

    def z_peer(self, step):
        return (self.z_at(step) * 2 + self.y, self.blk)

    def z_next(self, way):
        return ((self.z + way) * 2 + self.y, self.blk)

    def if_z(self, *distances):
        low, high = min(distances + (0,)), max(distances + (0,))
        if low < 0 and high > 0:
            return pl.when(jnp.logical_and(self.z >= -low, self.z < self.sizes.nz - high))
        return pl.when(self.z >= -low if low < 0 else self.z < self.sizes.nz - high)

    def y_peer(self):
        return (self.z * 2 + 1 - self.y, self.blk)

    def x_peer(self, step):
        return (self.dp, self.g_at(step) * 2 + self.c)

    def c_peer(self):
        return (self.dp, self.g * 2 + 1 - self.c)


class Gather:
    def __init__(
        self, place, wires, ref, half, spread=0, span=None, whole_core=False, across=False
    ):
        self.place, self.wires, self.ref, self.across = place, wires, ref, across
        self.half, self.spread, self.span, self.whole_core = half, spread, span, whole_core
        self.nz = place.sizes.nz
        self.groups = place.sizes.groups if spread else 1
        self.z_wires = {
            (way, far): wires.take(self.nz) for way in (1, -1) for far in range(1 + across)
        }
        self.y_wires = wires.take(self.nz)
        self.x_wires = {
            (step, far): wires.take(self.nz) for step in range(1, self.groups) for far in (0, 1)
        }
        self.c_wires = {
            (step, far): 0 if whole_core else wires.take(self.nz)
            for step in range(self.groups)
            for far in (0, 1)
        }

    def at(self, distance, far, step=0):
        place = self.place
        z_index = place.z + distance
        y_index = 1 - place.y if far else place.y
        if self.whole_core:
            return self.ref.at[z_index, y_index]
        rows = aligned(place.c * self.half, self.half)
        if self.span:
            return self.ref.at[z_index, y_index, rows, self.span[0] : self.span[1]]
        if not self.spread:
            return self.ref.at[z_index, y_index, rows]
        cols = aligned(place.g_at(-step) * self.spread, self.spread)
        return self.ref.at[z_index, y_index, rows, cols]

    def copy(self, first, peer, distance, far, step=0):
        def ends():
            piece = self.at(distance, far, step)
            return piece, piece, peer()

        return self.wires.copy(ends, (first, distance))

    def z_copy(self, way, distance, far=0):
        first = self.z_wires[way, far]
        return self.copy(first, lambda: self.place.z_next(way), distance, far)

    def y_copy(self, distance):
        return self.copy(self.y_wires, self.place.y_peer, distance, 0)

    def y_arrival(self, distance):
        return self.copy(self.y_wires, self.place.y_peer, distance, 1)

    def x_copy(self, step, distance, far):
        first = self.x_wires[step, far]
        return self.copy(first, lambda: self.place.x_peer(step), distance, far)

    def c_copy(self, step, distance, far):
        return self.copy(self.c_wires[step, far], self.place.c_peer, distance, far, step)

    def each(self, reach, body):
        if reach == 0:
            body(0)
            return
        for distance in (-reach, reach):
            self.place.if_z(distance)(functools.partial(body, distance))

    def start(self, far=0):
        for way in (1, -1):
            self.place.if_z(way)(lambda way=way: self.z_copy(way, 0, far).start())

    def own(self):
        self.forward(0, 0)

    def forward(self, distance, far):
        if not far and not (self.across and distance):
            self.y_copy(distance).start()
        for step in range(1, self.groups):
            self.x_copy(step, distance, far).start()
        if not self.whole_core:
            self.c_copy(0, distance, far).start()

    def z_step(self, reach, far=0):
        def body(distance):
            way = 1 if distance < 0 else -1
            self.z_copy(way, distance, far).wait_recv()
            self.place.if_z(way)(lambda: self.z_copy(way, distance, far).start())
            self.forward(distance, far)

        self.each(reach, body)

    def y_step(self, reach):
        if self.across and reach:
            self.z_step(reach, 1)
            return

        def body(distance):
            self.y_arrival(distance).wait_recv()
            if self.across:
                self.start(1)
            self.forward(distance, 1)

        self.each(reach, body)

    def x_step(self, reach, far):
        def body(distance):
            for step in range(1, self.groups):
                self.x_copy(step, distance, far).wait_recv()
                self.c_copy(step, distance, far).start()

        self.each(reach, body)

    def z_steps(self):
        for reach in range(1, self.nz):
            self.z_step(reach)

    def y_steps(self):
        for reach in range(self.nz):
            self.y_step(reach)

    def x_steps(self):
        for far in (0, 1):
            for reach in range(self.nz):
                self.x_step(reach, far)

    def c_wait(self, reach, far):
        def body(distance):
            for step in range(self.groups):
                self.c_copy(step, distance, far).wait_recv()

        self.each(reach, body)

    def finish(self):
        for far in (0, 1):
            for reach in range(self.nz):
                self.c_wait(reach, far)

    def drain(self):
        def body(distance):
            for way, far in self.z_wires:
                if way * distance <= 0:
                    copy = self.z_copy(way, distance, far)
                    self.place.if_z(way)(copy.wait_send)
            if not (self.across and distance):
                self.y_copy(distance).wait_send()
            for first in self.x_wires:
                self.x_copy(first[0], distance, first[1]).wait_send()
            if not self.whole_core:
                for first in self.c_wires:
                    self.c_copy(first[0], distance, first[1]).wait_send()

        for reach in range(self.nz):
            self.each(reach, body)


class Exchange:
    def __init__(self, place, wires):
        self.place, self.groups = place, place.sizes.groups
        self.wires = wires
        self.first = wires.take(self.groups)

    def copy(self, step, source, target):
        return self.wires.copy(
            lambda: (source(), target(), self.place.x_peer(step)), self.first + step
        )


class Reduce:
    def __init__(self, place, wires, grad, half, spread, core_in, x_in, y_in, z_in, out):
        self.place, self.wires, self.grad, self.half, self.spread = place, wires, grad, half, spread
        self.core_in, self.x_in, self.y_in, self.z_in, self.out = core_in, x_in, y_in, z_in, out
        self.nz, self.groups = place.sizes.nz, place.sizes.groups
        self.core_copies, self.x_copies, self.y_copies, self.z_copies = {}, {}, {}, {}
        self.fin_copies, self.fwd_copies = {}, {}

    def side(self, part):
        return 1 - self.place.y if part == 0 else self.place.y

    def core_send(self, part):
        def ends():
            side = self.side(part)
            rows = aligned((1 - self.place.c) * self.half, self.half)
            return self.grad.at[:, side, rows], self.core_in.at[:, side], self.place.c_peer()

        copy = self.wires.copy(ends)
        copy.start()
        self.core_copies[part] = copy

    def core_add(self, part):
        side = self.side(part)
        rows = aligned(self.place.c * self.half, self.half)
        self.core_copies[part].wait_recv()

        def body(z):
            self.core_in[z, side] = self.core_in[z, side] + self.grad[z, side, rows]

        loop(self.nz, body)
        if self.spread:
            cols = self.place.sizes.cols
            for step in range(1, self.groups):
                def ends(step=step):
                    side = self.side(part)
                    theirs = aligned(self.place.g_at(step) * cols, cols)
                    return (
                        self.core_in.at[:, side, :, theirs],
                        self.x_in.at[step - 1, :, side],
                        self.place.x_peer(step),
                    )

                copy = self.wires.copy(ends)
                copy.start()
                self.x_copies[part, step] = copy
        elif part == 0:
            self.y_send()

    def x_add(self, part):
        side = self.side(part)
        cols = self.place.sizes.cols
        mine = aligned(self.place.g * cols, cols)
        for step in range(1, self.groups):
            self.x_copies[part, step].wait_recv()

        def body(z):
            total = self.core_in[z, side, :, mine].astype(F32)
            for step in range(1, self.groups):
                total = total + self.x_in[step - 1, z, side].astype(F32)
            self.x_in[0, z, side] = total.astype(LOW)

        loop(self.nz, body)
        if part == 0:
            self.y_send()

    def held(self):
        return self.x_in.at[0] if self.spread else self.core_in

    def y_send(self):
        for step in [*range(1, self.nz), 0]:

            def ends(step=step):
                z_index = self.place.z_at(step)
                source = self.held().at[z_index, self.side(0)]
                return source, self.y_in.at[z_index], self.place.y_peer()

            self.y_copies[step] = self.wires.copy(ends)
            self.y_copies[step].start()

    def y_add(self, step):
        self.y_copies[step].wait_recv()
        z_index, side, held = self.place.z_at(step), self.side(1), self.held()
        self.y_in[z_index] = self.y_in[z_index] + held[z_index, side]
        if step:
            copy = self.wires.copy(
                lambda: (
                    self.y_in.at[self.place.z_at(step)],
                    self.z_in.at[step - 1],
                    self.place.z_peer(step),
                )
            )
            copy.start()
            self.z_copies[step] = copy

    def y_tasks(self):
        steps = [*range(1, self.nz), 0]
        return [functools.partial(self.y_add, step) for step in steps]

    def y_sent(self):
        for copy in self.y_copies.values():
            copy.wait_send()
        self.y_copies.clear()

    def z_add(self):
        place = self.place
        for step in range(1, self.nz):
            self.z_copies[step].wait_recv()

        def body(i):
            at = aligned(i * 16, 16)
            total = self.y_in[place.z, at].astype(F32)
            for step in range(1, self.nz):
                total = total + self.z_in[step - 1, at].astype(F32)
            self.out[place.g, place.c, at] = total.astype(LOW)

        loop(self.half // 16, body)
        for step in range(1, self.groups):
            self.fin_copies[step] = self.wires.copy(
                lambda step=step: self.spot(0) * 2 + (place.x_peer(step),)
            )
            self.fin_copies[step].start()
        self.forward(0)

    def spread_on(self):
        for step in range(1, self.groups):
            self.fin_copies[step].wait_recv()
            self.forward(step)

    def spot(self, step):
        return (self.out.at[self.place.g_at(-step), self.place.c],)

    def forward(self, step):
        self.fwd_copies[step] = self.wires.copy(
            lambda: self.spot(step) * 2 + (self.place.c_peer(),)
        )
        self.fwd_copies[step].start()

    def core_sent(self):
        for copy in self.core_copies.values():
            copy.wait_send()
        self.core_copies.clear()

    def drain(self):
        self.core_sent()
        self.y_sent()
        for copies in (self.x_copies, self.z_copies, self.fin_copies):
            for copy in copies.values():
                copy.wait_send()

    def finish(self):
        for copy in self.fwd_copies.values():
            copy.wait()


def norm_terms(held):
    centred = held - jnp.mean(held, axis=-1, keepdims=True)
    scale = lax.rsqrt(jnp.mean(centred * centred, axis=-1, keepdims=True) + EPSILON)
    return centred * scale, scale


def in_order(
    skip_start, skip_own, cot_share, rest_start, qkv_own, skip_z1, qkv_start, rest_own, skip_z2,
    rest_z1, skip_z3, skip_y0, small_own, skip_y1, small_start, out_start, rest_z2, skip_x0,
    small_z1, skip_x1, out_own, rest_z3, skip_y2, small_z2, small_z3, qkv_z1, rest_y0, skip_x2,
    skip_y3, small_y0, out_z1, skip_x3, skip_w0, rest_a, skip_a, rest_y1, skip_w1, qkv_z2,
    up_start, out_x0, small_y1, rest_y2, small_y2, joined_0, skip_w2, small_y3, vectors, seg_start,
    rest_y3, out_y0, skip_w3, rest_b, skip_b, merge, norm_first, qkv_y0, out_z2, down_start,
    qkv_z3, out_z3, up_own, qkv_y1, qkv_y2, qkv_a, down_own, seg_pass, up_z1, qkv_y3, qkv_b,
    mix_own, mix_others, down_z1, out_y1, out_x1, out_x2, out_y2, out_y3, seg_turn, turn_keys,
    att_other_a, att_other_b, out_w0, up_y0, out_x3, joined_1, up_z2, att_own_a, out_w1, out_w2,
    down_y0, att_own_b, out_w3, out_b, out_a, mid, down_z2, up_z3, up_y1, down_y1, up_a, up_y2,
    up_y3, joined_2, joined_3, down_z3, joined_4, joined_5, up_b, joined_6, feed_own, feed_others,
    down_y2, grad_d, down_a, feed_a, rd_c0, down_y3, down_b, feed_b, part_send, rd_c1, part_own,
    rd_y1, joined_7, grad_u, sums_early, rd_y2, out_parts, ru_c0, ru_c1, norm_second, branch,
    grad_o, rd_y3, back_own_a, ro_c0, back_own_b, ga_wait, ru_y1, back_other_a, ro_c1, ru_y2,
    back_other_b, ro_x0, ru_y3, merge_keys, mix_send, mix_back, ru_y0, ro_x1, up_free, grad_q,
    qkv_send, skips_sent, rq_c0, rd_y0, rd_z, ro_y1, ro_y2, ro_y3, norm_merged, sum_0, merged_send,
    rq_c1, rq_y1, sum_1, ro_y0, ru_z, rq_y2, out_send, rq_y3, grad_s, rs_c0, ro_z, ru_f, rq_y0,
    rs_c1, rs_y1, rs_y2, sum_2, rs_y3, rq_z, rd_f, rd_e, inputs_back, rs_y0, output, sum_3,
    blocks_sent, ru_e, rs_z, rq_f, ro_f, sum_4, ro_e, rq_e, parts_gone, rs_f,
):
    pass


ORDER = in_order.__code__.co_varnames


def kernel(
    sizes, frames, skip, cot, seg, b_skip, gain_a, bias_a, gain_f, bias_f, b_down, b_up, w_skip,
    w_qkv, w_out, w_up, w_down, o_out, o_frames, o_skip, p_skip, p_qkv, p_out, p_up, p_down,
    o_small, o_up, io, cot_all, ws, wqkv, wout, wup, wdown, small, vecs, bup, segs, segc, merged,
    middle, gmid, normed, second, kv, qt, kt, shift, attt, tot, att_own, att_send, active, ghid,
    p_send, p_recv, gb, ga_in, gm, far, vt, c_skip, c_out, c_up, c_down, x_skip, x_out, y_skip,
    y_qkv, y_out, y_up, y_down, z_skip, z_qkv, z_out, z_up, z_down, joined, gmx, grad_down, sums,
    sum_in, turned, send_sems, recv_sems, local_sems, free_sem,
):
    v = types.SimpleNamespace(**locals())
    place = Place(sizes)
    wires = Wires(place, v.send_sems, v.recv_sems)
    local = v.local_sems
    nz, groups, n_dp, n_blk = sizes.nz, sizes.groups, sizes.n_dp, sizes.n_blk
    rows, width, cols, units = sizes.rows, sizes.width, sizes.cols, sizes.units
    heads = sizes.heads
    z, y, g, c = place.z, place.y, place.g, place.c

    def each_group(body):
        if groups == 2:
            body(1)
        else:
            loop_from(1, groups, body)

    barrier = pltpu.get_barrier_semaphore()
    partners = [place.z_peer(step) for step in range(1, nz)] + [place.y_peer()]
    partners += [place.x_peer(step) for step in range(1, groups)] + [place.c_peer()]
    for partner in partners:
        pl.semaphore_signal(barrier, inc=1, device_id=partner, device_id_type=MESH)

    fr_v, sk_v = v.io.at[0], v.io.at[1]

    def input_loads():
        return [
            pltpu.make_async_copy(v.frames.at[0], fr_v, local.at[0]),
            pltpu.make_async_copy(v.skip.at[0], sk_v, local.at[1]),
        ]

    loads = input_loads() + [
        pltpu.make_async_copy(v.cot.at[0], v.cot_all.at[g], local.at[2]),
    ]

    h_skip, h_qkv = v.ws.shape[2] // 2, v.wqkv.shape[2] // 2
    h_out, h_up, h_down = v.wout.shape[2] // 2, v.wup.shape[2] // 2, v.wdown.shape[2] // 2

    stages = {}

    def fetch(name, start, size, tops, index):
        copies = [
            pltpu.make_async_copy(
                getattr(v, name).at[aligned(start, size), part * width : (part + 1) * width],
                buffer.at[top : top + size],
                local.at[index + part],
            )
            for part, (buffer, top) in enumerate(tops)
        ]
        for copy in copies:
            copy.start()
        stages[name] = copies

    merged, middle, gmid = v.merged, v.middle, v.gmid
    up_tops = [
        (middle, h_down), (middle, h_down + h_up), (merged, h_skip + h_out), (gmid, 3 * h_qkv)
    ]
    fetch("w_skip", c * h_skip, h_skip, [(merged, 0)], 3)
    fetch("w_qkv", c * h_qkv, h_qkv, [(gmid, third * h_qkv) for third in range(3)], 4)
    fetch("w_out", c * h_out, h_out, [(merged, h_skip)], 7)
    fetch("w_up", c * h_up, h_up, up_tops, 8)
    fetch("w_down", (g * 2 + c) * h_down, h_down, [(middle, 0)], 12)
    for load in loads:
        load.start()
    ws, wqkv, wout, wup, wdown = v.ws, v.wqkv, v.wout, v.wup, v.wdown
    own_cols = aligned(g * cols, cols)

    def arrived(name):
        for copy in stages[name]:
            copy.wait()

    arrived("w_skip")
    share, shared = sizes.share, groups * sizes.share
    own_share, skip_rows = aligned(g * share, share), aligned(c * h_skip, h_skip)
    ws[z, y, skip_rows, own_share] = merged[0:h_skip, own_share].astype(LOW)
    if shared < width:
        ws[z, y, skip_rows, shared:width] = merged[0:h_skip, shared:width].astype(LOW)
    arrived("w_qkv")
    for third in range(3):
        wqkv[z, y, aligned(c * h_qkv, h_qkv), third * cols : (third + 1) * cols] = gmid[
            third * h_qkv : (third + 1) * h_qkv, own_cols
        ].astype(LOW)
    arrived("w_out")
    wout[z, y, aligned(c * h_out, h_out), own_cols] = merged[
        h_skip : h_skip + h_out, own_cols
    ].astype(LOW)
    arrived("w_up")
    up_rows = aligned(c * h_up, h_up)
    if sizes.direct:
        part = sizes.part
        per_row = width // (part * groups)
        for s in range(n_dp):
            buffer, top = up_tops[s // per_row]
            lane = aligned(g * part + s % per_row * part * groups, part)
            wup[z, y, up_rows, s * part : (s + 1) * part] = buffer[top : top + h_up, lane].astype(LOW)
    else:
        for index, (buffer, top) in enumerate(up_tops):

            @pl.when(lax.div(g * units, width) == index)
            def _(buffer=buffer, top=top):
                lane = aligned(lax.rem(g * units, width), units)
                wup[z, y, up_rows] = buffer[top : top + h_up, lane].astype(LOW)

    arrived("w_down")
    wdown[z, y, aligned(c * h_down, h_down)] = middle[0:h_down].astype(LOW)

    small = v.small
    for row, name in enumerate(("b_skip", "gain_a", "bias_a", "gain_f", "bias_f", "b_down")):
        small[z, y, row : row + 1, 0 : sizes.shard] = getattr(v, name)[...].astype(LOW).astype(F32)
    if sizes.direct:
        own_up = v.b_up[:, aligned(g * sizes.part, sizes.part)]
    else:
        own_up = v.b_up[...]
    small[z, y, 6:7, 0 : sizes.part] = own_up.astype(LOW).astype(F32)
    segs = v.segs
    segs[c, g] = jnp.broadcast_to(v.seg[...].astype(F32), (8, rows))

    pl.semaphore_wait(barrier, len(partners))

    for load in loads:
        load.wait()
    steps = {}

    def step(function):
        steps[function.__name__] = function
        return function

    def none():
        pass

    last_reach = 3

    def reaches(reach):
        return range(reach, nz) if reach == last_reach else (reach,)

    def gather_steps(name, gather):
        many = {
            "z": [gather.z_step, range(1, last_reach + 1)],
            "y": [gather.y_step, range(last_reach + 1)],
        }
        if gather.spread:
            many["x"] = [lambda reach: gather.x_step(reach, 0), range(last_reach + 1)]
            many["w"] = [lambda reach: gather.x_step(reach, 1), range(last_reach + 1)]
        steps[name + "_start"], steps[name + "_own"] = gather.start, gather.own

        def run(method, reach):
            for one in reaches(reach):
                method(one)

        for letter, (method, which) in many.items():
            for reach in which:
                steps[f"{name}_{letter}{reach}"] = functools.partial(run, method, reach)
        if not gather.whole_core:
            steps[name + "_a"] = lambda: [gather.c_wait(reach, 0) for reach in range(nz)]
            steps[name + "_b"] = lambda: [gather.c_wait(reach, 1) for reach in range(nz)]

    g_small = Gather(place, wires, small, 0, whole_core=True)
    g_skip = Gather(place, wires, v.ws, h_skip, spread=share)
    g_qkv = Gather(place, wires, v.wqkv, h_qkv)
    g_out = Gather(place, wires, v.wout, h_out, spread=cols)
    g_up = Gather(place, wires, v.wup, h_up)
    g_down = Gather(place, wires, v.wdown, h_down, across=True)
    gather_steps("small", g_small)
    gather_steps("skip", g_skip)
    gather_steps("qkv", g_qkv)
    gather_steps("out", g_out)
    gather_steps("up", g_up)
    gather_steps("down", g_down)
    gathers = [g_small, g_skip, g_qkv, g_out, g_up, g_down]
    if shared < width:
        g_rest = Gather(place, wires, v.ws, h_skip, span=(shared, width))
        gather_steps("rest", g_rest)
        gathers.append(g_rest)
    else:
        for name in ("start", "own", "z1", "z2", "z3", "y0", "y1", "y2", "y3", "a", "b"):
            steps["rest_" + name] = none

    seg_swap = Exchange(place, wires)
    seg_copies = [
        seg_swap.copy(step, lambda: segs.at[c, g], lambda: segs.at[c, g])
        for step in range(1, groups)
    ]
    seg_core = wires.copy(lambda: (segs.at[c], segs.at[c], place.c_peer()))

    @step
    def seg_start():
        for copy in seg_copies:
            copy.start()

    @step
    def seg_pass():
        for copy in seg_copies:
            copy.wait_recv()
        seg_core.start()

    joined_copies = []
    lines = rows // 4
    for part in range(8):
        if sizes.pair:
            at = part // 4, pl.ds(part % 4 * lines, lines)
            copy = Exchange(place, wires).copy(
                1, lambda at=at: v.io.at[at], lambda at=at: v.joined.at[at]
            )
            joined_copies.append(copy)
            steps[f"joined_{part}"] = copy.start
        else:
            steps[f"joined_{part}"] = none

    vecs, segc = v.vecs, v.segc

    @step
    def vectors():
        for row in range(6):
            vecs[row : row + 1] = jnp.concatenate(
                [small[s // 2, s % 2, row : row + 1, 0 : sizes.shard] for s in range(n_dp)], axis=1
            )
        v.bup[...] = jnp.concatenate(
            [small[s // 2, s % 2, 6:7, 0 : sizes.part] for s in range(n_dp)], axis=1
        )

    @step
    def seg_turn():
        seg_core.wait_recv()
        for core in range(2):

            def turn(block, core=core):
                turned_ids = jnp.broadcast_to(segs[core, block, 0:1], (128, rows)).T
                segc[core, block] = turned_ids.astype(LOW)

            loop(groups, turn)

    tile = min(256, width)
    normed, second, cot_all = v.normed, v.second, v.cot_all

    @step
    def merge():
        def merge_tile(n):
            lane = aligned(n * tile, tile)
            merged[:, lane] = (
                dot(fr_v[...], ws[0 : nz // 2, :, :, lane].reshape(width, tile))
                + dot(sk_v[...], ws[nz // 2 : nz, :, :, lane].reshape(width, tile))
                + vecs[0:1, lane]
            )

        loop(width // tile, merge_tile)

    chunk = 64

    def norm_into(held, gain_row, target):
        def body(i):
            at = aligned(i * chunk, chunk)
            unit, _ = norm_terms(held[at])
            target[at] = (
                unit * vecs[gain_row : gain_row + 1] + vecs[gain_row + 1 : gain_row + 2]
            ).astype(LOW)

        loop(rows // chunk, body)

    def norm_back(held, gain_row, incoming, finish):
        def body(i, carry):
            at = aligned(i * chunk, chunk)
            unit, scale = norm_terms(held[at])
            t = incoming(at)
            scaled = t * vecs[gain_row : gain_row + 1]
            grad = scale * (
                scaled
                - jnp.mean(scaled, axis=-1, keepdims=True)
                - unit * jnp.mean(scaled * unit, axis=-1, keepdims=True)
            )
            finish(at, grad)
            return (
                carry[0] + jnp.sum(t * unit, axis=0, keepdims=True),
                carry[1] + jnp.sum(t, axis=0, keepdims=True),
            )

        zero = jnp.zeros((1, width), F32)
        return lax.fori_loop(0, rows // chunk, body, (zero, zero))


    def sharing(buffer):
        swap = Exchange(place, wires)
        return [
            swap.copy(step, lambda: buffer.at[g], lambda: buffer.at[g])
            for step in range(1, groups)
        ]

    def start_all(copies):
        for copy in copies:
            copy.start()

    def wait_all(copies):
        for copy in copies:
            copy.wait_recv()

    def sent_all(copies):
        for copy in copies:
            copy.wait_send()

    normed_copies, second_copies, cot_copies = sharing(normed), sharing(second), sharing(cot_all)

    @step
    def norm_first():
        norm_into(merged, 1, normed.at[g])
        start_all(normed_copies)

    @step
    def cot_share():
        start_all(cot_copies)

    kv, qt, kt = v.kv, v.qt, v.kt
    shift = v.shift
    pick = (
        lax.broadcasted_iota(jnp.int32, (max(8, heads), cols), 1)
        // (width // H)
        == lax.broadcasted_iota(jnp.int32, (max(8, heads), cols), 0)
    ).astype(F32)
    kv_first = wires.take(groups)

    def kv_copy(block, step):
        return wires.copy(
            lambda: (kv.at[c, block], kv.at[c, block], place.c_peer()), kv_first + step
        )

    def mix(block, step):
        rows_in = normed[block]
        for third in range(3):
            value = dot(
                rows_in,
                wqkv[:, :, :, third * cols : (third + 1) * cols].reshape(width, cols),
            ).astype(LOW)
            if third == 0:
                query = value
            else:
                kv[c, block, :, (third - 1) * cols : third * cols] = value
        kv_copy(block, step).start()
        found = 0.0
        for at in range(0, cols, 128):
            part = query[:, at : at + 128].astype(F32)
            product = part * kv[c, block, :, at : at + 128].astype(F32)
            found = found + lax.dot_general(
                pick[:, at : at + 128],
                product,
                (((1,), (1,)), ((), ())),
                precision=lax.Precision.HIGHEST,
                preferred_element_type=F32,
            )
            qt[block, at : at + 128] = (part * 0.125).T.astype(LOW)
        for head in range(heads):
            shift[block, head] = found[head : head + 1] * 0.125

    @step
    def mix_own():
        mix(g, 0)

    @step
    def mix_others():
        wait_all(normed_copies)
        each_group(lambda step: mix(place.g_at(-step), step))

    kv_waits = [kv_copy(place.g_at(-step), step) for step in range(groups)]
    def slope_row(head):
        index = jnp.full((1, rows), g * heads + head, jnp.int32).astype(F32)
        return jnp.exp2((index + 1.0) * (-8.0 / H))

    def fill_far(block):
        place_k = lax.broadcasted_iota(jnp.int32, (rows, rows), 0) * n_blk
        place_q = lax.broadcasted_iota(jnp.int32, (rows, rows), 1) * n_blk + (block * 2 + c)
        apart = place_k - place_q
        seg_q = segs[c, block, 0:1]
        for core in range(2):

            def body(b, core=core):
                seg_k = segc[core, b].astype(F32)
                same = jnp.concatenate([seg_k] * (rows // 128), axis=1) == seg_q
                distance = jnp.abs(apart + (b * 2 + core)).astype(F32)
                far[core, b] = jnp.where(same, distance, FAR)

            loop(groups, body)

    def padded(half_value, half):
        zero = jnp.zeros_like(half_value)
        return jnp.concatenate([half_value, zero] if half == 0 else [zero, half_value], axis=0)

    head_width = width // H
    pair_width = 2 * head_width
    attt, tot = v.attt, v.tot

    def score_terms(pair, core, b, queries_pad, slope, moved):
        keys = kv[core, b, :, aligned(pair * pair_width, pair_width)]
        return jnp.exp(dot(keys, queries_pad) - slope * far[core, b] - moved)

    def over_keys(body, first):
        def visit(index, carry):
            return body(lax.div(index, groups), lax.rem(index, groups), carry)

        if groups > 2:
            return lax.fori_loop(0, 2 * groups, visit, first)
        for index in range(2 * groups):
            first = body(index // groups, index % groups, first)
        return first

    def head_at(pair, half):
        return aligned(pair * pair_width + half * head_width, head_width)

    far, vt = v.far, v.vt

    pairs = heads // 2

    def attend(block, first, last):
        def body(pair):
            lanes = aligned(pair * pair_width, pair_width)
            fixed = []
            for half in range(2):
                head = pair * 2 + half
                fixed.append(
                    (padded(qt[block, head_at(pair, half)], half), slope_row(head), shift[block, head])
                )

            def keys_in(core, b, carry):
                done = []
                for half in range(2):
                    total, summed = carry[half]
                    terms = score_terms(pair, core, b, *fixed[half])
                    total = total + jnp.sum(terms, axis=0, keepdims=True)
                    done.append((total, summed + dot(vt[core, b, lanes], terms.astype(LOW))))
                return tuple(done)

            start = (jnp.zeros((1, rows), F32), jnp.zeros((pair_width, rows), F32))
            found = over_keys(keys_in, (start, start))
            for half in range(2):
                total, summed = found[half]
                tot[block, pair * 2 + half] = total
                own = summed[half * head_width : (half + 1) * head_width]
                attt[block, head_at(pair, half)] = own / total

        loop_from(first, last, body)

    att_own, att_send = v.att_own, v.att_send
    att_first = wires.take(groups)

    def att_copy(step, block):
        return wires.copy(
            lambda: (att_send.at[block], att_own.at[:, own_cols], place.x_peer(step)),
            att_first + step,
        )

    @step
    def turn_keys():
        wait_all(kv_waits)
        for core in range(2):

            def turn(b, core=core):
                vt[core, b] = kv[core, b, :, cols : 2 * cols].T
                kt[core, b] = kv[core, b, :, 0:cols].T

            loop(groups, turn)

    def attend_end(step):
        block = place.g_at(step)
        att_send[block] = attt[block].T.astype(LOW)
        att_copy(step, block).start()

    def attend_other(step):
        fill_far(place.g_at(step))
        attend(place.g_at(step), 0, pairs)
        attend_end(step)

    in_two = groups == 2

    @step
    def att_other_a():
        if in_two:
            fill_far(place.g_at(1))
            attend(place.g_at(1), 0, pairs // 2)

    @step
    def att_other_b():
        if in_two:
            attend(place.g_at(1), pairs // 2, pairs)
            attend_end(1)
        else:
            each_group(attend_other)

    @step
    def att_own_a():
        fill_far(g)
        attend(g, 0, pairs // 2)

    @step
    def att_own_b():
        attend(g, pairs // 2, pairs)
        att_own[:, own_cols] = attt[g].T.astype(LOW)

    @step
    def mid():
        wait_all([att_copy(step, place.g_at(step)) for step in range(1, groups)])

        def middle_tile(n):
            lane = aligned(n * tile, tile)
            middle[:, lane] = merged[:, lane] + dot(
                att_own[...], wout[:, :, :, lane].reshape(width, tile)
            )

        loop(width // tile, middle_tile)
        norm_into(middle, 3, second.at[g])
        start_all(second_copies)

    active, ghid = v.active, v.ghid
    unit_tile = 256
    shard_rows = wdown.shape[2]

    def feed(block):
        def body(u):
            lane = aligned(u * unit_tile, unit_tile)
            pre = dot(second[block], wup[:, :, :, lane].reshape(width, unit_tile)) + v.bup[:, lane]
            normal = 0.5 * (1.0 + lax.erf(pre * (0.5**0.5)))
            active[block, :, lane] = (pre * normal).astype(LOW)
            slope = normal + pre * (jnp.exp(-0.5 * pre * pre) * (1.0 / math.sqrt(2.0 * math.pi)))
            ghid[block, :, lane] = slope.astype(LOW)

        loop(units // unit_tile, body)

    def feed_back(lane, weight):
        def body(block):
            back = dot_nt(cot_all[block], weight)
            ghid[block, :, lane] = (back * ghid[block, :, lane].astype(F32)).astype(LOW)

        for block in range(groups) if groups == 2 else ():
            body(block)
        if groups > 2:
            loop(groups, body)

    def row_chunks(ref, most=512):
        per = min(nz, max(1, most // (2 * ref.shape[2])))
        return nz // per, per, per * 2 * ref.shape[2]

    def back_product(left, weight, store):
        count, per, size = row_chunks(weight)

        def body(j):
            value = dot_nt(left[...], weight[pl.ds(j * per, per)].reshape(size, weight.shape[3]))
            store(aligned(j * size, size), value)

        loop(count, body)

    turned = v.turned

    def weight_grad(lefts, right, grad, left_at=0):
        count, per, size = row_chunks(grad, turned.shape[0])
        step_cols = min(512, grad.shape[3])
        depth = len(lefts) * rows
        count = count * lefts[0].shape[1] // (n_dp * grad.shape[2])

        def body(j):
            lane = aligned(j * size, size)
            for b, left in enumerate(lefts):
                turned[0:size, b * rows : (b + 1) * rows] = left[:, lane].T

            def inner(n):
                out = aligned(n * step_cols, step_cols)
                part = right[:, out] if len(right.shape) == 2 else right[:, :, out]
                value = dot(turned[0:size, 0:depth], part.reshape(depth, step_cols))
                grad[pl.ds(left_at + j * per, per), :, :, out] = value.astype(LOW).reshape(
                    per, 2, size // per // 2, step_cols
                )

            loop(grad.shape[3] // step_cols, inner, 2)

        loop(count, body)

    def blocks(ref):
        return [ref.at[b] for b in range(groups)]

    @step
    def feed_own():
        feed(g)

    @step
    def feed_others():
        wait_all(second_copies)
        each_group(lambda step: feed(place.g_at(step)))

    early = shard_rows == unit_tile
    grad_down = v.grad_down if early else wdown
    r_down = Reduce(
        place, wires, grad_down, h_down, False, v.c_down, None, v.y_down, v.z_down,
        v.p_down,
    )

    def down_gradient():
        weight_grad(blocks(active), cot_all, grad_down)
        r_down.core_send(0)
        r_down.core_send(1)

    @step
    def grad_d():
        wait_all(cot_copies)
        if early:
            down_gradient()

    def feed_shard(z_index, y_index):
        lane = aligned((z_index * 2 + y_index) * unit_tile, unit_tile)
        feed_back(lane, wdown[z_index, y_index])

    @step
    def feed_a():
        if early:
            loop(nz, lambda z_index: feed_shard(z_index, y))

    @step
    def feed_b():
        if early:
            loop(nz, lambda z_index: feed_shard(z_index, 1 - y))
            return
        per = unit_tile // (2 * shard_rows)

        def feed_tile(u):
            weight = wdown[pl.ds(u * per, per)].reshape(unit_tile, width)
            feed_back(aligned(u * unit_tile, unit_tile), weight)

        loop(units // unit_tile, feed_tile)

    lend = groups > 2
    p_send, p_recv = v.io if lend else v.p_send, v.p_recv

    def store_into(ref, kind):
        def store(lane, value):
            ref[:, lane] = value.astype(kind)

        return store

    second_first, mix_first = wires.take(groups), wires.take(groups)

    def part_copy(step, first):
        return wires.copy(
            lambda: (p_send.at[part_slot(step)], p_recv.at[step - 1], place.x_peer(step)),
            first + step,
        )

    def part_slot(step):
        return 0 if groups == 2 else lax.rem(step, 2)

    def send_part(step, left, weight, first):
        if groups > 3:

            @pl.when(step > 2)
            def _():
                part_copy(step - 2, first).wait_send()

        back_product(left, weight, store_into(p_send.at[part_slot(step)], LOW))
        part_copy(step, first).start()

    def parts_sent(first):
        for step in range(max(1, groups - 2), groups):
            part_copy(step, first).wait_send()

    @step
    def part_send():
        each_group(lambda step: send_part(step, ghid.at[place.g_at(step)], wup, second_first))

    @step
    def part_own():
        back_product(ghid.at[g], wup, store_into(gmid, F32))

    def down_tile(left, target, n):
        lane = aligned(n * tile, tile)
        target(lane, dot(left[...], wdown[:, :, :, lane].reshape(units, tile)))

    r_up = Reduce(
        place, wires, wup, h_up, False, v.c_up, None, v.y_up, v.z_up, v.p_up
    )

    @step
    def grad_u():
        g_up.drain()
        weight_grad(blocks(second), ghid, wup)
        r_up.core_send(0)
        r_up.core_send(1)

    def other_down(step):
        block = place.g_at(step)

        def keep(lane, value):
            second[block, :, lane] = value.astype(LOW)

        loop(width // tile, lambda n: down_tile(active.at[block], keep, n))

    def own_down(lane, value):
        second[g, :, lane] = value.astype(LOW)

    @step
    def out_parts():
        sent_all(second_copies)
        each_group(other_down)
        loop(width // tile, lambda n: down_tile(active.at[g], own_down, n))
        g_down.drain()
        if not early:
            down_gradient()
            r_down.core_add(0)
            r_down.core_add(1)

    sums = v.sums
    sums[...] = jnp.zeros_like(sums)

    def column_sums(read, count, wide):
        def body(i, total):
            return total + jnp.sum(read(i).astype(F32), axis=0, keepdims=True)

        return lax.fori_loop(0, count, body, jnp.zeros((1, wide), F32))

    per_block = rows // chunk
    @step
    def sums_early():
        ghid_sum = column_sums(
            lambda i: ghid[lax.div(i, per_block), aligned(lax.rem(i, per_block) * chunk, chunk)],
            groups * per_block,
            units,
        )
        if units >= width:
            for row in range(sizes.up_rows):
                sums[6 + row : 7 + row] = ghid_sum[:, row * width : (row + 1) * width]
        else:
            sums[6:7, 0:units] = ghid_sum
        sums[5:6] = column_sums(lambda i: cot_all[g, aligned(i * chunk, chunk)], per_block, width)

    gb = v.gb

    @step
    def norm_second():
        wait_all([part_copy(step, second_first) for step in range(1, groups)])

        def second_in(at):
            t = gmid[at]
            for step in range(1, groups):
                t = t + p_recv[step - 1, at].astype(F32)
            return t

        def second_out(at, grad):
            total = grad + cot_all[g, at].astype(F32)
            gmid[at] = total
            gb[at] = total.astype(LOW)

        gain_sum, bias_sum = norm_back(middle, 3, second_in, second_out)
        sums[3:4] = gain_sum
        sums[4:5] = bias_sum

    ga_in, ga_send = v.ga_in, att_send
    ga_first = wires.take(groups)

    def ga_copy(step):
        block = place.g_at(step)
        return wires.copy(
            lambda: (ga_send.at[block], ga_in.at[g], place.x_peer(step)), ga_first + step
        )

    @step
    def branch():
        sent_all([att_copy(step, place.g_at(step)) for step in range(1, groups)])
        count, per, size = row_chunks(wout)

        def branch_back(j):
            value = dot_nt(gb[...], wout[pl.ds(j * per, per)].reshape(size, width)).astype(LOW)
            for b in range(max(1, size // cols)):
                if size >= cols:
                    ga_send[j * (size // cols) + b] = value[:, b * cols : (b + 1) * cols]
                else:
                    lane = aligned(lax.rem(j, cols // size) * size, size)
                    ga_send[lax.div(j, cols // size), :, lane] = value

        loop(count, branch_back)
        start_all([ga_copy(step) for step in range(1, groups)])
        ga_in[g] = ga_send[g]

    out_swap = Exchange(place, wires)
    out_copies = [
        out_swap.copy(
            step, lambda step=step: second.at[place.g_at(step)], lambda: cot_all.at[g]
        )
        for step in range(1, groups)
    ]
    r_out = Reduce(
        place, wires, wout, h_out, True, v.c_out, v.x_out, v.y_out, v.z_out, v.p_out
    )

    @step
    def grad_o():
        g_out.drain()
        weight_grad([att_own], gb, wout)
        r_out.core_send(0)
        r_out.core_send(1)

    gm = v.gm

    def dkv_lanes(core, start, size):
        return aligned(core * 2 * cols + start, size)

    gat, gqt, skt = vt.at[0, 0], vt.at[0, 1], vt.at[1, 0]

    def back_start(block):
        fill_far(block)
        gat[...] = ga_in[block].T

    def back_attend(block, fresh, first, last):
        def body(pair):
            lanes = aligned(pair * pair_width, pair_width)
            later = aligned(cols + pair * pair_width, pair_width)
            starts = pair * pair_width, cols + pair * pair_width
            fixed, scores = [], []
            for half in range(2):
                head = pair * 2 + half
                at = head_at(pair, half)
                total = tot[block, head]
                grad_att = gat[at].astype(F32)
                scaled = padded(grad_att / total, half)
                grad_total = -jnp.sum(grad_att * attt[block, at], axis=0, keepdims=True) / total
                queries = qt[block, at]
                scores.append((padded(queries, half), slope_row(head), shift[block, head]))
                fixed.append(
                    (
                        scaled.astype(LOW),
                        scaled.T.astype(LOW),
                        grad_total,
                        padded(queries.astype(F32), half).T.astype(LOW),
                    )
                )

            def keys_in(core, b, carry):
                values = kv[core, b, :, later]
                key_grad, value_grad, done = 0.0, 0.0, []
                for half in range(2):
                    shift_sum, query_grad = carry[half]
                    scaled, scaled_nat, grad_total, queries_nat = fixed[half]
                    terms = score_terms(pair, core, b, *scores[half])
                    grad_score = terms * (dot(values, scaled) + grad_total)
                    shift_sum = shift_sum - jnp.sum(grad_score, axis=0, keepdims=True)
                    grad_low = grad_score.astype(LOW)
                    value_grad = value_grad + dot(terms.astype(LOW), scaled_nat)
                    key_grad = key_grad + dot(grad_low, queries_nat)
                    done.append((shift_sum, query_grad + dot(kt[core, b, lanes], grad_low)))
                for start, found in zip(starts, (key_grad, value_grad)):
                    at = dkv_lanes(core, start, pair_width)
                    if not fresh:
                        found = found + active[b, :, at].astype(F32)
                    active[b, :, at] = found.astype(LOW)
                return tuple(done)

            start = (jnp.zeros((1, rows), F32), jnp.zeros((pair_width, rows), F32))
            found = over_keys(keys_in, (start, start))
            for half in range(2):
                shift_sum, query_grad = found[half]
                at = head_at(pair, half)
                own = query_grad[half * head_width : (half + 1) * head_width]
                own_keys = kt[c, block, at].astype(F32)
                gqt[at] = (0.125 * (own + shift_sum * own_keys)).astype(LOW)
                skt[at] = (shift_sum * qt[block, at].astype(F32)).astype(LOW)

        loop_from(first, last, body)

    def back_end(block):
        gm[block, :, 0:cols] = gqt[...].T
        at = dkv_lanes(c, 0, cols)
        active[block, :, at] = active[block, :, at] + skt[...].T

    dkv_wire = wires.take(1)

    def dkv_copy():
        return wires.copy(
            lambda: (
                active.at[:, :, dkv_lanes(1 - c, 0, 2 * cols)],
                gm.at[:, :, cols : 3 * cols],
                place.c_peer(),
            ),
            dkv_wire,
        )

    def back_other(step):
        block = place.g_at(-step)
        back_start(block)
        back_attend(block, False, 0, pairs)
        back_end(block)

    @step
    def back_own_a():
        back_start(g)
        back_attend(g, True, 0, pairs // 2)

    @step
    def back_own_b():
        back_attend(g, True, pairs // 2, pairs)
        back_end(g)

    @step
    def ga_wait():
        wait_all([ga_copy(step) for step in range(1, groups)])

    @step
    def out_send():
        sent_all(cot_copies)
        start_all(out_copies)

    @step
    def back_other_a():
        if in_two:
            back_start(place.g_at(-1))
            back_attend(place.g_at(-1), False, 0, pairs // 2)

    @step
    def back_other_b():
        if in_two:
            back_attend(place.g_at(-1), False, pairs // 2, pairs)
            back_end(place.g_at(-1))
        else:
            each_group(back_other)
        dkv_copy().start()

    @step
    def merge_keys():
        dkv_copy().wait_recv()

        def merge_block(b):
            at = dkv_lanes(c, 0, 2 * cols)
            gm[b, :, cols : 3 * cols] = gm[b, :, cols : 3 * cols] + active[b, :, at]

        loop(groups, merge_block)

    @step
    def mix_send():
        parts_sent(second_first)
        each_group(lambda step: send_part(step, gm.at[place.g_at(step)], wqkv, mix_first))

    own_parts = [far.at[i // groups, i % groups] for i in range(width // rows)]

    @step
    def mix_back():
        count, per, size = row_chunks(wqkv)
        for j in range(count):
            value = dot_nt(gm[g], wqkv[j * per : (j + 1) * per].reshape(size, 3 * cols))
            for i in range(size // rows):
                own_parts[j * (size // rows) + i][...] = value[:, i * rows : (i + 1) * rows]

    c_qkv = v.c_up.at[:, :, :, 0 : 3 * cols]
    r_qkv = Reduce(
        place, wires, wqkv, h_qkv, False, c_qkv, None, v.y_qkv, v.z_qkv, v.p_qkv
    )

    @step
    def grad_q():
        g_qkv.drain()
        weight_grad(blocks(normed), gm, wqkv)

    @step
    def up_free():
        r_up.y_sent()
        pl.semaphore_signal(v.free_sem, inc=1, device_id=place.c_peer(), device_id_type=MESH)

    @step
    def qkv_send():
        pl.semaphore_wait(v.free_sem, 1)
        r_qkv.core_send(0)
        r_qkv.core_send(1)

    @step
    def norm_merged():
        wait_all([part_copy(step, mix_first) for step in range(1, groups)])

        def first_in(at):
            t = jnp.concatenate([part[at] for part in own_parts], axis=1)
            for step in range(1, groups):
                t = t + p_recv[step - 1, at].astype(F32)
            return t

        def first_out(at, grad):
            gb[at] = (grad + gmid[at]).astype(LOW)

        gain_sum, bias_sum = norm_back(merged, 1, first_in, first_out)
        sums[1:2] = gain_sum
        sums[2:3] = bias_sum

    gmx = v.gmx
    merged_copies = []
    if sizes.pair:
        other_cols = aligned((1 - g) * cols, cols)
        merged_copies = [
            Exchange(place, wires).copy(1, lambda: gb.at[:, other_cols], lambda: gmx.at[1])
        ]

    @step
    def merged_send():
        start_all(merged_copies)
        if sizes.pair:
            gmx[0] = gb[:, own_cols]

    sum_in = v.sum_in

    def sum_copy(slot, peer):
        return wires.copy(lambda: (sums, sum_in.at[slot], peer()))

    sum_core = sum_copy(0, place.c_peer)
    sum_x = [sum_copy(k, functools.partial(place.x_peer, k)) for k in range(1, groups)]
    sum_y = sum_copy(groups, place.y_peer)
    sum_z = [sum_copy(groups + k, functools.partial(place.z_peer, k)) for k in range(1, nz)]
    o_up = v.o_up
    up_swap = Exchange(place, wires)
    up_copies = [up_swap.copy(k, lambda: o_up.at[g], lambda: o_up.at[g]) for k in range(1, groups)]

    @step
    def sum_0():
        r_down.y_sent()
        sums[0:1] = column_sums(lambda i: gb[aligned(i * chunk, chunk)], per_block, width)
        sum_core.start()

    @step
    def sum_1():
        sum_core.wait()
        sums[...] = sums[...] + sum_in[0]
        start_all(sum_x)

    @step
    def sum_2():
        for copy in sum_x:
            copy.wait()
        for k in range(1, groups):
            sums[0:6] = sums[0:6] + sum_in[k, 0:6]
        sum_y.start()

    @step
    def sum_3():
        sum_y.wait()
        sums[...] = sums[...] + sum_in[groups]
        start_all(sum_z)

    @step
    def sum_4():
        for copy in sum_z:
            copy.wait()
        for k in range(1, nz):
            sums[...] = sums[...] + sum_in[groups + k]
        o_up[g] = sums[...]
        v.o_small[...] = sums[...]
        start_all(up_copies)

    stores = []
    gj = normed

    @step
    def inputs_back():
        if sizes.pair:
            give_inputs()

    def give_inputs():
        sent_all(normed_copies)
        count, per, size = row_chunks(ws)
        span = width // size

        def body(j):
            value = dot_nt(gb[...], ws[pl.ds(j * per, per)].reshape(size, width))
            at = aligned(lax.rem(j, span) * size, size)
            gj[lax.div(j, span), :, at] = value.astype(LOW)

        loop(count, body)
        for half, name in enumerate(("o_frames", "o_skip")):
            stores.append(pltpu.make_async_copy(gj.at[half], getattr(v, name).at[0], local.at[1 + half]))
            stores[-1].start()

    @step
    def output():
        wait_all(out_copies)
        ob = second.at[g]

        def out_rows(i):
            at = aligned(i * chunk, chunk)
            value = middle[at] + second[g, at].astype(F32) + vecs[5:6]
            for step in range(1, groups):
                value = value + cot_all[place.g_at(-step), at].astype(F32)
            ob[at] = value.astype(LOW)

        loop(rows // chunk, out_rows)
        stores.append(pltpu.make_async_copy(ob, v.o_out.at[0], local.at[0]))
        stores[-1].start()

    if sizes.pair:
        grad_skip, c_skip = wdown.at[:, :, :, 0:cols], v.c_down.at[:, :, :, 0:cols]
    else:
        grad_skip, c_skip = ws, v.c_skip
    r_skip = Reduce(
        place, wires, grad_skip, h_skip, not sizes.pair, c_skip, v.x_skip, v.y_skip,
        v.z_skip, v.p_skip,
    )

    @step
    def grad_s():
        if sizes.pair:
            for copy in joined_copies + merged_copies:
                copy.wait()
            for half in range(2):
                lefts = [v.io.at[half], v.joined.at[half]]
                weight_grad(lefts, gmx, grad_skip, half * (nz // 2))
        else:
            give_inputs()
            parts_sent(mix_first)
            for load in input_loads():
                load.start()
            for load in input_loads():
                load.wait()
            g_skip.drain()
            weight_grad([fr_v], gb, grad_skip)
            weight_grad([sk_v], gb, grad_skip, nz // 2)
        r_skip.core_send(0)
        r_skip.core_send(1)

    def reduce_steps(name, reduced, ready=True):
        for part in range(2):
            add = functools.partial(reduced.core_add, part) if ready else none
            steps[f"{name}_c{part}"] = add

        def add_y(reach):
            for one in reaches(reach):
                reduced.y_add(one)

        for reach in range(last_reach + 1):
            steps[f"{name}_y{reach}"] = functools.partial(add_y, reach)
        steps[name + "_z"], steps[name + "_f"] = reduced.z_add, reduced.spread_on

    reduce_steps("rd", r_down, early)
    reduce_steps("ru", r_up)
    reduce_steps("ro", r_out)
    reduce_steps("rq", r_qkv)
    reduce_steps("rs", r_skip)
    steps["ro_x0"], steps["ro_x1"] = (functools.partial(r_out.x_add, part) for part in range(2))
    if r_skip.spread:
        steps["rs_c1"] = lambda: [r_skip.core_add(1), r_skip.x_add(0), r_skip.x_add(1)]

    @step
    def skips_sent():
        for gather in [g_small, *gathers[6:]] + ([g_skip] if sizes.pair else []):
            gather.drain()

    @step
    def blocks_sent():
        sent_all(seg_copies + [seg_core] + kv_waits + [ga_copy(k) for k in range(1, groups)])

    @step
    def parts_gone():
        if sizes.pair:
            sent_all(out_copies)
            parts_sent(mix_first)
        sent_all([dkv_copy()])

    def reduced_end(reduced):
        reduced.finish()
        reduced.drain()

    steps["rd_e"] = functools.partial(reduced_end, r_down)
    steps["ru_e"] = functools.partial(reduced_end, r_up)
    steps["ro_e"] = functools.partial(reduced_end, r_out)
    steps["rq_e"] = functools.partial(reduced_end, r_qkv)

    assert sorted(ORDER) == sorted(steps), set(ORDER) ^ set(steps)
    order = list(ORDER)
    if not early:
        cut = order.index("out_parts") + 1
        moved = [name for name in order[:cut] if name.startswith("rd_")]
        order[:cut] = [name for name in order[:cut] if not name.startswith("rd_")] + moved
    for name in order:
        steps[name]()

    for copy in up_copies:
        copy.wait()
    r_skip.finish()
    r_skip.drain()
    if not sizes.pair:
        sent_all(out_copies)
    for store in stores:
        store.wait()


def finish(sizes, *refs):
    wholes, pieces, small, up = refs[0:3], refs[3:8], refs[8], refs[9]
    whole_outs, outs, vectors, up_out = refs[10:13], refs[13:18], refs[18:24], refs[24]
    held, made, passed, sems = refs[25:30], refs[30:35], refs[35], refs[36]
    groups, cols, width = sizes.groups, sizes.cols, sizes.width
    copies = [
        pltpu.make_async_copy(pieces[i], held[i], sems.at[i]) for i in range(5)
    ]
    moves = [
        pltpu.make_async_copy(wholes[i].at[0], passed.at[i], sems.at[5 + i]) for i in range(3)
    ]
    for copy in moves + copies:
        copy.start()
    stores = []
    for i in range(3):
        moves[i].wait()
        stores.append(pltpu.make_async_copy(passed.at[i], whole_outs[i].at[0], sems.at[13 + i]))
        stores[-1].start()
    for i in range(5):
        copies[i].wait()
        half = held[i].shape[2]
        for group in range(groups):
            for core in range(2):
                rows = slice(core * half, (core + 1) * half)
                if i == 4:
                    top = (group * 2 + core) * half
                    made[i][top : top + half] = held[i][group, core].astype(F32)
                elif i == 3 and sizes.direct:
                    for s in range(sizes.n_dp):
                        at = (s * groups + group) * sizes.part
                        made[i][rows, at : at + sizes.part] = held[i][
                            group, core, :, s * sizes.part : (s + 1) * sizes.part
                        ].astype(F32)
                elif i == 3:
                    made[i][rows, group * sizes.units : (group + 1) * sizes.units] = held[i][
                        group, core
                    ].astype(F32)
                else:
                    for third in range(held[i].shape[3] // cols):
                        at = third * width + group * cols
                        made[i][rows, at : at + cols] = held[i][
                            group, core, :, third * cols : (third + 1) * cols
                        ].astype(F32)
        stores.append(pltpu.make_async_copy(made[i], outs[i], sems.at[8 + i]))
        stores[-1].start()
    dp = lax.axis_index("dp")
    if sizes.shard % 128 == 0 and sizes.direct:
        own = aligned(dp * sizes.shard, sizes.shard)
        for row in range(6):
            vectors[row][...] = small[row : row + 1, own]
        per_row = width // sizes.part
        at = aligned(lax.rem(dp, per_row) * sizes.part, sizes.part)
        for group in range(groups):
            up_out[:, group * sizes.part : (group + 1) * sizes.part] = up[
                group, pl.ds(6 + lax.div(dp, per_row), 1), at
            ]
    else:
        for row in range(6):
            vectors[row][...] = small[row : row + 1]
        for group in range(groups):
            up_out[:, group * sizes.units : (group + 1) * sizes.units] = up[
                group, 6:7, 0 : sizes.units
            ]
    for copy in stores:
        copy.wait()


def per_device(sizes, *args):
    (
        frames, skip_frames, cotangent, seg_ids, positions,
        w_skip, b_skip, gain_attn, bias_attn, w_qkv, w_out,
        gain_ffn, bias_ffn, w_up, b_up, w_down, b_down,
    ) = args
    del positions
    n_dp, nz, groups = sizes.n_dp, sizes.nz, sizes.groups
    rows, width, cols, units = sizes.rows, sizes.width, sizes.cols, sizes.units
    heads, part, shard = sizes.heads, sizes.part, sizes.shard
    depth = w_up.shape[0]
    if not sizes.direct:
        w_up = (
            w_up.reshape(depth, n_dp, groups, part).transpose(0, 2, 1, 3).reshape(depth, groups * units)
        )
        group = lax.axis_index("blk") // 2
        b_up = lax.dynamic_slice_in_dim(b_up, group * part, part)
    r_skip, r_down = w_skip.shape[0], w_down.shape[0] // groups
    span = -(-max(shard, part) // 128) * 128

    def low(*shape):
        return pltpu.VMEM(shape, LOW)

    def full(*shape):
        return pltpu.VMEM(shape, F32)

    sizes.pair = groups == 2 and r_skip == r_down
    scratch = [
        low(2, rows, width), low(groups, rows, width),
        low(nz, 2, r_skip, width), low(nz, 2, depth, 3 * cols), low(nz, 2, depth, width),
        low(nz, 2, depth, units), low(nz, 2, r_down, width),
        full(nz, 2, 8, span), full(8, width), full(1, units),
        full(2, groups, 8, rows), low(2, groups, rows, 128),
        full(rows, width), full(rows, width), full(rows, width),
        low(groups, rows, width), low(groups, rows, width),
        low(2, groups, rows, 2 * cols),
        low(groups, cols, rows), low(2, groups, cols, rows),
        full(groups, heads, 1, rows), full(groups, cols, rows), full(groups, heads, 1, rows),
        low(rows, width), low(groups, rows, cols),
        low(groups, rows, units), low(groups, rows, units),
        low(1, 16, 128) if groups > 2 else low(1, rows, width),
        low(groups - 1, rows, width),
        low(rows, width), low(groups, rows, cols),
        low(groups, rows, 3 * cols),
        full(2, groups, rows, rows), low(2, groups, cols, rows),
        low(1, 16, 128) if sizes.pair else low(nz, 2, r_skip // 2, width),
        low(nz, 2, depth // 2, width),
        low(nz, 2, depth // 2, units),
        low(nz, 2, r_down // 2, width),
        low(1, 16, 128) if sizes.pair else low(groups - 1, nz, 2, r_skip // 2, cols),
        low(groups - 1, nz, 2, depth // 2, cols),
        low(nz, r_skip // 2, cols), low(nz, depth // 2, 3 * cols), low(nz, depth // 2, cols),
        low(nz, depth // 2, units), low(nz, r_down // 2, width),
        low(nz - 1, r_skip // 2, cols), low(nz - 1, depth // 2, 3 * cols),
        low(nz - 1, depth // 2, cols), low(nz - 1, depth // 2, units),
        low(nz - 1, r_down // 2, width),
        low(2, rows, width) if sizes.pair else low(1, 16, 128),
        low(groups, rows, cols) if sizes.pair else low(1, 16, 128),
        low(nz, 2, r_down, width) if 2 * r_down == 512 else low(1, 16, 128),
        full(8, width), full(groups + nz, 8, width),
        low(512 if groups * rows <= 512 else 256, groups * rows),
    ]
    wires = 320 if groups * n_dp <= 16 else 1400
    scratch += [pltpu.SemaphoreType.DMA((wires,)), pltpu.SemaphoreType.DMA((wires,))]
    scratch += [pltpu.SemaphoreType.DMA((16,)), pltpu.SemaphoreType.REGULAR]
    hbm, vmem = pl.BlockSpec(memory_space=pltpu.HBM), pl.BlockSpec(memory_space=pltpu.VMEM)
    whole = jax.ShapeDtypeStruct((1, rows, width), LOW)

    def piece(*shape):
        return jax.ShapeDtypeStruct((groups, 2) + shape, LOW)

    vectors = (b_skip, gain_attn, bias_attn, gain_ffn, bias_ffn, b_down, b_up)
    found = pl.pallas_call(
        functools.partial(kernel, sizes),
        out_shape=(
            whole, whole, whole,
            piece(r_skip // 2, cols), piece(depth // 2, 3 * cols), piece(depth // 2, cols),
            piece(depth // 2, units), piece(r_down // 2, width),
            jax.ShapeDtypeStruct((8, width), F32), jax.ShapeDtypeStruct((groups, 8, width), F32),
        ),
        in_specs=[hbm] * 3 + [vmem] * 8 + [hbm] * 5,
        out_specs=[hbm] * 3 + [vmem] * 7,
        scratch_shapes=scratch,
        compiler_params=pltpu.CompilerParams(
            collective_id=0, has_side_effects=True, vmem_limit_bytes=64 * 2**20
        ),
    )(
        frames, skip_frames, cotangent, seg_ids,
        *[vector.reshape(1, -1) for vector in vectors],
        w_skip, w_qkv, w_out, w_up, w_down,
    )
    easy = shard % 128 == 0 and sizes.direct
    line = jax.ShapeDtypeStruct((1, shard if easy else width), F32)
    shapes = [w_skip.shape, w_qkv.shape, w_out.shape, w_up.shape, w_down.shape]
    done = pl.pallas_call(
        functools.partial(finish, sizes),
        out_shape=(whole,) * 3
        + tuple(jax.ShapeDtypeStruct(shape, F32) for shape in shapes)
        + (line,) * 6
        + (jax.ShapeDtypeStruct((1, groups * (part if easy else units)), F32),),
        in_specs=[hbm] * 8 + [vmem] * 2,
        out_specs=[hbm] * 8 + [vmem] * 7,
        scratch_shapes=[pltpu.VMEM(value.shape, LOW) for value in found[3:8]]
        + [pltpu.VMEM(shape, F32) for shape in shapes]
        + [low(3, rows, width), pltpu.SemaphoreType.DMA((16,))],
        compiler_params=pltpu.CompilerParams(vmem_limit_bytes=60 * 2**20),
    )(*found)
    output, grad_frames, grad_skip, g_skip, g_qkv, g_out, g_up, g_down = done[0:8]
    lines = [value.reshape(-1) for value in done[8:15]]
    if not easy:
        at = lax.axis_index("dp")
        lines[0:6] = [lax.dynamic_slice_in_dim(value, at * shard, shard) for value in lines[0:6]]
        by_group = lines[6].reshape(groups, units)
        lines[6] = lax.dynamic_slice_in_dim(by_group, at * part, part, 1).reshape(-1)
    if not sizes.direct:
        g_up = g_up.reshape(depth, groups, n_dp, part).transpose(0, 2, 1, 3).reshape(depth, -1)
    g_b_skip, g_gain_a, g_bias_a, g_gain_f, g_bias_f, g_b_down, g_b_up = lines
    return (
        output, grad_frames, grad_skip, g_skip, g_b_skip, g_gain_a, g_bias_a, g_qkv, g_out,
        g_gain_f, g_bias_f, g_up, g_b_up, g_down, g_b_down,
    )


def solution(mesh):
    rows, lone = P("dp", None), P("dp")
    frames = P("dp", "blk", None)
    in_specs = (frames,) * 3 + (P("dp", "blk"),) * 2
    in_specs += (rows, lone, lone, lone, rows, rows, lone, lone, rows, lone, rows, lone)
    out_specs = (frames,) * 3
    out_specs += (rows, lone, lone, lone, rows, rows, lone, lone, rows, lone, rows, lone)

    def body(*args):
        return per_device(Sizes(mesh.shape, args[0], args[13]), *args)

    return jax.shard_map(
        body, mesh=mesh, in_specs=in_specs, out_specs=out_specs, check_vma=False
    )
```

```python
import functools
import math
import types

import jax
import jax.numpy as jnp
from jax import lax
from jax.experimental import pallas as pl
from jax.experimental.pallas import tpu as pltpu
from jax.sharding import PartitionSpec as P

H = 16
EPSILON = 1e-05
LOW = jnp.bfloat16
F32 = jnp.float32
MESH = pl.DeviceIdType.MESH
FAR = 1e30


def dot(left, right):
    return jnp.dot(left, right, preferred_element_type=F32)


def dot_nt(left, right):
    return lax.dot_general(left, right, (((1,), (1,)), ((), ())), preferred_element_type=F32)


def loop(count, body, unroll=2):
    def visit(index, carry):
        body(index)
        return carry

    lax.fori_loop(0, count, visit, 0, unroll=min(unroll, count))


def loop_from(first, last, body):
    def visit(index, carry):
        body(index)
        return carry

    lax.fori_loop(first, last, visit, 0)


def aligned(start, size):
    return pl.ds(pl.multiple_of(start, size), size)


class Sizes:
    def __init__(self, mesh_shape, frames, w_up):
        self.n_dp, self.n_blk = mesh_shape["dp"], mesh_shape["blk"]
        self.nz = self.n_dp // 2
        self.groups = self.n_blk // 2
        self.rows = frames.shape[1]
        self.width = frames.shape[2]
        self.hidden = w_up.shape[1]
        self.shard = self.width // self.n_dp
        self.cols = self.width // self.groups
        self.heads = H // self.groups
        self.units = self.hidden // self.groups
        self.part = self.units // self.n_dp
        self.direct = self.part % 128 == 0
        self.share = max(1, self.width // (self.groups + 2) // 128) * 128
        self.up_rows = -(-self.units // self.width)


class Wires:
    def __init__(self, place, send_sems, recv_sems):
        self.place, self.send_sems, self.recv_sems, self.used = place, send_sems, recv_sems, 0

    def take(self, count=1):
        first = self.used
        self.used += count
        assert self.used <= self.send_sems.shape[0]
        return first

    def copy(self, ends, index=None):
        return Copy(self, ends, self.take() if index is None else index)


class Copy:
    def __init__(self, wires, ends, index):
        self.wires, self.ends, self.index = wires, ends, index

    def made(self):
        source, target, peer = self.ends()
        index = self.index
        if isinstance(index, tuple):
            index = index[0] + self.wires.place.z + index[1]
        return pltpu.make_async_remote_copy(
            src_ref=source,
            dst_ref=target,
            send_sem=self.wires.send_sems.at[index],
            recv_sem=self.wires.recv_sems.at[index],
            device_id=peer,
            device_id_type=MESH,
        )

    def start(self):
        self.made().start()

    def wait_send(self):
        self.made().wait_send()

    def wait_recv(self):
        self.made().wait_recv()

    def wait(self):
        self.made().wait()


class Place:
    def __init__(self, sizes):
        self.dp, self.blk = lax.axis_index("dp"), lax.axis_index("blk")
        self.z, self.y = lax.div(self.dp, 2), lax.rem(self.dp, 2)
        self.g, self.c = lax.div(self.blk, 2), lax.rem(self.blk, 2)
        self.sizes = sizes

    def z_at(self, step):
        nz = self.sizes.nz
        return lax.rem(self.z + (step + nz), nz)

    def g_at(self, step):
        groups = self.sizes.groups
        return lax.rem(self.g + (step + groups), groups)

    def z_peer(self, step):
        return (self.z_at(step) * 2 + self.y, self.blk)

    def z_next(self, way):
        return ((self.z + way) * 2 + self.y, self.blk)

    def if_z(self, *distances):
        low, high = min(distances + (0,)), max(distances + (0,))
        if low < 0 and high > 0:
            return pl.when(jnp.logical_and(self.z >= -low, self.z < self.sizes.nz - high))
        return pl.when(self.z >= -low if low < 0 else self.z < self.sizes.nz - high)

    def y_peer(self):
        return (self.z * 2 + 1 - self.y, self.blk)

    def x_peer(self, step):
        return (self.dp, self.g_at(step) * 2 + self.c)

    def c_peer(self):
        return (self.dp, self.g * 2 + 1 - self.c)


class Gather:
    def __init__(
        self, place, wires, ref, half, spread=0, span=None, whole_core=False, across=False
    ):
        self.place, self.wires, self.ref, self.across = place, wires, ref, across
        self.half, self.spread, self.span, self.whole_core = half, spread, span, whole_core
        self.nz = place.sizes.nz
        self.groups = place.sizes.groups if spread else 1
        self.z_wires = {
            (way, far): wires.take(self.nz) for way in (1, -1) for far in range(1 + across)
        }
        self.y_wires = wires.take(self.nz)
        self.x_wires = {
            (step, far): wires.take(self.nz) for step in range(1, self.groups) for far in (0, 1)
        }
        self.c_wires = {
            (step, far): 0 if whole_core else wires.take(self.nz)
            for step in range(self.groups)
            for far in (0, 1)
        }

    def at(self, distance, far, step=0):
        place = self.place
        z_index = place.z + distance
        y_index = 1 - place.y if far else place.y
        if self.whole_core:
            return self.ref.at[z_index, y_index]
        rows = aligned(place.c * self.half, self.half)
        if self.span:
            return self.ref.at[z_index, y_index, rows, self.span[0] : self.span[1]]
        if not self.spread:
            return self.ref.at[z_index, y_index, rows]
        cols = aligned(place.g_at(-step) * self.spread, self.spread)
        return self.ref.at[z_index, y_index, rows, cols]

    def copy(self, first, peer, distance, far, step=0):
        def ends():
            piece = self.at(distance, far, step)
            return piece, piece, peer()

        return self.wires.copy(ends, (first, distance))

    def z_copy(self, way, distance, far=0):
        first = self.z_wires[way, far]
        return self.copy(first, lambda: self.place.z_next(way), distance, far)

    def y_copy(self, distance):
        return self.copy(self.y_wires, self.place.y_peer, distance, 0)

    def y_arrival(self, distance):
        return self.copy(self.y_wires, self.place.y_peer, distance, 1)

    def x_copy(self, step, distance, far):
        first = self.x_wires[step, far]
        return self.copy(first, lambda: self.place.x_peer(step), distance, far)

    def c_copy(self, step, distance, far):
        return self.copy(self.c_wires[step, far], self.place.c_peer, distance, far, step)

    def each(self, reach, body):
        if reach == 0:
            body(0)
            return
        for distance in (-reach, reach):
            self.place.if_z(distance)(functools.partial(body, distance))

    def start(self, far=0):
        for way in (1, -1):
            self.place.if_z(way)(lambda way=way: self.z_copy(way, 0, far).start())

    def own(self):
        self.forward(0, 0)

    def forward(self, distance, far):
        if not far and not (self.across and distance):
            self.y_copy(distance).start()
        for step in range(1, self.groups):
            self.x_copy(step, distance, far).start()
        if not self.whole_core:
            self.c_copy(0, distance, far).start()

    def z_step(self, reach, far=0):
        def body(distance):
            way = 1 if distance < 0 else -1
            self.z_copy(way, distance, far).wait_recv()
            self.place.if_z(way)(lambda: self.z_copy(way, distance, far).start())
            self.forward(distance, far)

        self.each(reach, body)

    def y_step(self, reach):
        if self.across and reach:
            self.z_step(reach, 1)
            return

        def body(distance):
            self.y_arrival(distance).wait_recv()
            if self.across:
                self.start(1)
            self.forward(distance, 1)

        self.each(reach, body)

    def x_step(self, reach, far):
        def body(distance):
            for step in range(1, self.groups):
                self.x_copy(step, distance, far).wait_recv()
                self.c_copy(step, distance, far).start()

        self.each(reach, body)

    def z_steps(self):
        for reach in range(1, self.nz):
            self.z_step(reach)

    def y_steps(self):
        for reach in range(self.nz):
            self.y_step(reach)

    def x_steps(self):
        for far in (0, 1):
            for reach in range(self.nz):
                self.x_step(reach, far)

    def c_wait(self, reach, far):
        def body(distance):
            for step in range(self.groups):
                self.c_copy(step, distance, far).wait_recv()

        self.each(reach, body)

    def finish(self):
        for far in (0, 1):
            for reach in range(self.nz):
                self.c_wait(reach, far)

    def drain(self):
        def body(distance):
            for way, far in self.z_wires:
                if way * distance <= 0:
                    copy = self.z_copy(way, distance, far)
                    self.place.if_z(way)(copy.wait_send)
            if not (self.across and distance):
                self.y_copy(distance).wait_send()
            for first in self.x_wires:
                self.x_copy(first[0], distance, first[1]).wait_send()
            if not self.whole_core:
                for first in self.c_wires:
                    self.c_copy(first[0], distance, first[1]).wait_send()

        for reach in range(self.nz):
            self.each(reach, body)


class Exchange:
    def __init__(self, place, wires):
        self.place, self.groups = place, place.sizes.groups
        self.wires = wires
        self.first = wires.take(self.groups)

    def copy(self, step, source, target):
        return self.wires.copy(
            lambda: (source(), target(), self.place.x_peer(step)), self.first + step
        )


class Reduce:
    def __init__(self, place, wires, grad, half, spread, core_in, x_in, y_in, z_in, out):
        self.place, self.wires, self.grad, self.half, self.spread = place, wires, grad, half, spread
        self.core_in, self.x_in, self.y_in, self.z_in, self.out = core_in, x_in, y_in, z_in, out
        self.nz, self.groups = place.sizes.nz, place.sizes.groups
        self.core_copies, self.x_copies, self.y_copies, self.z_copies = {}, {}, {}, {}
        self.fin_copies, self.fwd_copies = {}, {}

    def side(self, part):
        return 1 - self.place.y if part == 0 else self.place.y

    def core_send(self, part):
        def ends():
            side = self.side(part)
            rows = aligned((1 - self.place.c) * self.half, self.half)
            return self.grad.at[:, side, rows], self.core_in.at[:, side], self.place.c_peer()

        copy = self.wires.copy(ends)
        copy.start()
        self.core_copies[part] = copy

    def core_add(self, part):
        side = self.side(part)
        rows = aligned(self.place.c * self.half, self.half)
        self.core_copies[part].wait_recv()

        def body(z):
            self.core_in[z, side] = self.core_in[z, side] + self.grad[z, side, rows]

        loop(self.nz, body)
        if self.spread:
            cols = self.place.sizes.cols
            for step in range(1, self.groups):
                def ends(step=step):
                    side = self.side(part)
                    theirs = aligned(self.place.g_at(step) * cols, cols)
                    return (
                        self.core_in.at[:, side, :, theirs],
                        self.x_in.at[step - 1, :, side],
                        self.place.x_peer(step),
                    )

                copy = self.wires.copy(ends)
                copy.start()
                self.x_copies[part, step] = copy
        elif part == 0:
            self.y_send()

    def x_add(self, part):
        side = self.side(part)
        cols = self.place.sizes.cols
        mine = aligned(self.place.g * cols, cols)
        for step in range(1, self.groups):
            self.x_copies[part, step].wait_recv()

        def body(z):
            total = self.core_in[z, side, :, mine].astype(F32)
            for step in range(1, self.groups):
                total = total + self.x_in[step - 1, z, side].astype(F32)
            self.x_in[0, z, side] = total.astype(LOW)

        loop(self.nz, body)
        if part == 0:
            self.y_send()

    def held(self):
        return self.x_in.at[0] if self.spread else self.core_in

    def y_send(self):
        for step in [*range(1, self.nz), 0]:

            def ends(step=step):
                z_index = self.place.z_at(step)
                source = self.held().at[z_index, self.side(0)]
                return source, self.y_in.at[z_index], self.place.y_peer()

            self.y_copies[step] = self.wires.copy(ends)
            self.y_copies[step].start()

    def y_add(self, step):
        self.y_copies[step].wait_recv()
        z_index, side, held = self.place.z_at(step), self.side(1), self.held()
        self.y_in[z_index] = self.y_in[z_index] + held[z_index, side]
        if step:
            copy = self.wires.copy(
                lambda: (
                    self.y_in.at[self.place.z_at(step)],
                    self.z_in.at[step - 1],
                    self.place.z_peer(step),
                )
            )
            copy.start()
            self.z_copies[step] = copy

    def y_tasks(self):
        steps = [*range(1, self.nz), 0]
        return [functools.partial(self.y_add, step) for step in steps]

    def y_sent(self):
        for copy in self.y_copies.values():
            copy.wait_send()
        self.y_copies.clear()

    def z_add(self):
        place = self.place
        for step in range(1, self.nz):
            self.z_copies[step].wait_recv()

        def body(i):
            at = aligned(i * 16, 16)
            total = self.y_in[place.z, at].astype(F32)
            for step in range(1, self.nz):
                total = total + self.z_in[step - 1, at].astype(F32)
            self.out[place.g, place.c, at] = total.astype(LOW)

        loop(self.half // 16, body)
        for step in range(1, self.groups):
            self.fin_copies[step] = self.wires.copy(
                lambda step=step: self.spot(0) * 2 + (place.x_peer(step),)
            )
            self.fin_copies[step].start()
        self.forward(0)

    def spread_on(self):
        for step in range(1, self.groups):
            self.fin_copies[step].wait_recv()
            self.forward(step)

    def spot(self, step):
        return (self.out.at[self.place.g_at(-step), self.place.c],)

    def forward(self, step):
        self.fwd_copies[step] = self.wires.copy(
            lambda: self.spot(step) * 2 + (self.place.c_peer(),)
        )
        self.fwd_copies[step].start()

    def core_sent(self):
        for copy in self.core_copies.values():
            copy.wait_send()
        self.core_copies.clear()

    def drain(self):
        self.core_sent()
        self.y_sent()
        for copies in (self.x_copies, self.z_copies, self.fin_copies):
            for copy in copies.values():
                copy.wait_send()

    def finish(self):
        for copy in self.fwd_copies.values():
            copy.wait()


def norm_terms(held):
    centred = held - jnp.mean(held, axis=-1, keepdims=True)
    scale = lax.rsqrt(jnp.mean(centred * centred, axis=-1, keepdims=True) + EPSILON)
    return centred * scale, scale


def in_order(
    skip_start, skip_own, cot_share, rest_start, qkv_own, skip_z1, qkv_start, rest_own, skip_z2,
    rest_z1, skip_z3, skip_y0, small_own, skip_y1, small_start, out_start, rest_z2, skip_x0,
    small_z1, skip_x1, out_own, rest_z3, skip_y2, small_z2, small_z3, qkv_z1, rest_y0, skip_x2,
    skip_y3, small_y0, out_z1, skip_x3, skip_w0, rest_a, skip_a, rest_y1, skip_w1, qkv_z2,
    up_start, out_x0, small_y1, rest_y2, small_y2, joined_0, skip_w2, small_y3, vectors, seg_start,
    rest_y3, out_y0, skip_w3, rest_b, skip_b, merge, norm_first, qkv_y0, out_z2, down_start,
    qkv_z3, out_z3, up_own, qkv_y1, qkv_y2, qkv_a, down_own, seg_pass, up_z1, qkv_y3, qkv_b,
    mix_own, mix_others, down_z1, out_y1, out_x1, out_x2, out_y2, out_y3, seg_turn, turn_keys,
    att_other_a, att_other_b, out_w0, up_y0, out_x3, joined_1, up_z2, att_own_a, out_w1, out_w2,
    down_y0, att_own_b, out_w3, out_b, out_a, mid, down_z2, up_z3, up_y1, down_y1, up_a, up_y2,
    up_y3, joined_2, joined_3, down_z3, joined_4, joined_5, up_b, joined_6, feed_own, feed_others,
    down_y2, grad_d, down_a, feed_a, rd_c0, down_y3, down_b, feed_b, part_send, rd_c1, part_own,
    rd_y1, joined_7, grad_u, sums_early, rd_y2, out_parts, ru_c0, ru_c1, norm_second, branch,
    grad_o, rd_y3, back_own_a, ro_c0, back_own_b, ga_wait, ru_y1, back_other_a, ro_c1, ru_y2,
    back_other_b, ro_x0, ru_y3, merge_keys, mix_send, mix_back, ru_y0, ro_x1, up_free, grad_q,
    qkv_send, skips_sent, rq_c0, rd_y0, rd_z, ro_y1, ro_y2, ro_y3, norm_merged, sum_0, merged_send,
    rq_c1, rq_y1, sum_1, ro_y0, ru_z, rq_y2, out_send, rq_y3, grad_s, rs_c0, ro_z, ru_f, rq_y0,
    rs_c1, rs_y1, rs_y2, sum_2, rs_y3, rq_z, rd_f, rd_e, inputs_back, rs_y0, output, sum_3,
    blocks_sent, ru_e, rs_z, rq_f, ro_f, sum_4, ro_e, rq_e, parts_gone, rs_f,
):
    pass


ORDER = in_order.__code__.co_varnames


def kernel(
    sizes, frames, skip, cot, seg, b_skip, gain_a, bias_a, gain_f, bias_f, b_down, b_up, w_skip,
    w_qkv, w_out, w_up, w_down, o_out, o_frames, o_skip, p_skip, p_qkv, p_out, p_up, p_down,
    o_small, o_up, io, cot_all, ws, wqkv, wout, wup, wdown, small, vecs, bup, segs, segc, merged,
    middle, gmid, normed, second, kv, qt, kt, shift, attt, tot, att_own, att_send, active, ghid,
    p_send, p_recv, gb, ga_in, gm, far, vt, c_skip, c_out, c_up, c_down, x_skip, x_out, y_skip,
    y_qkv, y_out, y_up, y_down, z_skip, z_qkv, z_out, z_up, z_down, joined, gmx, grad_down, sums,
    sum_in, turned, send_sems, recv_sems, local_sems, free_sem,
):
    v = types.SimpleNamespace(**locals())
    place = Place(sizes)
    wires = Wires(place, v.send_sems, v.recv_sems)
    local = v.local_sems
    nz, groups, n_dp, n_blk = sizes.nz, sizes.groups, sizes.n_dp, sizes.n_blk
    rows, width, cols, units = sizes.rows, sizes.width, sizes.cols, sizes.units
    heads = sizes.heads
    z, y, g, c = place.z, place.y, place.g, place.c

    def each_group(body):
        if groups == 2:
            body(1)
        else:
            loop_from(1, groups, body)

    barrier = pltpu.get_barrier_semaphore()
    partners = [place.z_peer(step) for step in range(1, nz)] + [place.y_peer()]
    partners += [place.x_peer(step) for step in range(1, groups)] + [place.c_peer()]
    for partner in partners:
        pl.semaphore_signal(barrier, inc=1, device_id=partner, device_id_type=MESH)

    fr_v, sk_v = v.io.at[0], v.io.at[1]

    def input_loads():
        return [
            pltpu.make_async_copy(v.frames.at[0], fr_v, local.at[0]),
            pltpu.make_async_copy(v.skip.at[0], sk_v, local.at[1]),
        ]

    loads = input_loads() + [
        pltpu.make_async_copy(v.cot.at[0], v.cot_all.at[g], local.at[2]),
    ]

    h_skip, h_qkv = v.ws.shape[2] // 2, v.wqkv.shape[2] // 2
    h_out, h_up, h_down = v.wout.shape[2] // 2, v.wup.shape[2] // 2, v.wdown.shape[2] // 2

    stages = {}

    def fetch(name, start, size, tops, index):
        copies = [
            pltpu.make_async_copy(
                getattr(v, name).at[aligned(start, size), part * width : (part + 1) * width],
                buffer.at[top : top + size],
                local.at[index + part],
            )
            for part, (buffer, top) in enumerate(tops)
        ]
        for copy in copies:
            copy.start()
        stages[name] = copies

    merged, middle, gmid = v.merged, v.middle, v.gmid
    up_tops = [
        (middle, h_down), (middle, h_down + h_up), (merged, h_skip + h_out), (gmid, 3 * h_qkv)
    ]
    fetch("w_skip", c * h_skip, h_skip, [(merged, 0)], 3)
    fetch("w_qkv", c * h_qkv, h_qkv, [(gmid, third * h_qkv) for third in range(3)], 4)
    fetch("w_out", c * h_out, h_out, [(merged, h_skip)], 7)
    fetch("w_up", c * h_up, h_up, up_tops, 8)
    fetch("w_down", (g * 2 + c) * h_down, h_down, [(middle, 0)], 12)
    for load in loads:
        load.start()
    ws, wqkv, wout, wup, wdown = v.ws, v.wqkv, v.wout, v.wup, v.wdown
    own_cols = aligned(g * cols, cols)

    def arrived(name):
        for copy in stages[name]:
            copy.wait()

    arrived("w_skip")
    share, shared = sizes.share, groups * sizes.share
    own_share, skip_rows = aligned(g * share, share), aligned(c * h_skip, h_skip)
    ws[z, y, skip_rows, own_share] = merged[0:h_skip, own_share].astype(LOW)
    if shared < width:
        ws[z, y, skip_rows, shared:width] = merged[0:h_skip, shared:width].astype(LOW)
    arrived("w_qkv")
    for third in range(3):
        wqkv[z, y, aligned(c * h_qkv, h_qkv), third * cols : (third + 1) * cols] = gmid[
            third * h_qkv : (third + 1) * h_qkv, own_cols
        ].astype(LOW)
    arrived("w_out")
    wout[z, y, aligned(c * h_out, h_out), own_cols] = merged[
        h_skip : h_skip + h_out, own_cols
    ].astype(LOW)
    arrived("w_up")
    up_rows = aligned(c * h_up, h_up)
    if sizes.direct:
        part = sizes.part
        per_row = width // (part * groups)
        for s in range(n_dp):
            buffer, top = up_tops[s // per_row]
            lane = aligned(g * part + s % per_row * part * groups, part)
            wup[z, y, up_rows, s * part : (s + 1) * part] = buffer[top : top + h_up, lane].astype(LOW)
    else:
        for index, (buffer, top) in enumerate(up_tops):

            @pl.when(lax.div(g * units, width) == index)
            def _(buffer=buffer, top=top):
                lane = aligned(lax.rem(g * units, width), units)
                wup[z, y, up_rows] = buffer[top : top + h_up, lane].astype(LOW)

    arrived("w_down")
    wdown[z, y, aligned(c * h_down, h_down)] = middle[0:h_down].astype(LOW)

    small = v.small
    for row, name in enumerate(("b_skip", "gain_a", "bias_a", "gain_f", "bias_f", "b_down")):
        small[z, y, row : row + 1, 0 : sizes.shard] = getattr(v, name)[...].astype(LOW).astype(F32)
    if sizes.direct:
        own_up = v.b_up[:, aligned(g * sizes.part, sizes.part)]
    else:
        own_up = v.b_up[...]
    small[z, y, 6:7, 0 : sizes.part] = own_up.astype(LOW).astype(F32)
    segs = v.segs
    segs[c, g] = jnp.broadcast_to(v.seg[...].astype(F32), (8, rows))

    pl.semaphore_wait(barrier, len(partners))

    for load in loads:
        load.wait()
    steps = {}

    def step(function):
        steps[function.__name__] = function
        return function

    def none():
        pass

    last_reach = 3

    def reaches(reach):
        return range(reach, nz) if reach == last_reach else (reach,)

    def gather_steps(name, gather):
        many = {
            "z": [gather.z_step, range(1, last_reach + 1)],
            "y": [gather.y_step, range(last_reach + 1)],
        }
        if gather.spread:
            many["x"] = [lambda reach: gather.x_step(reach, 0), range(last_reach + 1)]
            many["w"] = [lambda reach: gather.x_step(reach, 1), range(last_reach + 1)]
        steps[name + "_start"], steps[name + "_own"] = gather.start, gather.own

        def run(method, reach):
            for one in reaches(reach):
                method(one)

        for letter, (method, which) in many.items():
            for reach in which:
                steps[f"{name}_{letter}{reach}"] = functools.partial(run, method, reach)
        if not gather.whole_core:
            steps[name + "_a"] = lambda: [gather.c_wait(reach, 0) for reach in range(nz)]
            steps[name + "_b"] = lambda: [gather.c_wait(reach, 1) for reach in range(nz)]

    g_small = Gather(place, wires, small, 0, whole_core=True)
    g_skip = Gather(place, wires, v.ws, h_skip, spread=share)
    g_qkv = Gather(place, wires, v.wqkv, h_qkv)
    g_out = Gather(place, wires, v.wout, h_out, spread=cols)
    g_up = Gather(place, wires, v.wup, h_up)
    g_down = Gather(place, wires, v.wdown, h_down, across=True)
    gather_steps("small", g_small)
    gather_steps("skip", g_skip)
    gather_steps("qkv", g_qkv)
    gather_steps("out", g_out)
    gather_steps("up", g_up)
    gather_steps("down", g_down)
    gathers = [g_small, g_skip, g_qkv, g_out, g_up, g_down]
    if shared < width:
        g_rest = Gather(place, wires, v.ws, h_skip, span=(shared, width))
        gather_steps("rest", g_rest)
        gathers.append(g_rest)
    else:
        for name in ("start", "own", "z1", "z2", "z3", "y0", "y1", "y2", "y3", "a", "b"):
            steps["rest_" + name] = none

    seg_swap = Exchange(place, wires)
    seg_copies = [
        seg_swap.copy(step, lambda: segs.at[c, g], lambda: segs.at[c, g])
        for step in range(1, groups)
    ]
    seg_core = wires.copy(lambda: (segs.at[c], segs.at[c], place.c_peer()))

    @step
    def seg_start():
        for copy in seg_copies:
            copy.start()

    @step
    def seg_pass():
        for copy in seg_copies:
            copy.wait_recv()
        seg_core.start()

    joined_copies = []
    lines = rows // 4
    for part in range(8):
        if sizes.pair:
            at = part // 4, pl.ds(part % 4 * lines, lines)
            copy = Exchange(place, wires).copy(
                1, lambda at=at: v.io.at[at], lambda at=at: v.joined.at[at]
            )
            joined_copies.append(copy)
            steps[f"joined_{part}"] = copy.start
        else:
            steps[f"joined_{part}"] = none

    vecs, segc = v.vecs, v.segc

    @step
    def vectors():
        for row in range(6):
            vecs[row : row + 1] = jnp.concatenate(
                [small[s // 2, s % 2, row : row + 1, 0 : sizes.shard] for s in range(n_dp)], axis=1
            )
        v.bup[...] = jnp.concatenate(
            [small[s // 2, s % 2, 6:7, 0 : sizes.part] for s in range(n_dp)], axis=1
        )

    @step
    def seg_turn():
        seg_core.wait_recv()
        for core in range(2):

            def turn(block, core=core):
                turned_ids = jnp.broadcast_to(segs[core, block, 0:1], (128, rows)).T
                segc[core, block] = turned_ids.astype(LOW)

            loop(groups, turn)

    tile = min(256, width)
    normed, second, cot_all = v.normed, v.second, v.cot_all

    @step
    def merge():
        def merge_tile(n):
            lane = aligned(n * tile, tile)
            merged[:, lane] = (
                dot(fr_v[...], ws[0 : nz // 2, :, :, lane].reshape(width, tile))
                + dot(sk_v[...], ws[nz // 2 : nz, :, :, lane].reshape(width, tile))
                + vecs[0:1, lane]
            )

        loop(width // tile, merge_tile)

    chunk = 64

    def norm_into(held, gain_row, target):
        def body(i):
            at = aligned(i * chunk, chunk)
            unit, _ = norm_terms(held[at])
            target[at] = (
                unit * vecs[gain_row : gain_row + 1] + vecs[gain_row + 1 : gain_row + 2]
            ).astype(LOW)

        loop(rows // chunk, body)

    def norm_back(held, gain_row, incoming, finish):
        def body(i, carry):
            at = aligned(i * chunk, chunk)
            unit, scale = norm_terms(held[at])
            t = incoming(at)
            scaled = t * vecs[gain_row : gain_row + 1]
            grad = scale * (
                scaled
                - jnp.mean(scaled, axis=-1, keepdims=True)
                - unit * jnp.mean(scaled * unit, axis=-1, keepdims=True)
            )
            finish(at, grad)
            return (
                carry[0] + jnp.sum(t * unit, axis=0, keepdims=True),
                carry[1] + jnp.sum(t, axis=0, keepdims=True),
            )

        zero = jnp.zeros((1, width), F32)
        return lax.fori_loop(0, rows // chunk, body, (zero, zero))


    def sharing(buffer):
        swap = Exchange(place, wires)
        return [
            swap.copy(step, lambda: buffer.at[g], lambda: buffer.at[g])
            for step in range(1, groups)
        ]

    def start_all(copies):
        for copy in copies:
            copy.start()

    def wait_all(copies):
        for copy in copies:
            copy.wait_recv()

    def sent_all(copies):
        for copy in copies:
            copy.wait_send()

    normed_copies, second_copies, cot_copies = sharing(normed), sharing(second), sharing(cot_all)

    @step
    def norm_first():
        norm_into(merged, 1, normed.at[g])
        start_all(normed_copies)

    @step
    def cot_share():
        start_all(cot_copies)

    kv, qt, kt = v.kv, v.qt, v.kt
    shift = v.shift
    pick = (
        lax.broadcasted_iota(jnp.int32, (max(8, heads), cols), 1)
        // (width // H)
        == lax.broadcasted_iota(jnp.int32, (max(8, heads), cols), 0)
    ).astype(F32)
    kv_first = wires.take(groups)

    def kv_copy(block, step):
        return wires.copy(
            lambda: (kv.at[c, block], kv.at[c, block], place.c_peer()), kv_first + step
        )

    def mix(block, step):
        rows_in = normed[block]
        for third in range(3):
            value = dot(
                rows_in,
                wqkv[:, :, :, third * cols : (third + 1) * cols].reshape(width, cols),
            ).astype(LOW)
            if third == 0:
                query = value
            else:
                kv[c, block, :, (third - 1) * cols : third * cols] = value
        kv_copy(block, step).start()
        found = 0.0
        for at in range(0, cols, 128):
            part = query[:, at : at + 128].astype(F32)
            product = part * kv[c, block, :, at : at + 128].astype(F32)
            found = found + lax.dot_general(
                pick[:, at : at + 128],
                product,
                (((1,), (1,)), ((), ())),
                precision=lax.Precision.HIGHEST,
                preferred_element_type=F32,
            )
            qt[block, at : at + 128] = (part * 0.125).T.astype(LOW)
        for head in range(heads):
            shift[block, head] = found[head : head + 1] * 0.125

    @step
    def mix_own():
        mix(g, 0)

    @step
    def mix_others():
        wait_all(normed_copies)
        each_group(lambda step: mix(place.g_at(-step), step))

    kv_waits = [kv_copy(place.g_at(-step), step) for step in range(groups)]
    def slope_row(head):
        index = jnp.full((1, rows), g * heads + head, jnp.int32).astype(F32)
        return jnp.exp2((index + 1.0) * (-8.0 / H))

    def fill_far(block):
        place_k = lax.broadcasted_iota(jnp.int32, (rows, rows), 0) * n_blk
        place_q = lax.broadcasted_iota(jnp.int32, (rows, rows), 1) * n_blk + (block * 2 + c)
        apart = place_k - place_q
        seg_q = segs[c, block, 0:1]
        for core in range(2):

            def body(b, core=core):
                seg_k = segc[core, b].astype(F32)
                same = jnp.concatenate([seg_k] * (rows // 128), axis=1) == seg_q
                distance = jnp.abs(apart + (b * 2 + core)).astype(F32)
                far[core, b] = jnp.where(same, distance, FAR)

            loop(groups, body)

    def padded(half_value, half):
        zero = jnp.zeros_like(half_value)
        return jnp.concatenate([half_value, zero] if half == 0 else [zero, half_value], axis=0)

    head_width = width // H
    pair_width = 2 * head_width
    attt, tot = v.attt, v.tot

    def score_terms(pair, core, b, queries_pad, slope, moved):
        keys = kv[core, b, :, aligned(pair * pair_width, pair_width)]
        return jnp.exp(dot(keys, queries_pad) - slope * far[core, b] - moved)

    def over_keys(body, first):
        def visit(index, carry):
            return body(lax.div(index, groups), lax.rem(index, groups), carry)

        if groups > 2:
            return lax.fori_loop(0, 2 * groups, visit, first)
        for index in range(2 * groups):
            first = body(index // groups, index % groups, first)
        return first

    def head_at(pair, half):
        return aligned(pair * pair_width + half * head_width, head_width)

    far, vt = v.far, v.vt

    pairs = heads // 2

    def attend(block, first, last):
        def body(pair):
            lanes = aligned(pair * pair_width, pair_width)
            fixed = []
            for half in range(2):
                head = pair * 2 + half
                fixed.append(
                    (padded(qt[block, head_at(pair, half)], half), slope_row(head), shift[block, head])
                )

            def keys_in(core, b, carry):
                done = []
                for half in range(2):
                    total, summed = carry[half]
                    terms = score_terms(pair, core, b, *fixed[half])
                    total = total + jnp.sum(terms, axis=0, keepdims=True)
                    done.append((total, summed + dot(vt[core, b, lanes], terms.astype(LOW))))
                return tuple(done)

            start = (jnp.zeros((1, rows), F32), jnp.zeros((pair_width, rows), F32))
            found = over_keys(keys_in, (start, start))
            for half in range(2):
                total, summed = found[half]
                tot[block, pair * 2 + half] = total
                own = summed[half * head_width : (half + 1) * head_width]
                attt[block, head_at(pair, half)] = own / total

        loop_from(first, last, body)

    att_own, att_send = v.att_own, v.att_send
    att_first = wires.take(groups)

    def att_copy(step, block):
        return wires.copy(
            lambda: (att_send.at[block], att_own.at[:, own_cols], place.x_peer(step)),
            att_first + step,
        )

    @step
    def turn_keys():
        wait_all(kv_waits)
        for core in range(2):

            def turn(b, core=core):
                vt[core, b] = kv[core, b, :, cols : 2 * cols].T
                kt[core, b] = kv[core, b, :, 0:cols].T

            loop(groups, turn)

    def attend_end(step):
        block = place.g_at(step)
        att_send[block] = attt[block].T.astype(LOW)
        att_copy(step, block).start()

    def attend_other(step):
        fill_far(place.g_at(step))
        attend(place.g_at(step), 0, pairs)
        attend_end(step)

    in_two = groups == 2

    @step
    def att_other_a():
        if in_two:
            fill_far(place.g_at(1))
            attend(place.g_at(1), 0, pairs // 2)

    @step
    def att_other_b():
        if in_two:
            attend(place.g_at(1), pairs // 2, pairs)
            attend_end(1)
        else:
            each_group(attend_other)

    @step
    def att_own_a():
        fill_far(g)
        attend(g, 0, pairs // 2)

    @step
    def att_own_b():
        attend(g, pairs // 2, pairs)
        att_own[:, own_cols] = attt[g].T.astype(LOW)

    @step
    def mid():
        wait_all([att_copy(step, place.g_at(step)) for step in range(1, groups)])

        def middle_tile(n):
            lane = aligned(n * tile, tile)
            middle[:, lane] = merged[:, lane] + dot(
                att_own[...], wout[:, :, :, lane].reshape(width, tile)
            )

        loop(width // tile, middle_tile)
        norm_into(middle, 3, second.at[g])
        start_all(second_copies)

    active, ghid = v.active, v.ghid
    unit_tile = 256
    shard_rows = wdown.shape[2]

    def feed(block):
        def body(u):
            lane = aligned(u * unit_tile, unit_tile)
            pre = dot(second[block], wup[:, :, :, lane].reshape(width, unit_tile)) + v.bup[:, lane]
            normal = 0.5 * (1.0 + lax.erf(pre * (0.5**0.5)))
            active[block, :, lane] = (pre * normal).astype(LOW)
            slope = normal + pre * (jnp.exp(-0.5 * pre * pre) * (1.0 / math.sqrt(2.0 * math.pi)))
            ghid[block, :, lane] = slope.astype(LOW)

        loop(units // unit_tile, body)

    def feed_back(lane, weight):
        def body(block):
            back = dot_nt(cot_all[block], weight)
            ghid[block, :, lane] = (back * ghid[block, :, lane].astype(F32)).astype(LOW)

        for block in range(groups) if groups == 2 else ():
            body(block)
        if groups > 2:
            loop(groups, body)

    def row_chunks(ref, most=512):
        per = min(nz, max(1, most // (2 * ref.shape[2])))
        return nz // per, per, per * 2 * ref.shape[2]

    def back_product(left, weight, store):
        count, per, size = row_chunks(weight)

        def body(j):
            value = dot_nt(left[...], weight[pl.ds(j * per, per)].reshape(size, weight.shape[3]))
            store(aligned(j * size, size), value)

        loop(count, body)

    turned = v.turned

    def weight_grad(lefts, right, grad, left_at=0):
        count, per, size = row_chunks(grad, turned.shape[0])
        step_cols = min(512, grad.shape[3])
        depth = len(lefts) * rows
        count = count * lefts[0].shape[1] // (n_dp * grad.shape[2])

        def body(j):
            lane = aligned(j * size, size)
            for b, left in enumerate(lefts):
                turned[0:size, b * rows : (b + 1) * rows] = left[:, lane].T

            def inner(n):
                out = aligned(n * step_cols, step_cols)
                part = right[:, out] if len(right.shape) == 2 else right[:, :, out]
                value = dot(turned[0:size, 0:depth], part.reshape(depth, step_cols))
                grad[pl.ds(left_at + j * per, per), :, :, out] = value.astype(LOW).reshape(
                    per, 2, size // per // 2, step_cols
                )

            loop(grad.shape[3] // step_cols, inner)

        loop(count, body)

    def blocks(ref):
        return [ref.at[b] for b in range(groups)]

    @step
    def feed_own():
        feed(g)

    @step
    def feed_others():
        wait_all(second_copies)
        each_group(lambda step: feed(place.g_at(step)))

    early = shard_rows == unit_tile
    grad_down = v.grad_down if early else wdown
    r_down = Reduce(
        place, wires, grad_down, h_down, False, v.c_down, None, v.y_down, v.z_down,
        v.p_down,
    )

    def down_gradient():
        weight_grad(blocks(active), cot_all, grad_down)
        r_down.core_send(0)
        r_down.core_send(1)

    @step
    def grad_d():
        wait_all(cot_copies)
        if early:
            down_gradient()

    def feed_shard(z_index, y_index):
        lane = aligned((z_index * 2 + y_index) * unit_tile, unit_tile)
        feed_back(lane, wdown[z_index, y_index])

    @step
    def feed_a():
        if early:
            loop(nz, lambda z_index: feed_shard(z_index, y))

    @step
    def feed_b():
        if early:
            loop(nz, lambda z_index: feed_shard(z_index, 1 - y))
            return
        per = unit_tile // (2 * shard_rows)

        def feed_tile(u):
            weight = wdown[pl.ds(u * per, per)].reshape(unit_tile, width)
            feed_back(aligned(u * unit_tile, unit_tile), weight)

        loop(units // unit_tile, feed_tile)

    lend = groups > 2
    p_send, p_recv = v.io if lend else v.p_send, v.p_recv

    def store_into(ref, kind):
        def store(lane, value):
            ref[:, lane] = value.astype(kind)

        return store

    second_first, mix_first = wires.take(groups), wires.take(groups)

    def part_copy(step, first):
        return wires.copy(
            lambda: (p_send.at[part_slot(step)], p_recv.at[step - 1], place.x_peer(step)),
            first + step,
        )

    def part_slot(step):
        return 0 if groups == 2 else lax.rem(step, 2)

    def send_part(step, left, weight, first):
        if groups > 3:

            @pl.when(step > 2)
            def _():
                part_copy(step - 2, first).wait_send()

        back_product(left, weight, store_into(p_send.at[part_slot(step)], LOW))
        part_copy(step, first).start()

    def parts_sent(first):
        for step in range(max(1, groups - 2), groups):
            part_copy(step, first).wait_send()

    @step
    def part_send():
        each_group(lambda step: send_part(step, ghid.at[place.g_at(step)], wup, second_first))

    @step
    def part_own():
        back_product(ghid.at[g], wup, store_into(gmid, F32))

    def down_tile(left, target, n):
        lane = aligned(n * tile, tile)
        target(lane, dot(left[...], wdown[:, :, :, lane].reshape(units, tile)))

    r_up = Reduce(
        place, wires, wup, h_up, False, v.c_up, None, v.y_up, v.z_up, v.p_up
    )

    @step
    def grad_u():
        g_up.drain()
        weight_grad(blocks(second), ghid, wup)
        r_up.core_send(0)
        r_up.core_send(1)

    def other_down(step):
        block = place.g_at(step)

        def keep(lane, value):
            second[block, :, lane] = value.astype(LOW)

        loop(width // tile, lambda n: down_tile(active.at[block], keep, n))

    def own_down(lane, value):
        second[g, :, lane] = value.astype(LOW)

    @step
    def out_parts():
        sent_all(second_copies)
        each_group(other_down)
        loop(width // tile, lambda n: down_tile(active.at[g], own_down, n))
        g_down.drain()
        if not early:
            down_gradient()
            r_down.core_add(0)
            r_down.core_add(1)

    sums = v.sums
    sums[...] = jnp.zeros_like(sums)

    def column_sums(read, count, wide):
        def body(i, total):
            return total + jnp.sum(read(i).astype(F32), axis=0, keepdims=True)

        return lax.fori_loop(0, count, body, jnp.zeros((1, wide), F32))

    per_block = rows // chunk
    @step
    def sums_early():
        ghid_sum = column_sums(
            lambda i: ghid[lax.div(i, per_block), aligned(lax.rem(i, per_block) * chunk, chunk)],
            groups * per_block,
            units,
        )
        if units >= width:
            for row in range(sizes.up_rows):
                sums[6 + row : 7 + row] = ghid_sum[:, row * width : (row + 1) * width]
        else:
            sums[6:7, 0:units] = ghid_sum
        sums[5:6] = column_sums(lambda i: cot_all[g, aligned(i * chunk, chunk)], per_block, width)

    gb = v.gb

    @step
    def norm_second():
        wait_all([part_copy(step, second_first) for step in range(1, groups)])

        def second_in(at):
            t = gmid[at]
            for step in range(1, groups):
                t = t + p_recv[step - 1, at].astype(F32)
            return t

        def second_out(at, grad):
            total = grad + cot_all[g, at].astype(F32)
            gmid[at] = total
            gb[at] = total.astype(LOW)

        gain_sum, bias_sum = norm_back(middle, 3, second_in, second_out)
        sums[3:4] = gain_sum
        sums[4:5] = bias_sum

    ga_in, ga_send = v.ga_in, att_send
    ga_first = wires.take(groups)

    def ga_copy(step):
        block = place.g_at(step)
        return wires.copy(
            lambda: (ga_send.at[block], ga_in.at[g], place.x_peer(step)), ga_first + step
        )

    @step
    def branch():
        sent_all([att_copy(step, place.g_at(step)) for step in range(1, groups)])
        count, per, size = row_chunks(wout)

        def branch_back(j):
            value = dot_nt(gb[...], wout[pl.ds(j * per, per)].reshape(size, width)).astype(LOW)
            for b in range(max(1, size // cols)):
                if size >= cols:
                    ga_send[j * (size // cols) + b] = value[:, b * cols : (b + 1) * cols]
                else:
                    lane = aligned(lax.rem(j, cols // size) * size, size)
                    ga_send[lax.div(j, cols // size), :, lane] = value

        loop(count, branch_back)
        start_all([ga_copy(step) for step in range(1, groups)])
        ga_in[g] = ga_send[g]

    out_swap = Exchange(place, wires)
    out_copies = [
        out_swap.copy(
            step, lambda step=step: second.at[place.g_at(step)], lambda: cot_all.at[g]
        )
        for step in range(1, groups)
    ]
    r_out = Reduce(
        place, wires, wout, h_out, True, v.c_out, v.x_out, v.y_out, v.z_out, v.p_out
    )

    @step
    def grad_o():
        g_out.drain()
        weight_grad([att_own], gb, wout)
        r_out.core_send(0)
        r_out.core_send(1)

    gm = v.gm

    def dkv_lanes(core, start, size):
        return aligned(core * 2 * cols + start, size)

    gat, gqt, skt = vt.at[0, 0], vt.at[0, 1], vt.at[1, 0]

    def back_start(block):
        fill_far(block)
        gat[...] = ga_in[block].T

    def back_attend(block, fresh, first, last):
        def body(pair):
            lanes = aligned(pair * pair_width, pair_width)
            later = aligned(cols + pair * pair_width, pair_width)
            starts = pair * pair_width, cols + pair * pair_width
            fixed, scores = [], []
            for half in range(2):
                head = pair * 2 + half
                at = head_at(pair, half)
                total = tot[block, head]
                grad_att = gat[at].astype(F32)
                scaled = padded(grad_att / total, half)
                grad_total = -jnp.sum(grad_att * attt[block, at], axis=0, keepdims=True) / total
                queries = qt[block, at]
                scores.append((padded(queries, half), slope_row(head), shift[block, head]))
                fixed.append(
                    (
                        scaled.astype(LOW),
                        scaled.T.astype(LOW),
                        grad_total,
                        padded(queries.astype(F32), half).T.astype(LOW),
                    )
                )

            def keys_in(core, b, carry):
                values = kv[core, b, :, later]
                key_grad, value_grad, done = 0.0, 0.0, []
                for half in range(2):
                    shift_sum, query_grad = carry[half]
                    scaled, scaled_nat, grad_total, queries_nat = fixed[half]
                    terms = score_terms(pair, core, b, *scores[half])
                    grad_score = terms * (dot(values, scaled) + grad_total)
                    shift_sum = shift_sum - jnp.sum(grad_score, axis=0, keepdims=True)
                    grad_low = grad_score.astype(LOW)
                    value_grad = value_grad + dot(terms.astype(LOW), scaled_nat)
                    key_grad = key_grad + dot(grad_low, queries_nat)
                    done.append((shift_sum, query_grad + dot(kt[core, b, lanes], grad_low)))
                for start, found in zip(starts, (key_grad, value_grad)):
                    at = dkv_lanes(core, start, pair_width)
                    if not fresh:
                        found = found + active[b, :, at].astype(F32)
                    active[b, :, at] = found.astype(LOW)
                return tuple(done)

            start = (jnp.zeros((1, rows), F32), jnp.zeros((pair_width, rows), F32))
            found = over_keys(keys_in, (start, start))
            for half in range(2):
                shift_sum, query_grad = found[half]
                at = head_at(pair, half)
                own = query_grad[half * head_width : (half + 1) * head_width]
                own_keys = kt[c, block, at].astype(F32)
                gqt[at] = (0.125 * (own + shift_sum * own_keys)).astype(LOW)
                skt[at] = (shift_sum * qt[block, at].astype(F32)).astype(LOW)

        loop_from(first, last, body)

    def back_end(block):
        gm[block, :, 0:cols] = gqt[...].T
        at = dkv_lanes(c, 0, cols)
        active[block, :, at] = active[block, :, at] + skt[...].T

    dkv_wire = wires.take(1)

    def dkv_copy():
        return wires.copy(
            lambda: (
                active.at[:, :, dkv_lanes(1 - c, 0, 2 * cols)],
                gm.at[:, :, cols : 3 * cols],
                place.c_peer(),
            ),
            dkv_wire,
        )

    def back_other(step):
        block = place.g_at(-step)
        back_start(block)
        back_attend(block, False, 0, pairs)
        back_end(block)

    @step
    def back_own_a():
        back_start(g)
        back_attend(g, True, 0, pairs // 2)

    @step
    def back_own_b():
        back_attend(g, True, pairs // 2, pairs)
        back_end(g)

    @step
    def ga_wait():
        wait_all([ga_copy(step) for step in range(1, groups)])

    @step
    def out_send():
        sent_all(cot_copies)
        start_all(out_copies)

    @step
    def back_other_a():
        if in_two:
            back_start(place.g_at(-1))
            back_attend(place.g_at(-1), False, 0, pairs // 2)

    @step
    def back_other_b():
        if in_two:
            back_attend(place.g_at(-1), False, pairs // 2, pairs)
            back_end(place.g_at(-1))
        else:
            each_group(back_other)
        dkv_copy().start()

    @step
    def merge_keys():
        dkv_copy().wait_recv()

        def merge_block(b):
            at = dkv_lanes(c, 0, 2 * cols)
            gm[b, :, cols : 3 * cols] = gm[b, :, cols : 3 * cols] + active[b, :, at]

        loop(groups, merge_block)

    @step
    def mix_send():
        parts_sent(second_first)
        each_group(lambda step: send_part(step, gm.at[place.g_at(step)], wqkv, mix_first))

    own_parts = [far.at[i // groups, i % groups] for i in range(width // rows)]

    @step
    def mix_back():
        count, per, size = row_chunks(wqkv)
        for j in range(count):
            value = dot_nt(gm[g], wqkv[j * per : (j + 1) * per].reshape(size, 3 * cols))
            for i in range(size // rows):
                own_parts[j * (size // rows) + i][...] = value[:, i * rows : (i + 1) * rows]

    c_qkv = v.c_up.at[:, :, :, 0 : 3 * cols]
    r_qkv = Reduce(
        place, wires, wqkv, h_qkv, False, c_qkv, None, v.y_qkv, v.z_qkv, v.p_qkv
    )

    @step
    def grad_q():
        g_qkv.drain()
        weight_grad(blocks(normed), gm, wqkv)

    @step
    def up_free():
        r_up.y_sent()
        pl.semaphore_signal(v.free_sem, inc=1, device_id=place.c_peer(), device_id_type=MESH)

    @step
    def qkv_send():
        pl.semaphore_wait(v.free_sem, 1)
        r_qkv.core_send(0)
        r_qkv.core_send(1)

    @step
    def norm_merged():
        wait_all([part_copy(step, mix_first) for step in range(1, groups)])

        def first_in(at):
            t = jnp.concatenate([part[at] for part in own_parts], axis=1)
            for step in range(1, groups):
                t = t + p_recv[step - 1, at].astype(F32)
            return t

        def first_out(at, grad):
            gb[at] = (grad + gmid[at]).astype(LOW)

        gain_sum, bias_sum = norm_back(merged, 1, first_in, first_out)
        sums[1:2] = gain_sum
        sums[2:3] = bias_sum

    gmx = v.gmx
    merged_copies = []
    if sizes.pair:
        other_cols = aligned((1 - g) * cols, cols)
        merged_copies = [
            Exchange(place, wires).copy(1, lambda: gb.at[:, other_cols], lambda: gmx.at[1])
        ]

    @step
    def merged_send():
        start_all(merged_copies)
        if sizes.pair:
            gmx[0] = gb[:, own_cols]

    sum_in = v.sum_in

    def sum_copy(slot, peer):
        return wires.copy(lambda: (sums, sum_in.at[slot], peer()))

    sum_core = sum_copy(0, place.c_peer)
    sum_x = [sum_copy(k, functools.partial(place.x_peer, k)) for k in range(1, groups)]
    sum_y = sum_copy(groups, place.y_peer)
    sum_z = [sum_copy(groups + k, functools.partial(place.z_peer, k)) for k in range(1, nz)]
    o_up = v.o_up
    up_swap = Exchange(place, wires)
    up_copies = [up_swap.copy(k, lambda: o_up.at[g], lambda: o_up.at[g]) for k in range(1, groups)]

    @step
    def sum_0():
        r_down.y_sent()
        sums[0:1] = column_sums(lambda i: gb[aligned(i * chunk, chunk)], per_block, width)
        sum_core.start()

    @step
    def sum_1():
        sum_core.wait()
        sums[...] = sums[...] + sum_in[0]
        start_all(sum_x)

    @step
    def sum_2():
        for copy in sum_x:
            copy.wait()
        for k in range(1, groups):
            sums[0:6] = sums[0:6] + sum_in[k, 0:6]
        sum_y.start()

    @step
    def sum_3():
        sum_y.wait()
        sums[...] = sums[...] + sum_in[groups]
        start_all(sum_z)

    @step
    def sum_4():
        for copy in sum_z:
            copy.wait()
        for k in range(1, nz):
            sums[...] = sums[...] + sum_in[groups + k]
        o_up[g] = sums[...]
        v.o_small[...] = sums[...]
        start_all(up_copies)

    stores = []
    gj = normed

    @step
    def inputs_back():
        if sizes.pair:
            give_inputs()

    def give_inputs():
        sent_all(normed_copies)
        count, per, size = row_chunks(ws)
        span = width // size

        def body(j):
            value = dot_nt(gb[...], ws[pl.ds(j * per, per)].reshape(size, width))
            at = aligned(lax.rem(j, span) * size, size)
            gj[lax.div(j, span), :, at] = value.astype(LOW)

        loop(count, body)
        for half, name in enumerate(("o_frames", "o_skip")):
            stores.append(pltpu.make_async_copy(gj.at[half], getattr(v, name).at[0], local.at[1 + half]))
            stores[-1].start()

    @step
    def output():
        wait_all(out_copies)
        ob = second.at[g]

        def out_rows(i):
            at = aligned(i * chunk, chunk)
            value = middle[at] + second[g, at].astype(F32) + vecs[5:6]
            for step in range(1, groups):
                value = value + cot_all[place.g_at(-step), at].astype(F32)
            ob[at] = value.astype(LOW)

        loop(rows // chunk, out_rows)
        stores.append(pltpu.make_async_copy(ob, v.o_out.at[0], local.at[0]))
        stores[-1].start()

    if sizes.pair:
        grad_skip, c_skip = wdown.at[:, :, :, 0:cols], v.c_down.at[:, :, :, 0:cols]
    else:
        grad_skip, c_skip = ws, v.c_skip
    r_skip = Reduce(
        place, wires, grad_skip, h_skip, not sizes.pair, c_skip, v.x_skip, v.y_skip,
        v.z_skip, v.p_skip,
    )

    @step
    def grad_s():
        if sizes.pair:
            for copy in joined_copies + merged_copies:
                copy.wait()
            for half in range(2):
                lefts = [v.io.at[half], v.joined.at[half]]
                weight_grad(lefts, gmx, grad_skip, half * (nz // 2))
        else:
            give_inputs()
            parts_sent(mix_first)
            for load in input_loads():
                load.start()
            for load in input_loads():
                load.wait()
            g_skip.drain()
            weight_grad([fr_v], gb, grad_skip)
            weight_grad([sk_v], gb, grad_skip, nz // 2)
        r_skip.core_send(0)
        r_skip.core_send(1)

    def reduce_steps(name, reduced, ready=True):
        for part in range(2):
            add = functools.partial(reduced.core_add, part) if ready else none
            steps[f"{name}_c{part}"] = add

        def add_y(reach):
            for one in reaches(reach):
                reduced.y_add(one)

        for reach in range(last_reach + 1):
            steps[f"{name}_y{reach}"] = functools.partial(add_y, reach)
        steps[name + "_z"], steps[name + "_f"] = reduced.z_add, reduced.spread_on

    reduce_steps("rd", r_down, early)
    reduce_steps("ru", r_up)
    reduce_steps("ro", r_out)
    reduce_steps("rq", r_qkv)
    reduce_steps("rs", r_skip)
    steps["ro_x0"], steps["ro_x1"] = (functools.partial(r_out.x_add, part) for part in range(2))
    if r_skip.spread:
        steps["rs_c1"] = lambda: [r_skip.core_add(1), r_skip.x_add(0), r_skip.x_add(1)]

    @step
    def skips_sent():
        for gather in [g_small, *gathers[6:]] + ([g_skip] if sizes.pair else []):
            gather.drain()

    @step
    def blocks_sent():
        sent_all(seg_copies + [seg_core] + kv_waits + [ga_copy(k) for k in range(1, groups)])

    @step
    def parts_gone():
        if sizes.pair:
            sent_all(out_copies)
            parts_sent(mix_first)
        sent_all([dkv_copy()])

    def reduced_end(reduced):
        reduced.finish()
        reduced.drain()

    steps["rd_e"] = functools.partial(reduced_end, r_down)
    steps["ru_e"] = functools.partial(reduced_end, r_up)
    steps["ro_e"] = functools.partial(reduced_end, r_out)
    steps["rq_e"] = functools.partial(reduced_end, r_qkv)

    assert sorted(ORDER) == sorted(steps), set(ORDER) ^ set(steps)
    order = list(ORDER)
    if not early:
        cut = order.index("out_parts") + 1
        moved = [name for name in order[:cut] if name.startswith("rd_")]
        order[:cut] = [name for name in order[:cut] if not name.startswith("rd_")] + moved
    for name in order:
        steps[name]()

    for copy in up_copies:
        copy.wait()
    r_skip.finish()
    r_skip.drain()
    if not sizes.pair:
        sent_all(out_copies)
    for store in stores:
        store.wait()


def finish(sizes, *refs):
    wholes, pieces, small, up = refs[0:3], refs[3:8], refs[8], refs[9]
    whole_outs, outs, vectors, up_out = refs[10:13], refs[13:18], refs[18:24], refs[24]
    held, made, passed, sems = refs[25:30], refs[30:35], refs[35], refs[36]
    groups, cols, width = sizes.groups, sizes.cols, sizes.width
    copies = [
        pltpu.make_async_copy(pieces[i], held[i], sems.at[i]) for i in range(5)
    ]
    moves = [
        pltpu.make_async_copy(wholes[i].at[0], passed.at[i], sems.at[5 + i]) for i in range(3)
    ]
    for copy in moves + copies:
        copy.start()
    stores = []
    for i in range(3):
        moves[i].wait()
        stores.append(pltpu.make_async_copy(passed.at[i], whole_outs[i].at[0], sems.at[13 + i]))
        stores[-1].start()
    for i in range(5):
        copies[i].wait()
        half = held[i].shape[2]
        for group in range(groups):
            for core in range(2):
                rows = slice(core * half, (core + 1) * half)
                if i == 4:
                    top = (group * 2 + core) * half
                    made[i][top : top + half] = held[i][group, core].astype(F32)
                elif i == 3 and sizes.direct:
                    for s in range(sizes.n_dp):
                        at = (s * groups + group) * sizes.part
                        made[i][rows, at : at + sizes.part] = held[i][
                            group, core, :, s * sizes.part : (s + 1) * sizes.part
                        ].astype(F32)
                elif i == 3:
                    made[i][rows, group * sizes.units : (group + 1) * sizes.units] = held[i][
                        group, core
                    ].astype(F32)
                else:
                    for third in range(held[i].shape[3] // cols):
                        at = third * width + group * cols
                        made[i][rows, at : at + cols] = held[i][
                            group, core, :, third * cols : (third + 1) * cols
                        ].astype(F32)
        stores.append(pltpu.make_async_copy(made[i], outs[i], sems.at[8 + i]))
        stores[-1].start()
    dp = lax.axis_index("dp")
    if sizes.shard % 128 == 0 and sizes.direct:
        own = aligned(dp * sizes.shard, sizes.shard)
        for row in range(6):
            vectors[row][...] = small[row : row + 1, own]
        per_row = width // sizes.part
        at = aligned(lax.rem(dp, per_row) * sizes.part, sizes.part)
        for group in range(groups):
            up_out[:, group * sizes.part : (group + 1) * sizes.part] = up[
                group, pl.ds(6 + lax.div(dp, per_row), 1), at
            ]
    else:
        for row in range(6):
            vectors[row][...] = small[row : row + 1]
        for group in range(groups):
            up_out[:, group * sizes.units : (group + 1) * sizes.units] = up[
                group, 6:7, 0 : sizes.units
            ]
    for copy in stores:
        copy.wait()


def per_device(sizes, *args):
    (
        frames, skip_frames, cotangent, seg_ids, positions,
        w_skip, b_skip, gain_attn, bias_attn, w_qkv, w_out,
        gain_ffn, bias_ffn, w_up, b_up, w_down, b_down,
    ) = args
    del positions
    n_dp, nz, groups = sizes.n_dp, sizes.nz, sizes.groups
    rows, width, cols, units = sizes.rows, sizes.width, sizes.cols, sizes.units
    heads, part, shard = sizes.heads, sizes.part, sizes.shard
    depth = w_up.shape[0]
    if not sizes.direct:
        w_up = (
            w_up.reshape(depth, n_dp, groups, part).transpose(0, 2, 1, 3).reshape(depth, groups * units)
        )
        group = lax.axis_index("blk") // 2
        b_up = lax.dynamic_slice_in_dim(b_up, group * part, part)
    r_skip, r_down = w_skip.shape[0], w_down.shape[0] // groups
    span = -(-max(shard, part) // 128) * 128

    def low(*shape):
        return pltpu.VMEM(shape, LOW)

    def full(*shape):
        return pltpu.VMEM(shape, F32)

    sizes.pair = groups == 2 and r_skip == r_down
    scratch = [
        low(2, rows, width), low(groups, rows, width),
        low(nz, 2, r_skip, width), low(nz, 2, depth, 3 * cols), low(nz, 2, depth, width),
        low(nz, 2, depth, units), low(nz, 2, r_down, width),
        full(nz, 2, 8, span), full(8, width), full(1, units),
        full(2, groups, 8, rows), low(2, groups, rows, 128),
        full(rows, width), full(rows, width), full(rows, width),
        low(groups, rows, width), low(groups, rows, width),
        low(2, groups, rows, 2 * cols),
        low(groups, cols, rows), low(2, groups, cols, rows),
        full(groups, heads, 1, rows), full(groups, cols, rows), full(groups, heads, 1, rows),
        low(rows, width), low(groups, rows, cols),
        low(groups, rows, units), low(groups, rows, units),
        low(1, 16, 128) if groups > 2 else low(1, rows, width),
        low(groups - 1, rows, width),
        low(rows, width), low(groups, rows, cols),
        low(groups, rows, 3 * cols),
        full(2, groups, rows, rows), low(2, groups, cols, rows),
        low(1, 16, 128) if sizes.pair else low(nz, 2, r_skip // 2, width),
        low(nz, 2, depth // 2, width),
        low(nz, 2, depth // 2, units),
        low(nz, 2, r_down // 2, width),
        low(1, 16, 128) if sizes.pair else low(groups - 1, nz, 2, r_skip // 2, cols),
        low(groups - 1, nz, 2, depth // 2, cols),
        low(nz, r_skip // 2, cols), low(nz, depth // 2, 3 * cols), low(nz, depth // 2, cols),
        low(nz, depth // 2, units), low(nz, r_down // 2, width),
        low(nz - 1, r_skip // 2, cols), low(nz - 1, depth // 2, 3 * cols),
        low(nz - 1, depth // 2, cols), low(nz - 1, depth // 2, units),
        low(nz - 1, r_down // 2, width),
        low(2, rows, width) if sizes.pair else low(1, 16, 128),
        low(groups, rows, cols) if sizes.pair else low(1, 16, 128),
        low(nz, 2, r_down, width) if 2 * r_down == 512 else low(1, 16, 128),
        full(8, width), full(groups + nz, 8, width),
        low(512 if groups * rows <= 512 else 256, groups * rows),
    ]
    wires = 320 if groups * n_dp <= 16 else 1400
    scratch += [pltpu.SemaphoreType.DMA((wires,)), pltpu.SemaphoreType.DMA((wires,))]
    scratch += [pltpu.SemaphoreType.DMA((16,)), pltpu.SemaphoreType.REGULAR]
    hbm, vmem = pl.BlockSpec(memory_space=pltpu.HBM), pl.BlockSpec(memory_space=pltpu.VMEM)
    whole = jax.ShapeDtypeStruct((1, rows, width), LOW)

    def piece(*shape):
        return jax.ShapeDtypeStruct((groups, 2) + shape, LOW)

    vectors = (b_skip, gain_attn, bias_attn, gain_ffn, bias_ffn, b_down, b_up)
    found = pl.pallas_call(
        functools.partial(kernel, sizes),
        out_shape=(
            whole, whole, whole,
            piece(r_skip // 2, cols), piece(depth // 2, 3 * cols), piece(depth // 2, cols),
            piece(depth // 2, units), piece(r_down // 2, width),
            jax.ShapeDtypeStruct((8, width), F32), jax.ShapeDtypeStruct((groups, 8, width), F32),
        ),
        in_specs=[hbm] * 3 + [vmem] * 8 + [hbm] * 5,
        out_specs=[hbm] * 3 + [vmem] * 7,
        scratch_shapes=scratch,
        compiler_params=pltpu.CompilerParams(
            collective_id=0, has_side_effects=True, vmem_limit_bytes=64 * 2**20
        ),
    )(
        frames, skip_frames, cotangent, seg_ids,
        *[vector.reshape(1, -1) for vector in vectors],
        w_skip, w_qkv, w_out, w_up, w_down,
    )
    easy = shard % 128 == 0 and sizes.direct
    line = jax.ShapeDtypeStruct((1, shard if easy else width), F32)
    shapes = [w_skip.shape, w_qkv.shape, w_out.shape, w_up.shape, w_down.shape]
    done = pl.pallas_call(
        functools.partial(finish, sizes),
        out_shape=(whole,) * 3
        + tuple(jax.ShapeDtypeStruct(shape, F32) for shape in shapes)
        + (line,) * 6
        + (jax.ShapeDtypeStruct((1, groups * (part if easy else units)), F32),),
        in_specs=[hbm] * 8 + [vmem] * 2,
        out_specs=[hbm] * 8 + [vmem] * 7,
        scratch_shapes=[pltpu.VMEM(value.shape, LOW) for value in found[3:8]]
        + [pltpu.VMEM(shape, F32) for shape in shapes]
        + [low(3, rows, width), pltpu.SemaphoreType.DMA((16,))],
        compiler_params=pltpu.CompilerParams(vmem_limit_bytes=60 * 2**20),
    )(*found)
    output, grad_frames, grad_skip, g_skip, g_qkv, g_out, g_up, g_down = done[0:8]
    lines = [value.reshape(-1) for value in done[8:15]]
    if not easy:
        at = lax.axis_index("dp")
        lines[0:6] = [lax.dynamic_slice_in_dim(value, at * shard, shard) for value in lines[0:6]]
        by_group = lines[6].reshape(groups, units)
        lines[6] = lax.dynamic_slice_in_dim(by_group, at * part, part, 1).reshape(-1)
    if not sizes.direct:
        g_up = g_up.reshape(depth, groups, n_dp, part).transpose(0, 2, 1, 3).reshape(depth, -1)
    g_b_skip, g_gain_a, g_bias_a, g_gain_f, g_bias_f, g_b_down, g_b_up = lines
    return (
        output, grad_frames, grad_skip, g_skip, g_b_skip, g_gain_a, g_bias_a, g_qkv, g_out,
        g_gain_f, g_bias_f, g_up, g_b_up, g_down, g_b_down,
    )


def solution(mesh):
    rows, lone = P("dp", None), P("dp")
    frames = P("dp", "blk", None)
    in_specs = (frames,) * 3 + (P("dp", "blk"),) * 2
    in_specs += (rows, lone, lone, lone, rows, rows, lone, lone, rows, lone, rows, lone)
    out_specs = (frames,) * 3
    out_specs += (rows, lone, lone, lone, rows, rows, lone, lone, rows, lone, rows, lone)

    def body(*args):
        return per_device(Sizes(mesh.shape, args[0], args[13]), *args)

    return jax.shard_map(
        body, mesh=mesh, in_specs=in_specs, out_specs=out_specs, check_vma=False
    )
```
